32 devices in a mesh: member: 2 (over y), tile: 4 (over z), sub: 2 (over x), comp: 2 (over core).
Axes of the slice: x: 2, y: 2, z: 4, core: 2. Of those that a mesh axis runs over, the one named last changes fastest.
Arguments:
- atm_state: float32 [3, 16, 128, 512], P(None, None, ('member', 'tile'), ('sub', 'comp')), parts along dimension 2, may hold values from -6 to 6
- air_temp: float32 [128, 512], P(('member', 'tile'), ('sub', 'comp')), parts along dimension 0, may hold values from -6 to 6
- depth: float32 [128, 512], P(('member', 'tile'), ('sub', 'comp')), parts along dimension 0, may hold values from 0.5 to 1.5
- wave_speed: float32 [16], replicated, may hold values from 0.1 to 0.6
- ocean_state: float32 [2, 8, 128, 512], P(None, None, ('member', 'tile'), ('sub', 'comp')), parts along dimension 2, may hold values from -6 to 6
- wet_mask: int32 [128, 512], P(('member', 'tile'), ('sub', 'comp')), parts along dimension 0, may hold values 0 or 1
- diffusivity: float32 [128, 512], P(('member', 'tile'), ('sub', 'comp')), parts along dimension 0, may hold values from 0.05 to 0.2
- xg_atm_cell: int32 [8, 4, 2048], P(('member', 'tile'), ('sub', 'comp')), parts along dimension 0, may hold values from 0 to 2047
- xg_dest: int32 [8, 4, 2048, 1], P(('member', 'tile'), ('sub', 'comp')), parts along dimension 0, may hold values from 0 to 3; in each aligned block of 2048 rows (0 to 2047, 2048 to 4095, ..., all dimensions but the last counted through in order) at most 512 rows name the same one
- xg_ocean_cell: int32 [8, 4, 2048], P(('member', 'tile'), ('sub', 'comp')), parts along dimension 0, may hold values from 0 to 2047
- xg_weight: float32 [8, 4, 2048], P(('member', 'tile'), ('sub', 'comp')), parts along dimension 0, may hold values from 0.2 to 1
Outputs:
- atm_out: float32 [3, 16, 128, 512], P(None, None, ('member', 'tile'), ('sub', 'comp')), parts along dimension 2
- ocean_out: float32 [2, 8, 128, 512], P(None, None, ('member', 'tile'), ('sub', 'comp')), parts along dimension 2
The draws below stay inside these ranges and needn't reach their ends.
There are 2 independent parts, one for each index of `member`. The reference program is written for one: setup_inputs(seed, part) draws one part's arguments, and reference() takes and returns one part's arrays. A program takes and returns all parts, laid end to end along the dimension named above; an argument that names none is the same for every part. Nothing has to cross between parts.
Inputs may be any that keep to these rules, and one draw needn't show every extreme that they name: `xg_dest`: of the 2048 exchange-grid cells of one device at most 512 name any one row block, and some device names one row block exactly 512 times in every draw.
All inputs are finite; a program needn't handle non-finite values. No bound on the sum of `wet_mask` on one device may be relied on, other than what follows from the above.
Results may differ from the reference program's by a relative error of at most 0.00002.
Values sent between devices are 32-bit elements; how exact they have to be, the bound alone decides.
No kernel may reach another device: no remote copies, remote signals or barrier semaphores. Data moves between devices by JAX's collectives and lax.ppermute only.
A program may use at most 64 MiB of HBM per device.

```python
import math
import jax
import jax.numpy as jnp
import numpy as np

LA = 16
LO = 8
ACOUSTIC = 2
OCEAN_STEPS = 2
RA = 16
CA = 128
RO = 16
CO = 128
XDEV = 2048
CAP = 512
TILES = 4
COLBLK = 4
NRA = 64
NCA = 512
NRO = 64
NCO = 512
N_TILE = 4
N_SUB = 2
N_COMP = 2


def plant(array, rng, least, high):
    longest = array.shape.index(max(array.shape))
    spots = []
    for shift in (0, 1):
        where = [jax.random.randint(jax.random.fold_in(rng, axis), (), 0, length) for axis, length in enumerate(array.shape)]
        where[longest] = (where[longest] + shift) % array.shape[longest]
        spots.append(tuple(where))
    return array.at[spots[0]].set(least).at[spots[1]].set(high)


def shard_levels(own_key, extent, split, smallest, largest):
    factor_of, own = 1.0, jax.random.fold_in(own_key, 6)
    for dim, shards_of in split:
        draws = jnp.exp(jax.random.uniform(jax.random.fold_in(own, dim), (shards_of,), jnp.float32, smallest / len(split), largest / len(split)))
        factor_of = factor_of * jnp.repeat(draws, extent[dim] // shards_of).reshape([-1 if axis == dim else 1 for axis in range(len(extent))])
    return factor_of


def routed_block(own_key, own, number, rows, number_of, top, reach, lean):
    order = jax.random.permutation(own_key, number_of)
    crowded, usual = load_shares(number_of, rows * top, reach, lean, True), load_shares(number_of, rows * top, reach, lean, False)
    places = jnp.arange(number_of)

    def named(sizes, rotation):
        used = int((sizes > 0).sum())
        fixed = max(1, used // 4)
        shifted = fixed + (places - fixed + rotation * (used - fixed)) % max(1, number_of - fixed)
        return jnp.zeros((number_of,), jnp.int32).at[order[jnp.where(places < fixed, places, shifted)]].set(jnp.asarray(sizes, jnp.int32))

    sizes = jnp.where(number % 4 == 0, named(crowded, number // 4), named(usual, number - number // 4 - 1))
    mixed = jax.random.permutation(jax.random.fold_in(own, 3), number_of)
    giver, taker = mixed[0:number_of // 2 * 2:2], mixed[1:number_of // 2 * 2:2]
    margin = jnp.minimum(sizes[giver] - 1, reach - sizes[taker]) // 2
    margin = jnp.where((giver == order[0]) | (taker == order[0]) | (sizes[taker] == 0), 0, jnp.maximum(margin, 0))
    shifted = jax.random.randint(jax.random.fold_in(own, 4), (number_of // 2,), 0, 1 << 20) % (margin + 1)
    sizes = sizes.at[giver].add(-shifted).at[taker].add(shifted)
    members = jnp.searchsorted(jnp.cumsum(sizes), jnp.arange(rows * top), side="right").astype(jnp.int32)
    listing = members.reshape(top, rows).T
    listing = listing[jax.random.permutation(jax.random.fold_in(own, 1), rows)]
    rotation = jax.random.randint(jax.random.fold_in(own, 2), (rows, 1), 0, top)
    return jnp.take_along_axis(listing, (jnp.arange(top)[None, :] + rotation) % top, axis=1)


def load_shares(amount, total, limit, lean, full):
    weights = [(1 << 20) // math.isqrt(rank ** lean) + 1 for rank in range(1, amount + 1)]
    largest = limit if full else min(limit, max(-(-total // amount), total * weights[0] // sum(weights)))
    least = 1 if total - largest >= amount - 1 else 0
    holding, spare = [largest] + [least] * (amount - 1), total - largest - least * (amount - 1)
    while spare > 0:
        free = [i for i in range(1, amount) if holding[i] < largest] or [i for i in range(1, amount) if holding[i] < limit]
        pool, remaining = sum([weights[i] for i in free]), spare
        for i in free:
            extra = min(limit - holding[i], max(1, remaining * weights[i] // pool), spare)
            holding[i] = holding[i] + extra
            spare = spare - extra
    return np.array(holding)


def bell_draw(own_key, shape, width, reach, split=(), held_as=jnp.bfloat16):
    factor_of = shard_levels(own_key, shape, split, -0.22, 0.18) if split else 1.0
    values = jax.random.normal(own_key, shape, jnp.float32) * width * factor_of
    return jnp.minimum(jnp.maximum(values, -reach), reach).astype(held_as)


def setup_inputs(seed: int = 0, part: int = 0) -> dict:
    arg_keys = jax.random.split(jax.random.key(seed), 12)
    part_splits = jax.random.split(jax.random.fold_in(arg_keys[11], part), 12)
    atm_state = bell_draw(part_splits[0], (3, LA, NRA, NCA), 1.0, 6.0, ((2, 4), (3, 4)), jnp.float32)
    air_temp = bell_draw(part_splits[1], (NRA, NCA), 1.0, 6.0, ((0, 4), (1, 4)), jnp.float32)
    depth = jnp.clip(1.0 + 0.1 * jax.random.normal(part_splits[2], (NRA, NCA), jnp.float32), 0.5, 1.5)
    wave_speed = jnp.clip(jnp.exp(jax.random.uniform(arg_keys[3], (LA,), jnp.float32, math.log(0.1), math.log(0.6))), 0.1, 0.6)
    ocean_state = bell_draw(part_splits[4], (2, LO, NRO, NCO), 1.0, 6.0, ((2, 4), (3, 4)), jnp.float32)
    wet_mask = plant((jax.random.randint(part_splits[5], (NRO, NCO), 0, 4) < 3).astype(jnp.int32), jax.random.fold_in(part_splits[5], 1), 0, 1)
    diffusivity = jnp.clip(0.05 + 0.15 * jax.random.uniform(part_splits[6], (NRO, NCO), jnp.float32) ** shard_levels(part_splits[6], (NRO, NCO), ((0, 4), (1, 4)), -0.2, 0.2), 0.05, 0.2)
    xg_atm_cell = plant(jax.random.randint(part_splits[7], (TILES, COLBLK, XDEV), 0, RA * CA), jax.random.fold_in(part_splits[7], 1), 0, (RA * CA) - 1).astype(jnp.int32)
    xg_dest_keys = jax.random.split(jax.random.fold_in(part_splits[8], 1), TILES * COLBLK * XDEV // XDEV)
    xg_dest_turns = jax.random.permutation(jax.random.fold_in(part_splits[8], 3), TILES * COLBLK * XDEV // XDEV)
    xg_dest = jax.vmap(lambda own, number: routed_block(jax.random.fold_in(part_splits[8], 2), own, number, XDEV, TILES, 1, CAP, 2))(xg_dest_keys, xg_dest_turns).reshape((TILES, COLBLK, XDEV, 1))
    xg_ocean_cell = plant(jax.random.randint(part_splits[9], (TILES, COLBLK, XDEV), 0, RO * CO), jax.random.fold_in(part_splits[9], 1), 0, (RO * CO) - 1).astype(jnp.int32)
    xg_weight = jnp.clip(jnp.exp(math.log(1.0) - 1.609438 * jax.random.uniform(part_splits[10], (TILES, COLBLK, XDEV), jnp.float32) ** shard_levels(part_splits[10], (TILES, COLBLK, XDEV), ((0, 4), (1, 4)), -0.2, 0.2)), 0.2, 1.0)
    return {"atm_state": atm_state, "air_temp": air_temp, "depth": depth, "wave_speed": wave_speed, "ocean_state": ocean_state, "wet_mask": wet_mask, "diffusivity": diffusivity, "xg_atm_cell": xg_atm_cell, "xg_dest": xg_dest, "xg_ocean_cell": xg_ocean_cell, "xg_weight": xg_weight}


atm_gain = 0.5
sea_gain = 0.5


def east_west(field):
    return (jnp.roll(field, -1, -1) - jnp.roll(field, 1, -1)) * 0.5


def north_south(field):
    return (jnp.roll(field, -1, -2) - jnp.roll(field, 1, -2)) * 0.5


def diffuse(tracer, wetness, kappa):
    total = jnp.roll(wetness, -1, -1) * (jnp.roll(tracer, -1, -1) - tracer)
    total = total + jnp.roll(wetness, 1, -1) * (jnp.roll(tracer, 1, -1) - tracer)
    total = total + jnp.roll(wetness, -1, -2) * (jnp.roll(tracer, -1, -2) - tracer)
    total = total + jnp.roll(wetness, 1, -2) * (jnp.roll(tracer, 1, -2) - tracer)
    return tracer + kappa * (wetness * total)


def reference(atm_state, air_temp, depth, wave_speed, ocean_state, wet_mask, diffusivity, xg_atm_cell, xg_dest, xg_ocean_cell, xg_weight):
    tiles = jnp.arange(N_TILE, dtype=jnp.int32)[:, None, None]
    blocks = jnp.arange(N_SUB * N_COMP, dtype=jnp.int32)[None, :, None]
    target = xg_dest[..., 0]
    atm_row = tiles * RA + xg_atm_cell // CA
    atm_col = blocks * CA + xg_atm_cell % CA
    sea_row = target * RO + xg_ocean_cell // CO
    sea_col = blocks * CO + xg_ocean_cell % CO
    surface_sea = ocean_state[0, 0]
    heat_flux = xg_weight * (air_temp[atm_row, atm_col] - surface_sea[sea_row, sea_col])
    atm_flux = jnp.zeros(air_temp.shape, jnp.float32).at[atm_row, atm_col].add(heat_flux)
    sea_flux = jnp.zeros(surface_sea.shape, jnp.float32).at[sea_row, sea_col].add(heat_flux)
    column_speed = wave_speed[:, None, None] * depth[None]
    winds_east, winds_north, height = atm_state[0], atm_state[1], atm_state[2]
    for substep in range(ACOUSTIC):
        height = height - column_speed * (east_west(winds_east) + north_south(winds_north))
        winds_east = winds_east - east_west(height)
        winds_north = winds_north - north_south(height)
    height = height.at[LA - 1].add(-atm_gain * atm_flux)
    wetness = wet_mask.astype(jnp.float32)
    tracers = ocean_state
    for substep in range(OCEAN_STEPS):
        tracers = diffuse(tracers, wetness, diffusivity)
    tracers = tracers.at[0, 0].add(sea_gain * sea_flux)
    return jnp.stack([winds_east, winds_north, height]), tracers
```

```python
import functools

import jax
import jax.numpy as jnp
from jax import lax
from jax.experimental import pallas as pl
from jax.experimental.pallas import tpu as pltpu
from jax.sharding import PartitionSpec as P

ACOUSTIC = 2
OCEAN_STEPS = 2
AH = 2 * ACOUSTIC
OH = OCEAN_STEPS

ATM_GAIN = 0.5
SEA_GAIN = 0.5

F32 = jnp.float32
BF16 = jnp.bfloat16


def lane_slots(levels, tracers):
    slots = [AH * i for i in range(3 * levels)]
    base = AH * 3 * levels
    slots += [base + OH * i for i in range(tracers)]
    base += OH * tracers
    slots += [base + AH * i for i in range(3)]
    total = base + 3 * AH
    return slots, -(-total // 128) * 128


def row_slots(levels, tracers):
    per = 3 * AH - 2
    base = per * levels
    misc = base + OH * tracers
    return per, base, misc, misc + AH + 2 * OH


def pack_kernel(atm, ocean, depth, wet, kappa, up, down, left, right, lu, ld, ru, rd):
    levels = atm.shape[1]
    rows, cols = atm.shape[2:]
    tracers = ocean.shape[0] * ocean.shape[1]
    each = ocean.shape[1]
    per, obase, mbase, _ = row_slots(levels, tracers)
    slots, _ = lane_slots(levels, tracers)
    wetness = wet[...].astype(F32)

    for level in range(levels):
        base = per * level
        for at, which, width in ((0, 1, AH), (AH, 0, AH - 1), (2 * AH - 1, 2, AH - 1)):
            up[base + at : base + at + width, :] = atm[which, level, 0:width, :]
            down[base + at : base + at + width, :] = atm[which, level, rows - width : rows, :]
    for i in range(tracers):
        at = obase + OH * i
        up[at : at + OH, :] = ocean[i // each, i % each, 0:OH, :]
        down[at : at + OH, :] = ocean[i // each, i % each, rows - OH : rows, :]
    for at, value, width in (
        (mbase, depth[...], AH),
        (mbase + AH, wetness, OH),
        (mbase + AH + OH, kappa[...], OH),
    ):
        up[at : at + width, :] = value[0:width]
        down[at : at + width, :] = value[rows - width : rows]

    lane = lax.broadcasted_iota(jnp.int32, (rows, cols), 1)
    fields = [(atm, (k, l), AH) for k in range(3) for l in range(levels)]
    fields += [(ocean, (i // each, i % each), OH) for i in range(tracers)]
    fields += [(depth, None, AH), (None, None, AH), (kappa, None, AH)]
    packed = {}
    for (ref, at, width), slot in zip(fields, slots):
        value = wetness if ref is None else (ref[...] if at is None else ref[at[0], at[1]])
        tile, offset = slot // cols, slot % cols
        mask = (lane >= offset) & (lane < offset + width)
        first = pltpu.roll(value, offset, 1) if offset else value
        turn = (offset + width) % cols
        last = pltpu.roll(value, turn, 1) if turn else value
        if tile in packed:
            a, b = packed[tile]
            packed[tile] = (jnp.where(mask, first, a), jnp.where(mask, last, b))
        else:
            packed[tile] = (first, last)
    for tile, (a, b) in packed.items():
        where = slice(tile * cols, (tile + 1) * cols)
        left[:, where] = a
        right[:, where] = b
        lu[:, where] = a[0:AH]
        ld[:, where] = a[rows - AH : rows]
        ru[:, where] = b[0:AH]
        rd[:, where] = b[rows - AH : rows]


def split3(value):
    hi = value.astype(BF16)
    rest = value - hi.astype(F32)
    mid = rest.astype(BF16)
    low = (rest - mid.astype(F32)).astype(BF16)
    return hi, mid, low


def one_hot(index, size):
    shape = (size, index.shape[-1])
    return lax.broadcasted_iota(jnp.int32, shape, 0) == index


def gather_rows(table, hot_rows, hot_cols):
    r = table.shape[0]
    parts = jnp.concatenate(split3(table), axis=0)
    g = jnp.dot(parts, hot_cols, preferred_element_type=F32)
    g = g[0:r] + g[r : 2 * r] + g[2 * r : 3 * r]
    return jnp.sum(jnp.where(hot_rows, g, 0.0), axis=0, keepdims=True)


def scatter_rows(values, hot_rows, hot_cols):
    r = hot_rows.shape[0]
    parts = []
    for value in values:
        for part in split3(value):
            parts.append(jnp.where(hot_rows, part.astype(F32), 0.0).astype(BF16))
    s = lax.dot_general(
        jnp.concatenate(parts, axis=0),
        hot_cols,
        (((1,), (1,)), ((), ())),
        preferred_element_type=F32,
    )
    out = []
    for i in range(len(values)):
        base = 3 * r * i
        out.append(s[base : base + r] + s[base + r : base + 2 * r] + s[base + 2 * r : base + 3 * r])
    return out


def send_kernel(air, sst, atm_cell, dest, sea_cell, weight, message, wair_out):
    rows, cols = air.shape
    tiles = message.shape[0]
    cell = atm_cell[...]
    hot_atm = jnp.where(one_hot(cell % cols, cols), 1.0, 0.0).astype(BF16)
    airx = gather_rows(air[...], one_hot(cell // cols, rows), hot_atm)
    w = weight[...]
    wair = w * airx
    wair_out[...] = wair
    cell = sea_cell[...]
    hot_sea = jnp.where(one_hot(cell % cols, cols), 1.0, 0.0).astype(BF16)
    row = dest[...] * rows + cell // cols
    surface = sst[...].reshape(rows, cols)
    for tile in range(tiles):
        s1, s2 = scatter_rows([wair, w], one_hot(row - tile * rows, rows), hot_sea)
        message[tile, 0:rows, :] = s1
        message[tile, rows : 2 * rows, :] = s2
        message[tile, 2 * rows : 3 * rows, :] = surface


def flux_kernel(got, sst, atm_cell, dest, sea_cell, weight, wair, atm_in, ocean_in, atm_out, ocean_out):
    rows, cols = atm_in.shape[-2:]
    tiles = got.shape[0]
    surface = sst[...].reshape(rows, cols)
    s1, s2 = got[0, 0:rows, :], got[0, rows : 2 * rows, :]
    for tile in range(1, tiles):
        s1 = s1 + got[tile, 0:rows, :]
        s2 = s2 + got[tile, rows : 2 * rows, :]
    sea_flux = s1 - surface * s2
    ocean_out[...] = ocean_in[...] + (SEA_GAIN * sea_flux).reshape(ocean_in.shape)

    cell = sea_cell[...]
    hot_sea = jnp.where(one_hot(cell % cols, cols), 1.0, 0.0).astype(BF16)
    row = dest[...] * rows + cell // cols
    sstx = jnp.zeros(cell.shape, F32)
    for tile in range(tiles):
        table = got[tile, 2 * rows : 3 * rows, :]
        sstx = sstx + gather_rows(table, one_hot(row - tile * rows, rows), hot_sea)
    flux = wair[...] - weight[...] * sstx
    cell = atm_cell[...]
    hot_atm = jnp.where(one_hot(cell % cols, cols), 1.0, 0.0).astype(BF16)
    (atm_flux,) = scatter_rows([flux], one_hot(cell // cols, rows), hot_atm)
    atm_out[...] = atm_in[...] - (ATM_GAIN * atm_flux).reshape(atm_in.shape)


def step_kernel(
    speed,
    atm,
    ocean,
    depth,
    wet,
    kappa,
    from_up,
    from_down,
    from_left,
    from_right,
    from_ul,
    from_dl,
    from_ur,
    from_dr,
    atm_out,
    ocean_out,
    ext,
):
    levels = atm.shape[1]
    rows, cols = atm.shape[2:]
    tracers = ocean.shape[0] * ocean.shape[1]
    each = ocean.shape[1]
    per, obase, mbase, _ = row_slots(levels, tracers)
    slots, _ = lane_slots(levels, tracers)
    full = rows + 2 * AH
    lane = lax.broadcasted_iota(jnp.int32, (1, cols), 1)
    low_half = lane < cols // 2

    def strips(slot, width, left_ref, right_ref):
        where = slice(slot // cols * cols, slot // cols * cols + cols)
        offset = slot % cols
        a = right_ref[:, where]
        b = left_ref[:, where]
        if offset:
            a = pltpu.roll(a, cols - offset, 1)
        turn = (cols - width - offset) % cols
        if turn:
            b = pltpu.roll(b, turn, 1)
        return jnp.where(low_half, a, b)

    def extended(buffer, value, row_at, row_width, slot, width):
        view = ext.at[buffer]
        view[0:rows, 0:cols] = value
        view[rows : rows + row_width, 0:cols] = from_down[row_at : row_at + row_width, :]
        view[full - row_width : full, 0:cols] = from_up[row_at : row_at + row_width, :]
        view[0:rows, cols : 2 * cols] = strips(slot, width, from_left, from_right)
        view[rows : rows + AH, cols : 2 * cols] = strips(slot, width, from_dl, from_dr)
        view[full - AH : full, cols : 2 * cols] = strips(slot, width, from_ul, from_ur)
        return view[...]

    def east(f):
        return pltpu.roll(f, 2 * cols - 1, 1)

    def west(f):
        return pltpu.roll(f, 1, 1)

    def south(f):
        return pltpu.roll(f, full - 1, 0)

    def north(f):
        return pltpu.roll(f, 1, 0)

    base = 3 * levels + tracers
    depth_ext = extended(0, depth[...], mbase, AH, slots[base], AH)
    for level in range(levels):
        at = per * level
        u = extended(1, atm[0, level], at + AH, AH - 1, slots[level], AH)
        v = extended(2, atm[1, level], at, AH, slots[levels + level], AH)
        h = extended(3, atm[2, level], at + 2 * AH - 1, AH - 1, slots[2 * levels + level], AH)
        column_speed = speed[level] * depth_ext
        for _ in range(ACOUSTIC):
            h = h - column_speed * ((east(u) - west(u)) * 0.5 + (south(v) - north(v)) * 0.5)
            u = u - (east(h) - west(h)) * 0.5
            v = v - (south(h) - north(h)) * 0.5
        atm_out[0, level] = u[0:rows, 0:cols]
        atm_out[1, level] = v[0:rows, 0:cols]
        atm_out[2, level] = h[0:rows, 0:cols]

    w = extended(4, wet[...].astype(F32), mbase + AH, OH, slots[base + 1], AH)
    k = extended(5, kappa[...], mbase + AH + OH, OH, slots[base + 2], AH)
    we, ww, ws, wn = east(w), west(w), south(w), north(w)
    for i in range(tracers):
        f = extended(6, ocean[i // each, i % each], obase + OH * i, OH, slots[3 * levels + i], OH)
        for _ in range(OCEAN_STEPS):
            total = we * (east(f) - f)
            total = total + ww * (west(f) - f)
            total = total + ws * (south(f) - f)
            total = total + wn * (north(f) - f)
            f = f + k * (w * total)
        ocean_out[i // each, i % each] = f[0:rows, 0:cols]


def on_device(
    tile_count,
    atm_state,
    air_temp,
    depth,
    wave_speed,
    ocean_state,
    wet_mask,
    diffusivity,
    xg_atm_cell,
    xg_dest,
    xg_ocean_cell,
    xg_weight,
):
    levels = atm_state.shape[1]
    rows, cols = atm_state.shape[2:]
    tracers = ocean_state.shape[0] * ocean_state.shape[1]
    cells = xg_weight.shape[-1]
    _, lanes = lane_slots(levels, tracers)
    _, _, _, message_rows = row_slots(levels, tracers)
    vmem = pl.BlockSpec(memory_space=pltpu.VMEM)
    limit = 32 * 1024 * 1024

    def shape(*dims):
        return jax.ShapeDtypeStruct(dims, F32)

    up, down, left, right, lu, ld, ru, rd = pl.pallas_call(
        pack_kernel,
        out_shape=[shape(message_rows, cols)] * 2 + [shape(rows, lanes)] * 2 + [shape(AH, lanes)] * 4,
        in_specs=[vmem] * 5,
        out_specs=[vmem] * 8,
        compiler_params=pltpu.CompilerParams(vmem_limit_bytes=limit),
        name="pack",
    )(atm_state, ocean_state, depth, wet_mask, diffusivity)

    column_axes = ("sub", "comp")
    column_count = lax.axis_size("sub") * lax.axis_size("comp")
    axes = ("tile",) + column_axes

    def send(value, dt, dc):
        pairs = []
        for t in range(tile_count):
            for c in range(column_count):
                target = (t + dt) % tile_count * column_count + (c + dc) % column_count
                pairs.append((t * column_count + c, target))
        return lax.ppermute(value, axes, pairs)

    from_down = send(up, -1, 0)
    from_up = send(down, 1, 0)
    from_right = send(left, 0, -1)
    from_left = send(right, 0, 1)
    from_dr = send(lu, -1, -1)
    from_ur = send(ld, 1, -1)
    from_dl = send(ru, -1, 1)
    from_ul = send(rd, 1, 1)

    atm_cell = xg_atm_cell.reshape(1, cells)
    dest = xg_dest.reshape(1, cells)
    sea_cell = xg_ocean_cell.reshape(1, cells)
    weight = xg_weight.reshape(1, cells)
    surface = pl.BlockSpec((1, 1, rows, cols), lambda i: (0, 0, 0, 0))
    last = pl.BlockSpec((1, 1, rows, cols), lambda i: (2, levels - 1, 0, 0))

    message, wair = pl.pallas_call(
        send_kernel,
        grid=(1,),
        out_shape=[shape(tile_count, 3 * rows, cols), shape(1, cells)],
        in_specs=[vmem, surface] + [vmem] * 4,
        out_specs=[vmem] * 2,
        compiler_params=pltpu.CompilerParams(vmem_limit_bytes=limit),
        name="exchange_send",
    )(air_temp, ocean_state, atm_cell, dest, sea_cell, weight)
    got = lax.all_to_all(message, "tile", split_axis=0, concat_axis=0, tiled=True)

    atm_new, ocean_new = pl.pallas_call(
        step_kernel,
        out_shape=[shape(*atm_state.shape), shape(*ocean_state.shape)],
        in_specs=[pl.BlockSpec(memory_space=pltpu.SMEM)] + [vmem] * 13,
        out_specs=[vmem] * 2,
        scratch_shapes=[pltpu.VMEM((7, rows + 2 * AH, 2 * cols), F32)],
        compiler_params=pltpu.CompilerParams(vmem_limit_bytes=limit),
        name="steps",
    )(
        wave_speed,
        atm_state,
        ocean_state,
        depth,
        wet_mask,
        diffusivity,
        from_up,
        from_down,
        from_left,
        from_right,
        from_ul,
        from_dl,
        from_ur,
        from_dr,
    )

    return pl.pallas_call(
        flux_kernel,
        grid=(1,),
        out_shape=[shape(*atm_state.shape), shape(*ocean_state.shape)],
        in_specs=[vmem, surface] + [vmem] * 5 + [last, surface],
        out_specs=[last, surface],
        input_output_aliases={7: 0, 8: 1},
        compiler_params=pltpu.CompilerParams(vmem_limit_bytes=limit),
        name="exchange_receive",
    )(got, ocean_state, atm_cell, dest, sea_cell, weight, wair, atm_new, ocean_new)


def solution(mesh):
    grid = P(("member", "tile"), ("sub", "comp"))
    state = P(None, None, ("member", "tile"), ("sub", "comp"))
    cells = P(("member", "tile"), ("sub", "comp"), None)
    return jax.shard_map(
        functools.partial(on_device, mesh.shape["tile"]),
        mesh=mesh,
        in_specs=(
            state,
            grid,
            grid,
            P(),
            state,
            grid,
            grid,
            cells,
            P(("member", "tile"), ("sub", "comp"), None, None),
            cells,
            cells,
        ),
        out_specs=(state, state),
        check_vma=False,
    )
```

```python
import functools

import jax
import jax.numpy as jnp
from jax import lax
from jax.experimental import pallas as pl
from jax.experimental.pallas import tpu as pltpu
from jax.sharding import PartitionSpec as P

ACOUSTIC = 2
OCEAN_STEPS = 2
AH = 2 * ACOUSTIC
OH = OCEAN_STEPS

ATM_GAIN = 0.5
SEA_GAIN = 0.5

F32 = jnp.float32
BF16 = jnp.bfloat16


def lane_slots(levels, tracers):
    slots = [AH * i for i in range(3 * levels)]
    base = AH * 3 * levels
    slots += [base + OH * i for i in range(tracers)]
    base += OH * tracers
    slots += [base + AH * i for i in range(3)]
    total = base + 3 * AH
    return slots, -(-total // 128) * 128


def row_slots(levels, tracers):
    per = 3 * AH - 2
    base = per * levels
    misc = base + OH * tracers
    return per, base, misc, misc + AH + 2 * OH


def pack_kernel(*refs):
    sources, rest = refs[:11], refs[11:]
    atm, ocean, depth, wet, kappa = rest[:5]
    up, down, left, right, sems = rest[11:]
    copies = [
        pltpu.make_async_copy(source, target, sems.at[i])
        for i, (source, target) in enumerate(zip(sources, rest[:11]))
    ]
    for copy in copies:
        copy.start()
    levels = atm.shape[1]
    rows, cols = atm.shape[2:]
    tracers = ocean.shape[0] * ocean.shape[1]
    each = ocean.shape[1]
    per, obase, mbase, _ = row_slots(levels, tracers)
    slots, _ = lane_slots(levels, tracers)
    for copy in copies:
        copy.wait()
    wetness = wet[...].astype(F32)

    lane = lax.broadcasted_iota(jnp.int32, (rows, cols), 1)
    fields = [(atm, (k, l), AH) for k in range(3) for l in range(levels)]
    fields += [(ocean, (i // each, i % each), OH) for i in range(tracers)]
    fields += [(depth, None, AH), (None, None, AH), (kappa, None, AH)]
    packed = {}
    for (ref, at, width), slot in zip(fields, slots):
        value = wetness if ref is None else (ref[...] if at is None else ref[at[0], at[1]])
        tile, offset = slot // cols, slot % cols
        mask = (lane >= offset) & (lane < offset + width)
        first = pltpu.roll(value, offset, 1) if offset else value
        turn = (offset + width) % cols
        last = pltpu.roll(value, turn, 1) if turn else value
        if tile in packed:
            a, b = packed[tile]
            packed[tile] = (jnp.where(mask, first, a), jnp.where(mask, last, b))
        else:
            packed[tile] = (first, last)
    for tile, (a, b) in packed.items():
        where = slice(tile * cols, (tile + 1) * cols)
        left[:, where] = a
        right[:, where] = b

    for level in range(levels):
        base = per * level
        for at, which, width in ((0, 1, AH), (AH, 0, AH - 1), (2 * AH - 1, 2, AH - 1)):
            up[base + at : base + at + width, :] = atm[which, level, 0:width, :]
            down[base + at : base + at + width, :] = atm[which, level, rows - width : rows, :]
    for i in range(tracers):
        at = obase + OH * i
        up[at : at + OH, :] = ocean[i // each, i % each, 0:OH, :]
        down[at : at + OH, :] = ocean[i // each, i % each, rows - OH : rows, :]
    for at, value, width in (
        (mbase, depth[...], AH),
        (mbase + AH, wetness, OH),
        (mbase + AH + OH, kappa[...], OH),
    ):
        up[at : at + width, :] = value[0:width]
        down[at : at + width, :] = value[rows - width : rows]


def split3(value):
    hi = value.astype(BF16)
    rest = value - hi.astype(F32)
    mid = rest.astype(BF16)
    low = (rest - mid.astype(F32)).astype(BF16)
    return hi, mid, low


def one_hot(index, size):
    shape = (size, index.shape[-1])
    return lax.broadcasted_iota(jnp.int32, shape, 0) == index


def gather_rows(table, hot_rows, hot_cols):
    r = table.shape[0]
    parts = jnp.concatenate(split3(table), axis=0)
    g = jnp.dot(parts, hot_cols, preferred_element_type=F32)
    g = g[0:r] + g[r : 2 * r] + g[2 * r : 3 * r]
    return jnp.sum(jnp.where(hot_rows, g, 0.0), axis=0, keepdims=True)


def scatter_rows(values, hot_rows, hot_cols):
    r = hot_rows.shape[0]
    parts = []
    for value in values:
        for part in split3(value):
            parts.append(jnp.where(hot_rows, part.astype(F32), 0.0).astype(BF16))
    s = lax.dot_general(
        jnp.concatenate(parts, axis=0),
        hot_cols,
        (((1,), (1,)), ((), ())),
        preferred_element_type=F32,
    )
    out = []
    for i in range(len(values)):
        base = 3 * r * i
        out.append(s[base : base + r] + s[base + r : base + 2 * r] + s[base + 2 * r : base + 3 * r])
    return out


def send_kernel(air, ocean, atm_cell, dest, sea_cell, weight, from_left, from_right, message, wair_out):
    rows, cols = air.shape
    tiles = message.shape[0]
    tile_lanes = from_left.shape[1] // cols
    cell = atm_cell[...]
    hot_atm = jnp.where(one_hot(cell % cols, cols), 1.0, 0.0).astype(BF16)
    airx = gather_rows(air[...], one_hot(cell // cols, rows), hot_atm)
    w = weight[...]
    wair = w * airx
    wair_out[...] = wair
    cell = sea_cell[...]
    hot_sea = jnp.where(one_hot(cell % cols, cols), 1.0, 0.0).astype(BF16)
    row = dest[...] * rows + cell // cols
    surface = ocean[0, 0]
    for tile in range(tiles):
        s1, s2 = scatter_rows([wair, w], one_hot(row - tile * rows, rows), hot_sea)
        message[tile, 0:rows, :] = s1
        message[tile, rows : 2 * rows, :] = s2
        message[tile, 2 * rows : 3 * rows, :] = surface
        message[tile, 3 * rows :, :] = jnp.zeros((message.shape[1] - 3 * rows, cols), F32)
    me = lax.axis_index("tile")
    above, below = lax.rem(me + tiles - 1, tiles), lax.rem(me + 1, tiles)
    at = 3 * rows
    for ref in (from_left, from_right):
        for i in range(tile_lanes):
            where = slice(i * cols, (i + 1) * cols)
            message[above, at : at + AH, :] = ref[0:AH, where]
            message[below, at : at + AH, :] = ref[rows - AH : rows, where]
            at += AH


def final_kernel(
    speed,
    atm,
    ocean,
    depth,
    wet,
    kappa,
    atm_cell,
    dest,
    sea_cell,
    weight,
    wair,
    from_up,
    from_down,
    from_left,
    from_right,
    got,
    atm_out,
    ocean_out,
    us,
    vs,
    hs,
    fs,
    ms,
    atm_buf,
    ocean_buf,
    sems,
):
    levels = atm.shape[1]
    rows, cols = atm.shape[2:]
    tracers = ocean.shape[0] * ocean.shape[1]
    each = ocean.shape[1]
    per, obase, mbase, _ = row_slots(levels, tracers)
    slots, lanes = lane_slots(levels, tracers)
    full = rows + 2 * AH
    tiles = got.shape[0]
    me = lax.axis_index("tile")
    above, below = lax.rem(me + tiles - 1, tiles), lax.rem(me + 1, tiles)
    low_half = lax.broadcasted_iota(jnp.int32, (1, cols), 1) < cols // 2

    surface = ocean[0, 0]
    s1, s2 = got[0, 0:rows, :], got[0, rows : 2 * rows, :]
    for tile in range(1, tiles):
        s1 = s1 + got[tile, 0:rows, :]
        s2 = s2 + got[tile, rows : 2 * rows, :]
    sea_flux = s1 - surface * s2
    cell = sea_cell[...]
    hot_sea = jnp.where(one_hot(cell % cols, cols), 1.0, 0.0).astype(BF16)
    row = dest[...] * rows + cell // cols
    sstx = jnp.zeros(cell.shape, F32)
    for tile in range(tiles):
        table = got[tile, 2 * rows : 3 * rows, :]
        sstx = sstx + gather_rows(table, one_hot(row - tile * rows, rows), hot_sea)
    flux = wair[...] - weight[...] * sstx
    cell = atm_cell[...]
    hot_atm = jnp.where(one_hot(cell % cols, cols), 1.0, 0.0).astype(BF16)
    (atm_flux,) = scatter_rows([flux], one_hot(cell // cols, rows), hot_atm)

    def strips(slot, width, left_part, right_part):
        offset = slot % cols
        a, b = right_part(slot // cols), left_part(slot // cols)
        if offset:
            a = pltpu.roll(a, cols - offset, 1)
        turn = (cols - width - offset) % cols
        if turn:
            b = pltpu.roll(b, turn, 1)
        return jnp.where(low_half, a, b)

    def side(ref):
        return lambda i: ref[:, i * cols : (i + 1) * cols]

    def corner(tile, which):
        base = 3 * rows + which * AH * (lanes // cols)
        return lambda i: got[tile, base + AH * i : base + AH * (i + 1), :]

    def extend(view, value, row_at, row_width, slot, width):
        view[0:rows, 0:cols] = value
        view[rows : rows + row_width, 0:cols] = from_down[row_at : row_at + row_width, :]
        view[full - row_width : full, 0:cols] = from_up[row_at : row_at + row_width, :]
        view[0:rows, cols : 2 * cols] = strips(slot, width, side(from_left), side(from_right))
        view[rows : rows + AH, cols : 2 * cols] = strips(slot, width, corner(below, 0), corner(below, 1))
        view[full - AH : full, cols : 2 * cols] = strips(slot, width, corner(above, 0), corner(above, 1))

    def east(f):
        return pltpu.roll(f, 2 * cols - 1, 1)

    def west(f):
        return pltpu.roll(f, 1, 1)

    def south(f):
        return pltpu.roll(f, full - 1, 0)

    def north(f):
        return pltpu.roll(f, 1, 0)

    base = 3 * levels + tracers
    extend(ms.at[0], depth[...], mbase, AH, slots[base], AH)
    extend(ms.at[1], wet[...].astype(F32), mbase + AH, OH, slots[base + 1], AH)
    extend(ms.at[2], kappa[...], mbase + AH + OH, OH, slots[base + 2], AH)
    for i in range(tracers):
        extend(fs.at[i], ocean[i // each, i % each], obase + OH * i, OH, slots[3 * levels + i], OH)
    for level in range(levels):
        at = per * level
        extend(us.at[level], atm[0, level], at + AH, AH - 1, slots[level], AH)
        extend(vs.at[level], atm[1, level], at, AH, slots[levels + level], AH)
        extend(hs.at[level], atm[2, level], at + 2 * AH - 1, AH - 1, slots[2 * levels + level], AH)

    w = ms[1]
    k = ms[2]
    we, ww, ws, wn = east(w), west(w), south(w), north(w)
    for step in range(OCEAN_STEPS):
        for i in range(tracers):
            f = fs[i]
            total = we * (east(f) - f)
            total = total + ww * (west(f) - f)
            total = total + ws * (south(f) - f)
            total = total + wn * (north(f) - f)
            f = f + k * (w * total)
            if step < OCEAN_STEPS - 1:
                fs[i] = f
            else:
                f = f[0:rows, 0:cols]
                ocean_buf[i // each, i % each] = f + SEA_GAIN * sea_flux if i == 0 else f
    copies = [pltpu.make_async_copy(ocean_buf, ocean_out, sems.at[0])]
    copies[0].start()

    d = ms[0]
    chunk = max(1, levels // 4)
    for step in range(ACOUSTIC):
        for level in range(levels):
            u, v = us[level], vs[level]
            column_speed = speed[level] * d
            hs[level] = hs[level] - column_speed * (
                (east(u) - west(u)) * 0.5 + (south(v) - north(v)) * 0.5
            )
        for level in range(levels):
            u, v, h = us[level], vs[level], hs[level]
            u = u - (east(h) - west(h)) * 0.5
            v = v - (south(h) - north(h)) * 0.5
            if step < ACOUSTIC - 1:
                us[level], vs[level] = u, v
            else:
                h = h[0:rows, 0:cols]
                atm_buf[0, level] = u[0:rows, 0:cols]
                atm_buf[1, level] = v[0:rows, 0:cols]
                atm_buf[2, level] = h - ATM_GAIN * atm_flux if level == levels - 1 else h
                if (level + 1) % chunk == 0:
                    where = pl.ds(level + 1 - chunk, chunk)
                    copies.append(
                        pltpu.make_async_copy(
                            atm_buf.at[:, where], atm_out.at[:, where], sems.at[len(copies)]
                        )
                    )
                    copies[-1].start()
    for copy in copies:
        copy.wait()


def on_device(
    tile_count,
    atm_state,
    air_temp,
    depth,
    wave_speed,
    ocean_state,
    wet_mask,
    diffusivity,
    xg_atm_cell,
    xg_dest,
    xg_ocean_cell,
    xg_weight,
):
    levels = atm_state.shape[1]
    rows, cols = atm_state.shape[2:]
    tracers = ocean_state.shape[0] * ocean_state.shape[1]
    cells = xg_weight.shape[-1]
    _, lanes = lane_slots(levels, tracers)
    _, _, _, message_rows = row_slots(levels, tracers)
    vmem = pl.BlockSpec(memory_space=pltpu.VMEM)
    hbm = pl.BlockSpec(memory_space=pltpu.HBM)
    smem = pl.BlockSpec(memory_space=pltpu.SMEM)
    params = pltpu.CompilerParams(vmem_limit_bytes=32 * 1024 * 1024)
    full = rows + 2 * AH

    def shape(*dims):
        return jax.ShapeDtypeStruct(dims, F32)

    operands = (
        atm_state,
        ocean_state,
        depth,
        wet_mask,
        diffusivity,
        air_temp,
        xg_atm_cell.reshape(1, cells),
        xg_dest.reshape(1, cells),
        xg_ocean_cell.reshape(1, cells),
        xg_weight.reshape(1, cells),
        wave_speed,
    )
    atm, ocean, dep, wet, kappa, air, atm_cell, dest, sea_cell, weight, speed, up, down, left, right = pl.pallas_call(
        pack_kernel,
        out_shape=[jax.ShapeDtypeStruct(x.shape, x.dtype) for x in operands]
        + [shape(message_rows, cols)] * 2
        + [shape(rows, lanes)] * 2,
        in_specs=[hbm] * 11,
        out_specs=[vmem] * 10 + [smem] + [vmem] * 4,
        scratch_shapes=[pltpu.SemaphoreType.DMA((11,))],
        compiler_params=params,
        name="pack",
    )(*operands)

    column_axes = ("sub", "comp")
    column_count = lax.axis_size("sub") * lax.axis_size("comp")

    def shift(value, axes, count, by):
        return lax.ppermute(value, axes, [(i, (i + by) % count) for i in range(count)])

    from_right = shift(left, column_axes, column_count, -1)
    from_left = shift(right, column_axes, column_count, 1)
    from_down = shift(up, "tile", tile_count, -1)
    from_up = shift(down, "tile", tile_count, 1)

    corner_rows = 2 * AH * (lanes // cols)
    message, wair = pl.pallas_call(
        send_kernel,
        out_shape=[shape(tile_count, 3 * rows + corner_rows, cols), shape(1, cells)],
        in_specs=[vmem] * 8,
        out_specs=[vmem] * 2,
        compiler_params=params,
        name="exchange_send",
    )(air, ocean, atm_cell, dest, sea_cell, weight, from_left, from_right)
    got = lax.all_to_all(message, "tile", split_axis=0, concat_axis=0, tiled=True)

    return tuple(
        pl.pallas_call(
            final_kernel,
            out_shape=[shape(*atm_state.shape), shape(*ocean_state.shape)],
            in_specs=[smem] + [vmem] * 15,
            out_specs=[hbm] * 2,
            scratch_shapes=[pltpu.VMEM((levels, full, 2 * cols), F32)] * 3
            + [
                pltpu.VMEM((tracers, full, 2 * cols), F32),
                pltpu.VMEM((3, full, 2 * cols), F32),
                pltpu.VMEM(atm_state.shape, F32),
                pltpu.VMEM(ocean_state.shape, F32),
                pltpu.SemaphoreType.DMA((8,)),
            ],
            compiler_params=params,
            name="steps",
        )(
            speed,
            atm,
            ocean,
            dep,
            wet,
            kappa,
            atm_cell,
            dest,
            sea_cell,
            weight,
            wair,
            from_up,
            from_down,
            from_left,
            from_right,
            got,
        )
    )


def solution(mesh):
    grid = P(("member", "tile"), ("sub", "comp"))
    state = P(None, None, ("member", "tile"), ("sub", "comp"))
    cells = P(("member", "tile"), ("sub", "comp"), None)
    return jax.shard_map(
        functools.partial(on_device, mesh.shape["tile"]),
        mesh=mesh,
        in_specs=(
            state,
            grid,
            grid,
            P(),
            state,
            grid,
            grid,
            cells,
            P(("member", "tile"), ("sub", "comp"), None, None),
            cells,
            cells,
        ),
        out_specs=(state, state),
        check_vma=False,
    )
```

```python
import functools

import jax
import jax.numpy as jnp
from jax import lax
from jax.experimental import pallas as pl
from jax.experimental.pallas import tpu as pltpu
from jax.sharding import PartitionSpec as P

ACOUSTIC = 2
OCEAN_STEPS = 2
AH = 2 * ACOUSTIC
OH = OCEAN_STEPS

ATM_GAIN = 0.5
SEA_GAIN = 0.5

F32 = jnp.float32
BF16 = jnp.bfloat16


def lane_slots(levels, tracers):
    slots = [AH * i for i in range(3 * levels)]
    base = AH * 3 * levels
    slots += [base + OH * i for i in range(tracers)]
    base += OH * tracers
    slots += [base + AH * i for i in range(3)]
    total = base + 3 * AH
    return slots, -(-total // 128) * 128


def row_slots(levels, tracers):
    per = 3 * AH - 2
    base = per * levels
    misc = base + OH * tracers
    return per, base, misc, misc + AH + 2 * OH


def pack_kernel(*refs):
    sources, (up, down, left, right), held, sems = refs[:5], refs[5:9], refs[9:14], refs[14]
    atm, ocean, depth, wet, kappa = held
    copies = [
        pltpu.make_async_copy(source, target, sems.at[i])
        for i, (source, target) in enumerate(zip(sources, held))
    ]
    for copy in copies:
        copy.start()
    levels = atm.shape[1]
    rows, cols = atm.shape[2:]
    tracers = ocean.shape[0] * ocean.shape[1]
    each = ocean.shape[1]
    per, obase, mbase, _ = row_slots(levels, tracers)
    slots, _ = lane_slots(levels, tracers)
    for copy in copies:
        copy.wait()
    wetness = wet[...].astype(F32)

    lane = lax.broadcasted_iota(jnp.int32, (rows, cols), 1)
    fields = [(atm, (k, l), AH) for k in range(3) for l in range(levels)]
    fields += [(ocean, (i // each, i % each), OH) for i in range(tracers)]
    fields += [(depth, None, AH), (None, None, AH), (kappa, None, AH)]
    packed = {}
    for (ref, at, width), slot in zip(fields, slots):
        value = wetness if ref is None else (ref[...] if at is None else ref[at[0], at[1]])
        tile, offset = slot // cols, slot % cols
        mask = (lane >= offset) & (lane < offset + width)
        first = pltpu.roll(value, offset, 1) if offset else value
        turn = (offset + width) % cols
        last = pltpu.roll(value, turn, 1) if turn else value
        if tile in packed:
            a, b = packed[tile]
            packed[tile] = (jnp.where(mask, first, a), jnp.where(mask, last, b))
        else:
            packed[tile] = (first, last)
    for tile, (a, b) in packed.items():
        where = slice(tile * cols, (tile + 1) * cols)
        left[:, where] = a
        right[:, where] = b

    for level in range(levels):
        base = per * level
        for at, which, width in ((0, 1, AH), (AH, 0, AH - 1), (2 * AH - 1, 2, AH - 1)):
            up[base + at : base + at + width, :] = atm[which, level, 0:width, :]
            down[base + at : base + at + width, :] = atm[which, level, rows - width : rows, :]
    for i in range(tracers):
        at = obase + OH * i
        up[at : at + OH, :] = ocean[i // each, i % each, 0:OH, :]
        down[at : at + OH, :] = ocean[i // each, i % each, rows - OH : rows, :]
    for at, value, width in (
        (mbase, depth[...], AH),
        (mbase + AH, wetness, OH),
        (mbase + AH + OH, kappa[...], OH),
    ):
        up[at : at + width, :] = value[0:width]
        down[at : at + width, :] = value[rows - width : rows]


def split3(value):
    hi = value.astype(BF16)
    rest = value - hi.astype(F32)
    mid = rest.astype(BF16)
    low = (rest - mid.astype(F32)).astype(BF16)
    return hi, mid, low


def one_hot(index, size):
    shape = (size, index.shape[-1])
    return lax.broadcasted_iota(jnp.int32, shape, 0) == index


def gather_rows(table, hot_rows, hot_cols):
    r = table.shape[0]
    parts = jnp.concatenate(split3(table), axis=0)
    g = jnp.dot(parts, hot_cols, preferred_element_type=F32)
    g = g[0:r] + g[r : 2 * r] + g[2 * r : 3 * r]
    return jnp.sum(jnp.where(hot_rows, g, 0.0), axis=0, keepdims=True)


def scatter_rows(values, hot_rows, hot_cols):
    r = hot_rows.shape[0]
    parts = []
    for value in values:
        for part in split3(value):
            parts.append(jnp.where(hot_rows, part.astype(F32), 0.0).astype(BF16))
    s = lax.dot_general(
        jnp.concatenate(parts, axis=0),
        hot_cols,
        (((1,), (1,)), ((), ())),
        preferred_element_type=F32,
    )
    out = []
    for i in range(len(values)):
        base = 3 * r * i
        out.append(s[base : base + r] + s[base + r : base + 2 * r] + s[base + 2 * r : base + 3 * r])
    return out


def send_kernel(*refs):
    sources, (message, wair_out), held, sems = refs[:8], refs[8:10], refs[10:18], refs[18]
    air, surface, atm_cell, dest, sea_cell, weight, from_left, from_right = held
    copies = [
        pltpu.make_async_copy(source.at[0, 0] if i == 1 else source, target, sems.at[i])
        for i, (source, target) in enumerate(zip(sources, held))
    ]
    for copy in copies:
        copy.start()
    for copy in copies:
        copy.wait()
    rows, cols = air.shape
    tiles = message.shape[0]
    tile_lanes = from_left.shape[1] // cols
    cell = atm_cell[...]
    hot_atm = jnp.where(one_hot(cell % cols, cols), 1.0, 0.0).astype(BF16)
    airx = gather_rows(air[...], one_hot(cell // cols, rows), hot_atm)
    w = weight[...]
    wair = w * airx
    wair_out[...] = wair
    cell = sea_cell[...]
    hot_sea = jnp.where(one_hot(cell % cols, cols), 1.0, 0.0).astype(BF16)
    row = dest[...] * rows + cell // cols
    for tile in range(tiles):
        s1, s2 = scatter_rows([wair, w], one_hot(row - tile * rows, rows), hot_sea)
        message[tile, 0:rows, :] = s1
        message[tile, rows : 2 * rows, :] = s2
        message[tile, 2 * rows : 3 * rows, :] = surface[...]
        message[tile, 3 * rows :, :] = jnp.zeros((message.shape[1] - 3 * rows, cols), F32)
    me = lax.axis_index("tile")
    above, below = lax.rem(me + tiles - 1, tiles), lax.rem(me + 1, tiles)
    at = 3 * rows
    for ref in (from_left, from_right):
        for i in range(tile_lanes):
            where = slice(i * cols, (i + 1) * cols)
            message[above, at : at + AH, :] = ref[0:AH, where]
            message[below, at : at + AH, :] = ref[rows - AH : rows, where]
            at += AH


def strips(cols, slot, width, left_part, right_part):
    low_half = lax.broadcasted_iota(jnp.int32, (1, cols), 1) < cols // 2
    offset = slot % cols
    a, b = right_part(slot // cols), left_part(slot // cols)
    if offset:
        a = pltpu.roll(a, cols - offset, 1)
    turn = (cols - width - offset) % cols
    if turn:
        b = pltpu.roll(b, turn, 1)
    return jnp.where(low_half, a, b)


def extend_kernel(atm, ocean, depth, wet, kappa, from_up, from_down, from_left, from_right, us, vs, hs, fs, ms):
    levels = atm.shape[1]
    rows, cols = atm.shape[2:]
    tracers = ocean.shape[0] * ocean.shape[1]
    each = ocean.shape[1]
    per, obase, mbase, _ = row_slots(levels, tracers)
    slots, _ = lane_slots(levels, tracers)
    full = rows + 2 * AH

    def side(ref):
        return lambda i: ref[:, i * cols : (i + 1) * cols]

    def extend(view, value, row_at, row_width, slot, width):
        view[0:rows, 0:cols] = value
        view[rows : rows + row_width, 0:cols] = from_down[row_at : row_at + row_width, :]
        view[full - row_width : full, 0:cols] = from_up[row_at : row_at + row_width, :]
        view[0:rows, cols : 2 * cols] = strips(cols, slot, width, side(from_left), side(from_right))

    base = 3 * levels + tracers
    extend(ms.at[0], depth[...], mbase, AH, slots[base], AH)
    extend(ms.at[1], wet[...].astype(F32), mbase + AH, OH, slots[base + 1], AH)
    extend(ms.at[2], kappa[...], mbase + AH + OH, OH, slots[base + 2], AH)
    for i in range(tracers):
        extend(fs.at[i], ocean[i // each, i % each], obase + OH * i, OH, slots[3 * levels + i], OH)
    for level in range(levels):
        at = per * level
        extend(us.at[level], atm[0, level], at + AH, AH - 1, slots[level], AH)
        extend(vs.at[level], atm[1, level], at, AH, slots[levels + level], AH)
        extend(hs.at[level], atm[2, level], at + 2 * AH - 1, AH - 1, slots[2 * levels + level], AH)


def final_kernel(
    speed,
    us_in,
    vs_in,
    hs_in,
    fs_in,
    ms_in,
    ocean,
    atm_cell,
    dest,
    sea_cell,
    weight,
    wair,
    got,
    atm_out,
    ocean_out,
    us,
    vs,
    hs,
    fs,
    edge,
    atm_buf,
    ocean_buf,
    sems,
):
    levels = us.shape[0]
    rows, cols = ocean.shape[2:]
    tracers = fs.shape[0]
    each = ocean.shape[1]
    slots, lanes = lane_slots(levels, tracers)
    full = rows + 2 * AH
    tiles = got.shape[0]
    me = lax.axis_index("tile")
    above, below = lax.rem(me + tiles - 1, tiles), lax.rem(me + 1, tiles)

    surface = ocean[0, 0]
    s1, s2 = got[0, 0:rows, :], got[0, rows : 2 * rows, :]
    for tile in range(1, tiles):
        s1 = s1 + got[tile, 0:rows, :]
        s2 = s2 + got[tile, rows : 2 * rows, :]
    sea_flux = s1 - surface * s2
    cell = sea_cell[...]
    hot_sea = jnp.where(one_hot(cell % cols, cols), 1.0, 0.0).astype(BF16)
    row = dest[...] * rows + cell // cols
    sstx = jnp.zeros(cell.shape, F32)
    for tile in range(tiles):
        table = got[tile, 2 * rows : 3 * rows, :]
        sstx = sstx + gather_rows(table, one_hot(row - tile * rows, rows), hot_sea)
    flux = wair[...] - weight[...] * sstx
    cell = atm_cell[...]
    hot_atm = jnp.where(one_hot(cell % cols, cols), 1.0, 0.0).astype(BF16)
    (atm_flux,) = scatter_rows([flux], one_hot(cell // cols, rows), hot_atm)

    for i in range(2 * (lanes // cols)):
        at = 3 * rows + AH * i
        edge[i, 0:AH, :] = got[below, at : at + AH, :]
        edge[i, AH : 2 * AH, :] = got[above, at : at + AH, :]
    half = lanes // cols

    def load(ref, i, slot, width):
        corner = strips(cols, slot, width, lambda t: edge[t], lambda t: edge[half + t])
        outer = jnp.concatenate([ref[i, rows:full, 0:cols], corner], axis=1)
        return jnp.concatenate([ref[i, 0:rows, :], outer], axis=0)

    def east(f):
        return pltpu.roll(f, 2 * cols - 1, 1)

    def west(f):
        return pltpu.roll(f, 1, 1)

    def south(f):
        return pltpu.roll(f, full - 1, 0)

    def north(f):
        return pltpu.roll(f, 1, 0)

    base = 3 * levels + tracers
    w = load(ms_in, 1, slots[base + 1], AH)
    k = load(ms_in, 2, slots[base + 2], AH)
    we, ww, ws, wn = east(w), west(w), south(w), north(w)
    for step in range(OCEAN_STEPS):
        for i in range(tracers):
            f = load(fs_in, i, slots[3 * levels + i], OH) if step == 0 else fs[i]
            total = we * (east(f) - f)
            total = total + ww * (west(f) - f)
            total = total + ws * (south(f) - f)
            total = total + wn * (north(f) - f)
            f = f + k * (w * total)
            if step < OCEAN_STEPS - 1:
                fs[i] = f
            else:
                f = f[0:rows, 0:cols]
                ocean_buf[i // each, i % each] = f + SEA_GAIN * sea_flux if i == 0 else f
    copies = [pltpu.make_async_copy(ocean_buf, ocean_out, sems.at[0])]
    copies[0].start()

    d = load(ms_in, 0, slots[base], AH)
    chunk = max(1, levels // 4)
    for step in range(ACOUSTIC):
        for level in range(levels):
            if step == 0:
                u = load(us_in, level, slots[level], AH)
                v = load(vs_in, level, slots[levels + level], AH)
                h = load(hs_in, level, slots[2 * levels + level], AH)
                us[level], vs[level] = u, v
            else:
                u, v, h = us[level], vs[level], hs[level]
            column_speed = speed[level] * d
            hs[level] = h - column_speed * ((east(u) - west(u)) * 0.5 + (south(v) - north(v)) * 0.5)
        for level in range(levels):
            u, v, h = us[level], vs[level], hs[level]
            u = u - (east(h) - west(h)) * 0.5
            v = v - (south(h) - north(h)) * 0.5
            if step < ACOUSTIC - 1:
                us[level], vs[level] = u, v
            else:
                h = h[0:rows, 0:cols]
                atm_buf[0, level] = u[0:rows, 0:cols]
                atm_buf[1, level] = v[0:rows, 0:cols]
                atm_buf[2, level] = h - ATM_GAIN * atm_flux if level == levels - 1 else h
                if (level + 1) % chunk == 0:
                    where = pl.ds(level + 1 - chunk, chunk)
                    copies.append(
                        pltpu.make_async_copy(
                            atm_buf.at[:, where], atm_out.at[:, where], sems.at[len(copies)]
                        )
                    )
                    copies[-1].start()
    for copy in copies:
        copy.wait()


def on_device(
    tile_count,
    atm_state,
    air_temp,
    depth,
    wave_speed,
    ocean_state,
    wet_mask,
    diffusivity,
    xg_atm_cell,
    xg_dest,
    xg_ocean_cell,
    xg_weight,
):
    levels = atm_state.shape[1]
    rows, cols = atm_state.shape[2:]
    tracers = ocean_state.shape[0] * ocean_state.shape[1]
    cells = xg_weight.shape[-1]
    _, lanes = lane_slots(levels, tracers)
    _, _, _, message_rows = row_slots(levels, tracers)
    vmem = pl.BlockSpec(memory_space=pltpu.VMEM)
    hbm = pl.BlockSpec(memory_space=pltpu.HBM)
    smem = pl.BlockSpec(memory_space=pltpu.SMEM)
    params = pltpu.CompilerParams(vmem_limit_bytes=16 * 1024 * 1024)
    whole = pltpu.CompilerParams(vmem_limit_bytes=64 * 1024 * 1024)
    full = rows + 2 * AH

    def shape(*dims):
        return jax.ShapeDtypeStruct(dims, F32)

    fields = (atm_state, ocean_state, depth, wet_mask, diffusivity)
    up, down, left, right = pl.pallas_call(
        pack_kernel,
        out_shape=[shape(message_rows, cols)] * 2 + [shape(rows, lanes)] * 2,
        in_specs=[hbm] * 5,
        out_specs=[vmem] * 4,
        scratch_shapes=[pltpu.VMEM(x.shape, x.dtype) for x in fields] + [pltpu.SemaphoreType.DMA((5,))],
        compiler_params=whole,
        name="pack",
    )(*fields)
    atm_cell = xg_atm_cell.reshape(1, cells)
    dest = xg_dest.reshape(1, cells)
    sea_cell = xg_ocean_cell.reshape(1, cells)
    weight = xg_weight.reshape(1, cells)

    column_axes = ("sub", "comp")
    column_count = lax.axis_size("sub") * lax.axis_size("comp")

    def shift(value, axes, count, by):
        return lax.ppermute(value, axes, [(i, (i + by) % count) for i in range(count)])

    from_right = shift(left, column_axes, column_count, -1)
    from_left = shift(right, column_axes, column_count, 1)
    from_down = shift(up, "tile", tile_count, -1)
    from_up = shift(down, "tile", tile_count, 1)

    corner_rows = 2 * AH * (lanes // cols)
    message, wair = pl.pallas_call(
        send_kernel,
        out_shape=[shape(tile_count, 3 * rows + corner_rows, cols), shape(1, cells)],
        in_specs=[hbm] * 8,
        out_specs=[vmem] * 2,
        scratch_shapes=[pltpu.VMEM((rows, cols), F32)] * 2
        + [pltpu.VMEM((1, cells), jnp.int32)] * 3
        + [pltpu.VMEM((1, cells), F32)]
        + [pltpu.VMEM((rows, lanes), F32)] * 2
        + [pltpu.SemaphoreType.DMA((8,))],
        compiler_params=whole,
        cost_estimate=pl.CostEstimate(flops=0, bytes_accessed=20_000_000, transcendentals=0),
        name="exchange_send",
    )(air_temp, ocean_state, atm_cell, dest, sea_cell, weight, from_left, from_right)
    got = lax.all_to_all(message, "tile", split_axis=0, concat_axis=0, tiled=True)

    extended = [shape(levels, full, 2 * cols)] * 3 + [shape(tracers, full, 2 * cols), shape(3, full, 2 * cols)]
    us, vs, hs, fs, ms = pl.pallas_call(
        extend_kernel,
        out_shape=extended,
        in_specs=[vmem] * 9,
        out_specs=[vmem] * 5,
        compiler_params=params,
        cost_estimate=pl.CostEstimate(flops=0, bytes_accessed=8_000_000, transcendentals=0),
        name="extend",
    )(*fields, from_up, from_down, from_left, from_right)

    results = pl.pallas_call(
        final_kernel,
        out_shape=[shape(*atm_state.shape), shape(*ocean_state.shape)],
        in_specs=[smem] + [vmem] * 12,
        out_specs=[hbm] * 2,
        scratch_shapes=[pltpu.VMEM(x.shape, F32) for x in extended[:4]]
        + [
            pltpu.VMEM((2 * (lanes // cols), 2 * AH, cols), F32),
            pltpu.VMEM(atm_state.shape, F32),
            pltpu.VMEM(ocean_state.shape, F32),
            pltpu.SemaphoreType.DMA((8,)),
        ],
        compiler_params=params,
        name="steps",
    )(wave_speed, us, vs, hs, fs, ms, ocean_state, atm_cell, dest, sea_cell, weight, wair, got)
    return tuple(results)


def solution(mesh):
    grid = P(("member", "tile"), ("sub", "comp"))
    state = P(None, None, ("member", "tile"), ("sub", "comp"))
    cells = P(("member", "tile"), ("sub", "comp"), None)
    return jax.shard_map(
        functools.partial(on_device, mesh.shape["tile"]),
        mesh=mesh,
        in_specs=(
            state,
            grid,
            grid,
            P(),
            state,
            grid,
            grid,
            cells,
            P(("member", "tile"), ("sub", "comp"), None, None),
            cells,
            cells,
        ),
        out_specs=(state, state),
        check_vma=False,
    )
```

```python
import functools

import jax
import jax.numpy as jnp
from jax import lax
from jax.experimental import pallas as pl
from jax.experimental.pallas import tpu as pltpu
from jax.sharding import PartitionSpec as P

ACOUSTIC = 2
OCEAN_STEPS = 2
AH = 2 * ACOUSTIC
OH = OCEAN_STEPS

ATM_GAIN = 0.5
SEA_GAIN = 0.5

F32 = jnp.float32
BF16 = jnp.bfloat16


def lane_slots(levels, tracers):
    slots = [AH * i for i in range(3 * levels)]
    base = AH * 3 * levels
    slots += [base + OH * i for i in range(tracers)]
    base += OH * tracers
    slots += [base + AH * i for i in range(3)]
    total = base + 3 * AH
    return slots, -(-total // 128) * 128


def row_slots(levels, tracers):
    per = 3 * AH - 2
    base = per * levels
    misc = base + OH * tracers
    return per, base, misc, misc + AH + 2 * OH


def pack_kernel(*refs):
    sources, (up, down, left, right), held, sems = refs[:5], refs[5:9], refs[9:14], refs[14]
    atm, ocean, depth, wet, kappa = held
    copies = [
        pltpu.make_async_copy(source, target, sems.at[i])
        for i, (source, target) in enumerate(zip(sources, held))
    ]
    for copy in copies:
        copy.start()
    levels = atm.shape[1]
    rows, cols = atm.shape[2:]
    tracers = ocean.shape[0] * ocean.shape[1]
    each = ocean.shape[1]
    per, obase, mbase, _ = row_slots(levels, tracers)
    slots, _ = lane_slots(levels, tracers)
    for copy in copies:
        copy.wait()
    wetness = wet[...].astype(F32)

    lane = lax.broadcasted_iota(jnp.int32, (rows, cols), 1)
    fields = [(atm, (k, l), AH) for k in range(3) for l in range(levels)]
    fields += [(ocean, (i // each, i % each), OH) for i in range(tracers)]
    fields += [(depth, None, AH), (None, None, AH), (kappa, None, AH)]
    packed = {}
    for (ref, at, width), slot in zip(fields, slots):
        value = wetness if ref is None else (ref[...] if at is None else ref[at[0], at[1]])
        tile, offset = slot // cols, slot % cols
        mask = (lane >= offset) & (lane < offset + width)
        first = pltpu.roll(value, offset, 1) if offset else value
        turn = (offset + width) % cols
        last = pltpu.roll(value, turn, 1) if turn else value
        if tile in packed:
            a, b = packed[tile]
            packed[tile] = (jnp.where(mask, first, a), jnp.where(mask, last, b))
        else:
            packed[tile] = (first, last)
    for tile, (a, b) in packed.items():
        where = slice(tile * cols, (tile + 1) * cols)
        left[:, where] = a
        right[:, where] = b

    for level in range(levels):
        base = per * level
        for at, which, width in ((0, 1, AH), (AH, 0, AH - 1), (2 * AH - 1, 2, AH - 1)):
            up[base + at : base + at + width, :] = atm[which, level, 0:width, :]
            down[base + at : base + at + width, :] = atm[which, level, rows - width : rows, :]
    for i in range(tracers):
        at = obase + OH * i
        up[at : at + OH, :] = ocean[i // each, i % each, 0:OH, :]
        down[at : at + OH, :] = ocean[i // each, i % each, rows - OH : rows, :]
    for at, value, width in (
        (mbase, depth[...], AH),
        (mbase + AH, wetness, OH),
        (mbase + AH + OH, kappa[...], OH),
    ):
        up[at : at + width, :] = value[0:width]
        down[at : at + width, :] = value[rows - width : rows]


def split3(value):
    hi = value.astype(BF16)
    rest = value - hi.astype(F32)
    mid = rest.astype(BF16)
    low = (rest - mid.astype(F32)).astype(BF16)
    return hi, mid, low


def one_hot(index, size):
    shape = (size, index.shape[-1])
    return lax.broadcasted_iota(jnp.int32, shape, 0) == index


def gather_rows(table, hot_rows, hot_cols):
    r = table.shape[0]
    parts = jnp.concatenate(split3(table), axis=0)
    g = jnp.dot(parts, hot_cols, preferred_element_type=F32)
    g = g[0:r] + g[r : 2 * r] + g[2 * r : 3 * r]
    return jnp.sum(jnp.where(hot_rows, g, 0.0), axis=0, keepdims=True)


def scatter_rows(values, hot_rows, hot_cols):
    r = hot_rows.shape[0]
    parts = []
    for value in values:
        for part in split3(value):
            parts.append(jnp.where(hot_rows, part.astype(F32), 0.0).astype(BF16))
    s = lax.dot_general(
        jnp.concatenate(parts, axis=0),
        hot_cols,
        (((1,), (1,)), ((), ())),
        preferred_element_type=F32,
    )
    out = []
    for i in range(len(values)):
        base = 3 * r * i
        out.append(s[base : base + r] + s[base + r : base + 2 * r] + s[base + 2 * r : base + 3 * r])
    return out


def send_kernel(*refs):
    sources, (message, wair_out), held, sems = refs[:8], refs[8:10], refs[10:18], refs[18]
    air, surface, atm_cell, dest, sea_cell, weight, from_left, from_right = held
    copies = [
        pltpu.make_async_copy(source.at[0, 0] if i == 1 else source, target, sems.at[i])
        for i, (source, target) in enumerate(zip(sources, held))
    ]
    for copy in copies:
        copy.start()
    for copy in copies:
        copy.wait()
    rows, cols = air.shape
    tiles = message.shape[0]
    tile_lanes = from_left.shape[1] // cols
    cell = atm_cell[...]
    hot_atm = jnp.where(one_hot(cell % cols, cols), 1.0, 0.0).astype(BF16)
    airx = gather_rows(air[...], one_hot(cell // cols, rows), hot_atm)
    w = weight[...]
    wair = w * airx
    wair_out[...] = wair
    cell = sea_cell[...]
    hot_sea = jnp.where(one_hot(cell % cols, cols), 1.0, 0.0).astype(BF16)
    row = dest[...] * rows + cell // cols
    for tile in range(tiles):
        s1, s2 = scatter_rows([wair, w], one_hot(row - tile * rows, rows), hot_sea)
        message[tile, 0:rows, :] = s1
        message[tile, rows : 2 * rows, :] = s2
        message[tile, 2 * rows : 3 * rows, :] = surface[...]
        message[tile, 3 * rows :, :] = jnp.zeros((message.shape[1] - 3 * rows, cols), F32)
    me = lax.axis_index("tile")
    above, below = lax.rem(me + tiles - 1, tiles), lax.rem(me + 1, tiles)
    at = 3 * rows
    for ref in (from_left, from_right):
        for i in range(tile_lanes):
            where = slice(i * cols, (i + 1) * cols)
            message[above, at : at + AH, :] = ref[0:AH, where]
            message[below, at : at + AH, :] = ref[rows - AH : rows, where]
            at += AH


def strips(cols, slot, width, left_part, right_part):
    low_half = lax.broadcasted_iota(jnp.int32, (1, cols), 1) < cols // 2
    offset = slot % cols
    a, b = right_part(slot // cols), left_part(slot // cols)
    if offset:
        a = pltpu.roll(a, cols - offset, 1)
    turn = (cols - width - offset) % cols
    if turn:
        b = pltpu.roll(b, turn, 1)
    return jnp.where(low_half, a, b)


def row_slices(levels, tracers):
    per, obase, mbase, _ = row_slots(levels, tracers)
    out = [(per * level + AH, AH - 1) for level in range(levels)]
    out += [(per * level, AH) for level in range(levels)]
    out += [(per * level + 2 * AH - 1, AH - 1) for level in range(levels)]
    out += [(obase + OH * i, OH) for i in range(tracers)]
    return out + [(mbase, AH), (mbase + AH, OH), (mbase + AH + OH, OH)]


def regroup_kernel(slices, from_up, from_down, tiles):
    for i, (at, width) in enumerate(slices):
        tiles[i, 0:width, :] = from_down[at : at + width, :]
        tiles[i, 2 * AH - width : 2 * AH, :] = from_up[at : at + width, :]


def final_kernel(
    speed,
    atm,
    ocean,
    depth,
    wet,
    kappa,
    atm_cell,
    dest,
    sea_cell,
    weight,
    wair,
    row_tiles,
    from_left,
    from_right,
    got,
    atm_out,
    ocean_out,
    us,
    vs,
    hs,
    fs,
    ms,
    edge,
    atm_buf,
    ocean_buf,
    sems,
):
    levels = atm.shape[1]
    rows, cols = atm.shape[2:]
    tracers = fs.shape[0]
    each = ocean.shape[1]
    slots, lanes = lane_slots(levels, tracers)
    full = rows + 2 * AH
    tiles = got.shape[0]
    me = lax.axis_index("tile")
    above, below = lax.rem(me + tiles - 1, tiles), lax.rem(me + 1, tiles)

    surface = ocean[0, 0]
    s1, s2 = got[0, 0:rows, :], got[0, rows : 2 * rows, :]
    for tile in range(1, tiles):
        s1 = s1 + got[tile, 0:rows, :]
        s2 = s2 + got[tile, rows : 2 * rows, :]
    sea_flux = s1 - surface * s2
    cell = sea_cell[...]
    hot_sea = jnp.where(one_hot(cell % cols, cols), 1.0, 0.0).astype(BF16)
    row = dest[...] * rows + cell // cols
    sstx = jnp.zeros(cell.shape, F32)
    for tile in range(tiles):
        table = got[tile, 2 * rows : 3 * rows, :]
        sstx = sstx + gather_rows(table, one_hot(row - tile * rows, rows), hot_sea)
    flux = wair[...] - weight[...] * sstx
    cell = atm_cell[...]
    hot_atm = jnp.where(one_hot(cell % cols, cols), 1.0, 0.0).astype(BF16)
    (atm_flux,) = scatter_rows([flux], one_hot(cell // cols, rows), hot_atm)

    for i in range(2 * (lanes // cols)):
        at = 3 * rows + AH * i
        edge[i, 0:AH, :] = got[below, at : at + AH, :]
        edge[i, AH : 2 * AH, :] = got[above, at : at + AH, :]
    half = lanes // cols

    def extend(view, value, field, width):
        slot = slots[field]
        view[0:rows, 0:cols] = value
        view[rows:full, 0:cols] = row_tiles[field]
        view[0:rows, cols : 2 * cols] = strips(
            cols, slot, width, lambda t: from_left[:, t * cols : (t + 1) * cols], lambda t: from_right[:, t * cols : (t + 1) * cols]
        )
        view[rows:full, cols : 2 * cols] = strips(cols, slot, width, lambda t: edge[t], lambda t: edge[half + t])

    def east(f):
        return pltpu.roll(f, 2 * cols - 1, 1)

    def west(f):
        return pltpu.roll(f, 1, 1)

    def south(f):
        return pltpu.roll(f, full - 1, 0)

    def north(f):
        return pltpu.roll(f, 1, 0)

    base = 3 * levels + tracers
    extend(ms.at[0], depth[...], base, AH)
    extend(ms.at[1], wet[...].astype(F32), base + 1, AH)
    extend(ms.at[2], kappa[...], base + 2, AH)
    for i in range(tracers):
        extend(fs.at[i], ocean[i // each, i % each], 3 * levels + i, OH)
    for level in range(levels):
        extend(us.at[level], atm[0, level], level, AH)
        extend(vs.at[level], atm[1, level], levels + level, AH)
        extend(hs.at[level], atm[2, level], 2 * levels + level, AH)

    w = ms[1]
    k = ms[2]
    we, ww, ws, wn = east(w), west(w), south(w), north(w)
    for step in range(OCEAN_STEPS):
        for i in range(tracers):
            f = fs[i]
            total = we * (east(f) - f)
            total = total + ww * (west(f) - f)
            total = total + ws * (south(f) - f)
            total = total + wn * (north(f) - f)
            f = f + k * (w * total)
            if step < OCEAN_STEPS - 1:
                fs[i] = f
            else:
                f = f[0:rows, 0:cols]
                ocean_buf[i // each, i % each] = f + SEA_GAIN * sea_flux if i == 0 else f
    copies = [pltpu.make_async_copy(ocean_buf, ocean_out, sems.at[0])]
    copies[0].start()

    d = ms[0]
    chunk = max(1, levels // 4)
    for step in range(ACOUSTIC):
        for level in range(levels):
            u, v, h = us[level], vs[level], hs[level]
            column_speed = speed[level] * d
            hs[level] = h - column_speed * ((east(u) - west(u)) * 0.5 + (south(v) - north(v)) * 0.5)
        for level in range(levels):
            u, v, h = us[level], vs[level], hs[level]
            u = u - (east(h) - west(h)) * 0.5
            v = v - (south(h) - north(h)) * 0.5
            if step < ACOUSTIC - 1:
                us[level], vs[level] = u, v
            else:
                h = h[0:rows, 0:cols]
                atm_buf[0, level] = u[0:rows, 0:cols]
                atm_buf[1, level] = v[0:rows, 0:cols]
                atm_buf[2, level] = h - ATM_GAIN * atm_flux if level == levels - 1 else h
                if (level + 1) % chunk == 0:
                    where = pl.ds(level + 1 - chunk, chunk)
                    copies.append(
                        pltpu.make_async_copy(
                            atm_buf.at[:, where], atm_out.at[:, where], sems.at[len(copies)]
                        )
                    )
                    copies[-1].start()
    for copy in copies:
        copy.wait()


def on_device(
    tile_count,
    atm_state,
    air_temp,
    depth,
    wave_speed,
    ocean_state,
    wet_mask,
    diffusivity,
    xg_atm_cell,
    xg_dest,
    xg_ocean_cell,
    xg_weight,
):
    levels = atm_state.shape[1]
    rows, cols = atm_state.shape[2:]
    tracers = ocean_state.shape[0] * ocean_state.shape[1]
    cells = xg_weight.shape[-1]
    _, lanes = lane_slots(levels, tracers)
    _, _, _, message_rows = row_slots(levels, tracers)
    vmem = pl.BlockSpec(memory_space=pltpu.VMEM)
    hbm = pl.BlockSpec(memory_space=pltpu.HBM)
    smem = pl.BlockSpec(memory_space=pltpu.SMEM)
    params = pltpu.CompilerParams(vmem_limit_bytes=16 * 1024 * 1024)
    whole = pltpu.CompilerParams(vmem_limit_bytes=64 * 1024 * 1024)
    full = rows + 2 * AH

    def shape(*dims):
        return jax.ShapeDtypeStruct(dims, F32)

    fields = (atm_state, ocean_state, depth, wet_mask, diffusivity)
    up, down, left, right = pl.pallas_call(
        pack_kernel,
        out_shape=[shape(message_rows, cols)] * 2 + [shape(rows, lanes)] * 2,
        in_specs=[hbm] * 5,
        out_specs=[vmem] * 4,
        scratch_shapes=[pltpu.VMEM(x.shape, x.dtype) for x in fields] + [pltpu.SemaphoreType.DMA((5,))],
        compiler_params=whole,
        name="pack",
    )(*fields)
    atm_cell = xg_atm_cell.reshape(1, cells)
    dest = xg_dest.reshape(1, cells)
    sea_cell = xg_ocean_cell.reshape(1, cells)
    weight = xg_weight.reshape(1, cells)

    column_axes = ("sub", "comp")
    column_count = lax.axis_size("sub") * lax.axis_size("comp")

    def shift(value, axes, count, by):
        return lax.ppermute(value, axes, [(i, (i + by) % count) for i in range(count)])

    from_right = shift(left, column_axes, column_count, -1)
    from_left = shift(right, column_axes, column_count, 1)
    from_down = shift(up, "tile", tile_count, -1)
    from_up = shift(down, "tile", tile_count, 1)

    corner_rows = 2 * AH * (lanes // cols)
    message, wair = pl.pallas_call(
        send_kernel,
        out_shape=[shape(tile_count, 3 * rows + corner_rows, cols), shape(1, cells)],
        in_specs=[hbm] * 8,
        out_specs=[vmem] * 2,
        scratch_shapes=[pltpu.VMEM((rows, cols), F32)] * 2
        + [pltpu.VMEM((1, cells), jnp.int32)] * 3
        + [pltpu.VMEM((1, cells), F32)]
        + [pltpu.VMEM((rows, lanes), F32)] * 2
        + [pltpu.SemaphoreType.DMA((8,))],
        compiler_params=whole,
        cost_estimate=pl.CostEstimate(flops=0, bytes_accessed=200_000_000, transcendentals=0),
        name="exchange_send",
    )(air_temp, ocean_state, atm_cell, dest, sea_cell, weight, from_left, from_right)
    got = lax.all_to_all(message, "tile", split_axis=0, concat_axis=0, tiled=True)

    slices = row_slices(levels, tracers)
    row_tiles = pl.pallas_call(
        functools.partial(regroup_kernel, slices),
        out_shape=shape(len(slices), 2 * AH, cols),
        in_specs=[vmem] * 2,
        out_specs=vmem,
        compiler_params=params,
        cost_estimate=pl.CostEstimate(flops=0, bytes_accessed=200_000_000, transcendentals=0),
        name="regroup",
    )(from_up, from_down)

    return tuple(
        pl.pallas_call(
            final_kernel,
            out_shape=[shape(*atm_state.shape), shape(*ocean_state.shape)],
            in_specs=[smem] + [vmem] * 14,
            out_specs=[hbm] * 2,
            scratch_shapes=[pltpu.VMEM((levels, full, 2 * cols), F32)] * 3
            + [
                pltpu.VMEM((tracers, full, 2 * cols), F32),
                pltpu.VMEM((3, full, 2 * cols), F32),
                pltpu.VMEM((2 * (lanes // cols), 2 * AH, cols), F32),
                pltpu.VMEM(atm_state.shape, F32),
                pltpu.VMEM(ocean_state.shape, F32),
                pltpu.SemaphoreType.DMA((8,)),
            ],
            compiler_params=params,
            name="steps",
        )(
            wave_speed,
            *fields,
            atm_cell,
            dest,
            sea_cell,
            weight,
            wair,
            row_tiles,
            from_left,
            from_right,
            got,
        )
    )


def solution(mesh):
    grid = P(("member", "tile"), ("sub", "comp"))
    state = P(None, None, ("member", "tile"), ("sub", "comp"))
    cells = P(("member", "tile"), ("sub", "comp"), None)
    return jax.shard_map(
        functools.partial(on_device, mesh.shape["tile"]),
        mesh=mesh,
        in_specs=(
            state,
            grid,
            grid,
            P(),
            state,
            grid,
            grid,
            cells,
            P(("member", "tile"), ("sub", "comp"), None, None),
            cells,
            cells,
        ),
        out_specs=(state, state),
        check_vma=False,
    )
```

```python
import functools

import jax
import jax.numpy as jnp
from jax import lax
from jax.experimental import pallas as pl
from jax.experimental.pallas import tpu as pltpu
from jax.sharding import PartitionSpec as P

ACOUSTIC = 2
OCEAN_STEPS = 2
AH = 2 * ACOUSTIC
OH = OCEAN_STEPS

ATM_GAIN = 0.5
SEA_GAIN = 0.5

F32 = jnp.float32
BF16 = jnp.bfloat16


def lane_slots(levels, tracers):
    slots = [AH * i for i in range(3 * levels)]
    base = AH * 3 * levels
    slots += [base + OH * i for i in range(tracers)]
    base += OH * tracers
    slots += [base + AH * i for i in range(3)]
    total = base + 3 * AH
    return slots, -(-total // 128) * 128


def row_slots(levels, tracers):
    per = 3 * AH - 2
    base = per * levels
    misc = base + OH * tracers
    return per, base, misc, misc + AH + 2 * OH


def pack_kernel(*refs):
    sources, (up, down, left, right), held, sems = refs[:5], refs[5:9], refs[9:14], refs[14]
    atm, ocean, depth, wet, kappa = held
    copies = [
        pltpu.make_async_copy(source, target, sems.at[i])
        for i, (source, target) in enumerate(zip(sources, held))
    ]
    for copy in copies:
        copy.start()
    levels = atm.shape[1]
    rows, cols = atm.shape[2:]
    tracers = ocean.shape[0] * ocean.shape[1]
    each = ocean.shape[1]
    per, obase, mbase, _ = row_slots(levels, tracers)
    slots, _ = lane_slots(levels, tracers)
    for copy in copies:
        copy.wait()
    wetness = wet[...].astype(F32)

    lane = lax.broadcasted_iota(jnp.int32, (rows, cols), 1)
    fields = [(atm, (k, l), AH) for k in range(3) for l in range(levels)]
    fields += [(ocean, (i // each, i % each), OH) for i in range(tracers)]
    fields += [(depth, None, AH), (None, None, AH), (kappa, None, AH)]
    packed = {}
    for (ref, at, width), slot in zip(fields, slots):
        value = wetness if ref is None else (ref[...] if at is None else ref[at[0], at[1]])
        tile, offset = slot // cols, slot % cols
        mask = (lane >= offset) & (lane < offset + width)
        first = pltpu.roll(value, offset, 1) if offset else value
        turn = (offset + width) % cols
        last = pltpu.roll(value, turn, 1) if turn else value
        if tile in packed:
            a, b = packed[tile]
            packed[tile] = (jnp.where(mask, first, a), jnp.where(mask, last, b))
        else:
            packed[tile] = (first, last)
    for tile, (a, b) in packed.items():
        where = slice(tile * cols, (tile + 1) * cols)
        left[:, where] = a
        right[:, where] = b

    for level in range(levels):
        base = per * level
        for at, which, width in ((0, 1, AH), (AH, 0, AH - 1), (2 * AH - 1, 2, AH - 1)):
            up[base + at : base + at + width, :] = atm[which, level, 0:width, :]
            down[base + at : base + at + width, :] = atm[which, level, rows - width : rows, :]
    for i in range(tracers):
        at = obase + OH * i
        up[at : at + OH, :] = ocean[i // each, i % each, 0:OH, :]
        down[at : at + OH, :] = ocean[i // each, i % each, rows - OH : rows, :]
    for at, value, width in (
        (mbase, depth[...], AH),
        (mbase + AH, wetness, OH),
        (mbase + AH + OH, kappa[...], OH),
    ):
        up[at : at + width, :] = value[0:width]
        down[at : at + width, :] = value[rows - width : rows]


def split3(value):
    hi = value.astype(BF16)
    rest = value - hi.astype(F32)
    mid = rest.astype(BF16)
    low = (rest - mid.astype(F32)).astype(BF16)
    return hi, mid, low


def one_hot(index, size):
    shape = (size, index.shape[-1])
    return lax.broadcasted_iota(jnp.int32, shape, 0) == index


def gather_rows(table, hot_rows, hot_cols):
    r = table.shape[0]
    parts = jnp.concatenate(split3(table), axis=0)
    g = jnp.dot(parts, hot_cols, preferred_element_type=F32)
    g = g[0:r] + g[r : 2 * r] + g[2 * r : 3 * r]
    return jnp.sum(jnp.where(hot_rows, g, 0.0), axis=0, keepdims=True)


def scatter_rows(values, hot_rows, hot_cols):
    r = hot_rows.shape[0]
    parts = []
    for value in values:
        for part in split3(value):
            parts.append(jnp.where(hot_rows, part.astype(F32), 0.0).astype(BF16))
    s = lax.dot_general(
        jnp.concatenate(parts, axis=0),
        hot_cols,
        (((1,), (1,)), ((), ())),
        preferred_element_type=F32,
    )
    out = []
    for i in range(len(values)):
        base = 3 * r * i
        out.append(s[base : base + r] + s[base + r : base + 2 * r] + s[base + 2 * r : base + 3 * r])
    return out


def tile_at(shift, tiles):
    return lax.rem(lax.axis_index("tile") + shift % tiles, tiles)


def send_kernel(tiles, *refs):
    sources, (*messages, wair_out) = refs[:8], refs[8:-9]
    held, sems = refs[-9:-1], refs[-1]
    air, surface, atm_cell, dest, sea_cell, weight, from_left, from_right = held
    copies = [
        pltpu.make_async_copy(source.at[0, 0] if i == 1 else source, target, sems.at[i])
        for i, (source, target) in enumerate(zip(sources, held))
    ]
    for copy in copies:
        copy.start()
    for copy in copies:
        copy.wait()
    rows, cols = air.shape
    cell = atm_cell[...]
    hot_atm = jnp.where(one_hot(cell % cols, cols), 1.0, 0.0).astype(BF16)
    airx = gather_rows(air[...], one_hot(cell // cols, rows), hot_atm)
    w = weight[...]
    wair = w * airx
    wair_out[...] = wair
    cell = sea_cell[...]
    hot_sea = jnp.where(one_hot(cell % cols, cols), 1.0, 0.0).astype(BF16)
    row = dest[...] * rows + cell // cols
    strip_tiles = from_left.shape[1] // cols
    for shift in range(tiles):
        target = tile_at(shift, tiles)
        message = messages[shift] if len(messages) > 1 else messages[0].at[target]
        s1, s2 = scatter_rows([wair, w], one_hot(row - target * rows, rows), hot_sea)
        message[0:rows, :] = s1
        message[rows : 2 * rows, :] = s2
        message[2 * rows : 3 * rows, :] = surface[...]
        if shift in (1, tiles - 1):
            near = slice(rows - AH, rows) if shift == 1 else slice(0, AH)
            at = 3 * rows
            for ref in (from_left, from_right):
                for i in range(strip_tiles):
                    message[at : at + AH, :] = ref[near, i * cols : (i + 1) * cols]
                    at += AH


def strips(cols, slot, width, left_part, right_part):
    low_half = lax.broadcasted_iota(jnp.int32, (1, cols), 1) < cols // 2
    offset = slot % cols
    a, b = right_part(slot // cols), left_part(slot // cols)
    if offset:
        a = pltpu.roll(a, cols - offset, 1)
    turn = (cols - width - offset) % cols
    if turn:
        b = pltpu.roll(b, turn, 1)
    return jnp.where(low_half, a, b)


def row_slices(levels, tracers):
    per, obase, mbase, _ = row_slots(levels, tracers)
    out = [(per * level + AH, AH - 1) for level in range(levels)]
    out += [(per * level, AH) for level in range(levels)]
    out += [(per * level + 2 * AH - 1, AH - 1) for level in range(levels)]
    out += [(obase + OH * i, OH) for i in range(tracers)]
    return out + [(mbase, AH), (mbase + AH, OH), (mbase + AH + OH, OH)]


def regroup_kernel(slices, from_up, from_down, tiles):
    for i, (at, width) in enumerate(slices):
        tiles[i, 0:width, :] = from_down[at : at + width, :]
        tiles[i, 2 * AH - width : 2 * AH, :] = from_up[at : at + width, :]


def final_kernel(tiles, *refs):
    speed, atm, ocean, depth, wet, kappa, atm_cell, dest, sea_cell, weight, wair, row_tiles, from_left, from_right = refs[:14]
    messages, (atm_out, ocean_out, us, vs, hs, fs, ms, edge, atm_buf, ocean_buf, sems) = refs[14:-11], refs[-11:]
    levels = atm.shape[1]
    rows, cols = atm.shape[2:]
    tracers = fs.shape[0]
    each = ocean.shape[1]
    slots, lanes = lane_slots(levels, tracers)
    full = rows + 2 * AH

    def message(shift):
        return messages[shift] if len(messages) > 1 else messages[0].at[tile_at(-shift, tiles)]

    surface = ocean[0, 0]
    cell = sea_cell[...]
    hot_sea = jnp.where(one_hot(cell % cols, cols), 1.0, 0.0).astype(BF16)
    row = dest[...] * rows + cell // cols
    s1, s2 = message(0)[0:rows, :], message(0)[rows : 2 * rows, :]
    sstx = jnp.zeros(cell.shape, F32)
    for shift in range(tiles):
        if shift:
            s1 = s1 + message(shift)[0:rows, :]
            s2 = s2 + message(shift)[rows : 2 * rows, :]
        table = message(shift)[2 * rows : 3 * rows, :]
        sstx = sstx + gather_rows(table, one_hot(row - tile_at(-shift, tiles) * rows, rows), hot_sea)
    sea_flux = s1 - surface * s2
    flux = wair[...] - weight[...] * sstx
    cell = atm_cell[...]
    hot_atm = jnp.where(one_hot(cell % cols, cols), 1.0, 0.0).astype(BF16)
    (atm_flux,) = scatter_rows([flux], one_hot(cell // cols, rows), hot_atm)

    half = lanes // cols
    for i in range(2 * half):
        at = 3 * rows + AH * i
        edge[i, 0:AH, :] = message(tiles - 1)[at : at + AH, :]
        edge[i, AH : 2 * AH, :] = message(1)[at : at + AH, :]

    def extend(view, value, field, width):
        slot = slots[field]
        view[0:rows, 0:cols] = value
        view[rows:full, 0:cols] = row_tiles[field]
        view[0:rows, cols : 2 * cols] = strips(
            cols, slot, width, lambda t: from_left[:, t * cols : (t + 1) * cols], lambda t: from_right[:, t * cols : (t + 1) * cols]
        )
        view[rows:full, cols : 2 * cols] = strips(cols, slot, width, lambda t: edge[t], lambda t: edge[half + t])

    def east(f):
        return pltpu.roll(f, 2 * cols - 1, 1)

    def west(f):
        return pltpu.roll(f, 1, 1)

    def south(f):
        return pltpu.roll(f, full - 1, 0)

    def north(f):
        return pltpu.roll(f, 1, 0)

    base = 3 * levels + tracers
    extend(ms.at[0], depth[...], base, AH)
    extend(ms.at[1], wet[...].astype(F32), base + 1, AH)
    extend(ms.at[2], kappa[...], base + 2, AH)
    for i in range(tracers):
        extend(fs.at[i], ocean[i // each, i % each], 3 * levels + i, OH)
    for level in range(levels):
        extend(us.at[level], atm[0, level], level, AH)
        extend(vs.at[level], atm[1, level], levels + level, AH)
        extend(hs.at[level], atm[2, level], 2 * levels + level, AH)

    w = ms[1]
    k = ms[2]
    we, ww, ws, wn = east(w), west(w), south(w), north(w)
    for step in range(OCEAN_STEPS):
        for i in range(tracers):
            f = fs[i]
            total = we * (east(f) - f)
            total = total + ww * (west(f) - f)
            total = total + ws * (south(f) - f)
            total = total + wn * (north(f) - f)
            f = f + k * (w * total)
            if step < OCEAN_STEPS - 1:
                fs[i] = f
            else:
                f = f[0:rows, 0:cols]
                ocean_buf[i // each, i % each] = f + SEA_GAIN * sea_flux if i == 0 else f
    copies = [pltpu.make_async_copy(ocean_buf, ocean_out, sems.at[0])]
    copies[0].start()

    d = ms[0]
    chunk = max(1, levels // 4)
    for step in range(ACOUSTIC):
        for level in range(levels):
            u, v, h = us[level], vs[level], hs[level]
            column_speed = speed[level] * d
            hs[level] = h - column_speed * ((east(u) - west(u)) * 0.5 + (south(v) - north(v)) * 0.5)
        for level in range(levels):
            u, v, h = us[level], vs[level], hs[level]
            u = u - (east(h) - west(h)) * 0.5
            v = v - (south(h) - north(h)) * 0.5
            if step < ACOUSTIC - 1:
                us[level], vs[level] = u, v
            else:
                h = h[0:rows, 0:cols]
                atm_buf[0, level] = u[0:rows, 0:cols]
                atm_buf[1, level] = v[0:rows, 0:cols]
                atm_buf[2, level] = h - ATM_GAIN * atm_flux if level == levels - 1 else h
                if (level + 1) % chunk == 0:
                    where = pl.ds(level + 1 - chunk, chunk)
                    copies.append(
                        pltpu.make_async_copy(
                            atm_buf.at[:, where], atm_out.at[:, where], sems.at[len(copies)]
                        )
                    )
                    copies[-1].start()
    for copy in copies:
        copy.wait()


def on_device(
    tile_count,
    atm_state,
    air_temp,
    depth,
    wave_speed,
    ocean_state,
    wet_mask,
    diffusivity,
    xg_atm_cell,
    xg_dest,
    xg_ocean_cell,
    xg_weight,
):
    levels = atm_state.shape[1]
    rows, cols = atm_state.shape[2:]
    tracers = ocean_state.shape[0] * ocean_state.shape[1]
    cells = xg_weight.shape[-1]
    _, lanes = lane_slots(levels, tracers)
    _, _, _, message_rows = row_slots(levels, tracers)
    vmem = pl.BlockSpec(memory_space=pltpu.VMEM)
    hbm = pl.BlockSpec(memory_space=pltpu.HBM)
    smem = pl.BlockSpec(memory_space=pltpu.SMEM)
    params = pltpu.CompilerParams(vmem_limit_bytes=16 * 1024 * 1024)
    whole = pltpu.CompilerParams(vmem_limit_bytes=64 * 1024 * 1024)
    full = rows + 2 * AH

    def shape(*dims):
        return jax.ShapeDtypeStruct(dims, F32)

    fields = (atm_state, ocean_state, depth, wet_mask, diffusivity)
    up, down, left, right = pl.pallas_call(
        pack_kernel,
        out_shape=[shape(message_rows, cols)] * 2 + [shape(rows, lanes)] * 2,
        in_specs=[hbm] * 5,
        out_specs=[vmem] * 4,
        scratch_shapes=[pltpu.VMEM(x.shape, x.dtype) for x in fields] + [pltpu.SemaphoreType.DMA((5,))],
        compiler_params=whole,
        name="pack",
    )(*fields)
    atm_cell = xg_atm_cell.reshape(1, cells)
    dest = xg_dest.reshape(1, cells)
    sea_cell = xg_ocean_cell.reshape(1, cells)
    weight = xg_weight.reshape(1, cells)

    column_axes = ("sub", "comp")
    column_count = lax.axis_size("sub") * lax.axis_size("comp")

    def shift(value, axes, count, by):
        return lax.ppermute(value, axes, [(i, (i + by) % count) for i in range(count)])

    from_right = shift(left, column_axes, column_count, -1)
    from_left = shift(right, column_axes, column_count, 1)
    from_down = shift(up, "tile", tile_count, -1)
    from_up = shift(down, "tile", tile_count, 1)

    corner_rows = 2 * AH * (lanes // cols)
    by_shift = tile_count <= 4
    if by_shift:
        sums = [shape(3 * rows + (corner_rows if s in (1, tile_count - 1) else 0), cols) for s in range(tile_count)]
    else:
        sums = [shape(tile_count, 3 * rows + corner_rows, cols)]
    *messages, wair = pl.pallas_call(
        functools.partial(send_kernel, tile_count),
        out_shape=sums + [shape(1, cells)],
        in_specs=[hbm] * 8,
        out_specs=[vmem] * (len(sums) + 1),
        scratch_shapes=[pltpu.VMEM((rows, cols), F32)] * 2
        + [pltpu.VMEM((1, cells), jnp.int32)] * 3
        + [pltpu.VMEM((1, cells), F32)]
        + [pltpu.VMEM((rows, lanes), F32)] * 2
        + [pltpu.SemaphoreType.DMA((8,))],
        compiler_params=whole,
        cost_estimate=pl.CostEstimate(flops=0, bytes_accessed=200_000_000, transcendentals=0),
        name="exchange_send",
    )(air_temp, ocean_state, atm_cell, dest, sea_cell, weight, from_left, from_right)
    if by_shift:
        got = messages[:1] + [shift(messages[s], "tile", tile_count, s) for s in range(1, tile_count)]
    else:
        got = [lax.all_to_all(messages[0], "tile", split_axis=0, concat_axis=0, tiled=True)]

    slices = row_slices(levels, tracers)
    row_tiles = pl.pallas_call(
        functools.partial(regroup_kernel, slices),
        out_shape=shape(len(slices), 2 * AH, cols),
        in_specs=[vmem] * 2,
        out_specs=vmem,
        compiler_params=params,
        cost_estimate=pl.CostEstimate(flops=0, bytes_accessed=200_000_000, transcendentals=0),
        name="regroup",
    )(from_up, from_down)

    return tuple(
        pl.pallas_call(
            functools.partial(final_kernel, tile_count),
            out_shape=[shape(*atm_state.shape), shape(*ocean_state.shape)],
            in_specs=[smem] + [vmem] * (13 + len(got)),
            out_specs=[hbm] * 2,
            scratch_shapes=[pltpu.VMEM((levels, full, 2 * cols), F32)] * 3
            + [
                pltpu.VMEM((tracers, full, 2 * cols), F32),
                pltpu.VMEM((3, full, 2 * cols), F32),
                pltpu.VMEM((2 * (lanes // cols), 2 * AH, cols), F32),
                pltpu.VMEM(atm_state.shape, F32),
                pltpu.VMEM(ocean_state.shape, F32),
                pltpu.SemaphoreType.DMA((8,)),
            ],
            compiler_params=params,
            name="steps",
        )(
            wave_speed,
            *fields,
            atm_cell,
            dest,
            sea_cell,
            weight,
            wair,
            row_tiles,
            from_left,
            from_right,
            *got,
        )
    )


def solution(mesh):
    grid = P(("member", "tile"), ("sub", "comp"))
    state = P(None, None, ("member", "tile"), ("sub", "comp"))
    cells = P(("member", "tile"), ("sub", "comp"), None)
    return jax.shard_map(
        functools.partial(on_device, mesh.shape["tile"]),
        mesh=mesh,
        in_specs=(
            state,
            grid,
            grid,
            P(),
            state,
            grid,
            grid,
            cells,
            P(("member", "tile"), ("sub", "comp"), None, None),
            cells,
            cells,
        ),
        out_specs=(state, state),
        check_vma=False,
    )
```

```python
import functools

import jax
import jax.numpy as jnp
from jax import lax
from jax.experimental import pallas as pl
from jax.experimental.pallas import tpu as pltpu
from jax.sharding import PartitionSpec as P

ACOUSTIC = 2
OCEAN_STEPS = 2
AH = 2 * ACOUSTIC
OH = OCEAN_STEPS

ATM_GAIN = 0.5
SEA_GAIN = 0.5

F32 = jnp.float32
BF16 = jnp.bfloat16


def lane_slots(levels, tracers):
    slots = [AH * i for i in range(3 * levels)]
    base = AH * 3 * levels
    slots += [base + OH * i for i in range(tracers)]
    base += OH * tracers
    slots += [base + AH * i for i in range(3)]
    total = base + 3 * AH
    return slots, -(-total // 128) * 128


def row_slots(levels, tracers):
    per = 3 * AH - 2
    base = per * levels
    misc = base + OH * tracers
    return per, base, misc, misc + AH + 2 * OH


def pack_kernel(*refs):
    sources, (up, down, left, right), held, sems = refs[:5], refs[5:9], refs[9:14], refs[14]
    atm, ocean, depth, wet, kappa = held
    copies = [
        pltpu.make_async_copy(source, target, sems.at[i])
        for i, (source, target) in enumerate(zip(sources, held))
    ]
    for copy in copies:
        copy.start()
    levels = atm.shape[1]
    rows, cols = atm.shape[2:]
    tracers = ocean.shape[0] * ocean.shape[1]
    each = ocean.shape[1]
    per, obase, mbase, _ = row_slots(levels, tracers)
    slots, _ = lane_slots(levels, tracers)
    for copy in copies:
        copy.wait()
    wetness = wet[...].astype(F32)

    lane = lax.broadcasted_iota(jnp.int32, (rows, cols), 1)
    fields = [(atm, (k, l), AH) for k in range(3) for l in range(levels)]
    fields += [(ocean, (i // each, i % each), OH) for i in range(tracers)]
    fields += [(depth, None, AH), (None, None, AH), (kappa, None, AH)]
    packed = {}
    for (ref, at, width), slot in zip(fields, slots):
        value = wetness if ref is None else (ref[...] if at is None else ref[at[0], at[1]])
        tile, offset = slot // cols, slot % cols
        mask = (lane >= offset) & (lane < offset + width)
        first = pltpu.roll(value, offset, 1) if offset else value
        turn = (offset + width) % cols
        last = pltpu.roll(value, turn, 1) if turn else value
        if tile in packed:
            a, b = packed[tile]
            packed[tile] = (jnp.where(mask, first, a), jnp.where(mask, last, b))
        else:
            packed[tile] = (first, last)
    for tile, (a, b) in packed.items():
        where = slice(tile * cols, (tile + 1) * cols)
        left[:, where] = a
        right[:, where] = b

    for level in range(levels):
        base = per * level
        for at, which, width in ((0, 1, AH), (AH, 0, AH - 1), (2 * AH - 1, 2, AH - 1)):
            up[base + at : base + at + width, :] = atm[which, level, 0:width, :]
            down[base + at : base + at + width, :] = atm[which, level, rows - width : rows, :]
    for i in range(tracers):
        at = obase + OH * i
        up[at : at + OH, :] = ocean[i // each, i % each, 0:OH, :]
        down[at : at + OH, :] = ocean[i // each, i % each, rows - OH : rows, :]
    for at, value, width in (
        (mbase, depth[...], AH),
        (mbase + AH, wetness, OH),
        (mbase + AH + OH, kappa[...], OH),
    ):
        up[at : at + width, :] = value[0:width]
        down[at : at + width, :] = value[rows - width : rows]


def split3(value):
    hi = value.astype(BF16)
    rest = value - hi.astype(F32)
    mid = rest.astype(BF16)
    low = (rest - mid.astype(F32)).astype(BF16)
    return hi, mid, low


def one_hot(index, size):
    shape = (size, index.shape[-1])
    return lax.broadcasted_iota(jnp.int32, shape, 0) == index


def gather_rows(table, hot_rows, hot_cols):
    r = table.shape[0]
    parts = jnp.concatenate(split3(table), axis=0)
    g = jnp.dot(parts, hot_cols, preferred_element_type=F32)
    g = g[0:r] + g[r : 2 * r] + g[2 * r : 3 * r]
    return jnp.sum(jnp.where(hot_rows, g, 0.0), axis=0, keepdims=True)


def scatter_rows(values, hot_rows, hot_cols):
    r = hot_rows.shape[0]
    parts = []
    for value in values:
        for part in split3(value):
            parts.append(jnp.where(hot_rows, part.astype(F32), 0.0).astype(BF16))
    s = lax.dot_general(
        jnp.concatenate(parts, axis=0),
        hot_cols,
        (((1,), (1,)), ((), ())),
        preferred_element_type=F32,
    )
    out = []
    for i in range(len(values)):
        base = 3 * r * i
        out.append(s[base : base + r] + s[base + r : base + 2 * r] + s[base + 2 * r : base + 3 * r])
    return out


def tile_at(shift, tiles):
    return lax.rem(lax.axis_index("tile") + shift % tiles, tiles)


def send_kernel(tiles, *refs):
    sources, (*messages, wair_out) = refs[:6], refs[6:-7]
    held, sems = refs[-7:-1], refs[-1]
    air, surface, atm_cell, dest, sea_cell, weight = held
    copies = [
        pltpu.make_async_copy(source.at[0, 0] if i == 1 else source, target, sems.at[i])
        for i, (source, target) in enumerate(zip(sources, held))
    ]
    for copy in copies:
        copy.start()
    for copy in copies:
        copy.wait()
    rows, cols = air.shape
    cell = atm_cell[...]
    hot_atm = jnp.where(one_hot(cell % cols, cols), 1.0, 0.0).astype(BF16)
    airx = gather_rows(air[...], one_hot(cell // cols, rows), hot_atm)
    w = weight[...]
    wair = w * airx
    wair_out[...] = wair
    cell = sea_cell[...]
    hot_sea = jnp.where(one_hot(cell % cols, cols), 1.0, 0.0).astype(BF16)
    row = dest[...] * rows + cell // cols
    for shift in range(tiles):
        target = tile_at(shift, tiles)
        message = messages[shift] if len(messages) > 1 else messages[0].at[target]
        s1, s2 = scatter_rows([wair, w], one_hot(row - target * rows, rows), hot_sea)
        message[0:rows, :] = s1
        message[rows : 2 * rows, :] = s2
        message[2 * rows : 3 * rows, :] = surface[...]


def strips(cols, slot, width, left_part, right_part):
    low_half = lax.broadcasted_iota(jnp.int32, (1, cols), 1) < cols // 2
    offset = slot % cols
    a, b = right_part(slot // cols), left_part(slot // cols)
    if offset:
        a = pltpu.roll(a, cols - offset, 1)
    turn = (cols - width - offset) % cols
    if turn:
        b = pltpu.roll(b, turn, 1)
    return jnp.where(low_half, a, b)


def row_slices(levels, tracers):
    per, obase, mbase, _ = row_slots(levels, tracers)
    out = [(per * level + AH, AH - 1) for level in range(levels)]
    out += [(per * level, AH) for level in range(levels)]
    out += [(per * level + 2 * AH - 1, AH - 1) for level in range(levels)]
    out += [(obase + OH * i, OH) for i in range(tracers)]
    return out + [(mbase, AH), (mbase + AH, OH), (mbase + AH + OH, OH)]


def final_kernel(tiles, parts, *refs):
    speed_in, atm_in, ocean_in, depth_in, kappa_in = refs[:5]
    sources, rest = refs[5 : 15 + parts], refs[15 + parts :]
    atm_out, ocean_out, speed, us, vs, hs, fs, ms = rest[:8]
    held, (edge, atm_buf, ocean_buf, sems) = rest[8 : 18 + parts], rest[18 + parts :]
    wet, atm_cell, dest, sea_cell, weight, wair, from_up, from_down, from_left, from_right = held[:10]
    messages = held[10:]
    levels = us.shape[0]
    each = ocean_out.shape[1]
    tracers = ocean_out.shape[0] * each
    rows, cols = atm_out.shape[2:]
    slots, lanes = lane_slots(levels, tracers)
    slices = row_slices(levels, tracers)
    full = rows + 2 * AH
    block = (slice(None), slice(0, rows), slice(0, cols))
    pairs = list(zip(sources, held)) + [(speed_in, speed)]
    pairs += [(atm_in.at[i], ref.at[block]) for i, ref in enumerate((us, vs, hs))]
    pairs += [(ocean_in.at[i], fs.at[(i, *block)]) for i in range(ocean_out.shape[0])]
    pairs += [(ref, ms.at[(i, *block[1:])]) for i, ref in ((0, depth_in), (2, kappa_in))]
    copies = [pltpu.make_async_copy(source, target, sems.at[i]) for i, (source, target) in enumerate(pairs)]
    for copy in copies:
        copy.start()
    for copy in copies:
        copy.wait()

    def message(shift):
        return messages[shift] if len(messages) > 1 else messages[0].at[tile_at(-shift, tiles)]

    surface = fs[0, 0, 0:rows, 0:cols]
    cell = sea_cell[...]
    hot_sea = jnp.where(one_hot(cell % cols, cols), 1.0, 0.0).astype(BF16)
    row = dest[...] * rows + cell // cols
    s1, s2 = message(0)[0:rows, :], message(0)[rows : 2 * rows, :]
    sstx = jnp.zeros(cell.shape, F32)
    for shift in range(tiles):
        if shift:
            s1 = s1 + message(shift)[0:rows, :]
            s2 = s2 + message(shift)[rows : 2 * rows, :]
        table = message(shift)[2 * rows : 3 * rows, :]
        sstx = sstx + gather_rows(table, one_hot(row - tile_at(-shift, tiles) * rows, rows), hot_sea)
    sea_flux = s1 - surface * s2
    flux = wair[...] - weight[...] * sstx
    cell = atm_cell[...]
    hot_atm = jnp.where(one_hot(cell % cols, cols), 1.0, 0.0).astype(BF16)
    (atm_flux,) = scatter_rows([flux], one_hot(cell // cols, rows), hot_atm)

    half = lanes // cols
    for i in range(2 * half):
        at = 3 * rows + AH * i
        edge[i, 0:AH, :] = message(tiles - 1)[at : at + AH, :]
        edge[i, AH : 2 * AH, :] = message(1)[at : at + AH, :]

    def extend(view, field, width):
        at, high = slices[field]
        slot = slots[field]
        view[rows : rows + high, 0:cols] = from_down[at : at + high, :]
        view[full - high : full, 0:cols] = from_up[at : at + high, :]
        view[0:rows, cols : 2 * cols] = strips(
            cols,
            slot,
            width,
            lambda t: from_left[:, t * cols : (t + 1) * cols],
            lambda t: from_right[:, t * cols : (t + 1) * cols],
        )
        view[rows:full, cols : 2 * cols] = strips(cols, slot, width, lambda t: edge[t], lambda t: edge[half + t])

    def east(f):
        return pltpu.roll(f, 2 * cols - 1, 1)

    def west(f):
        return pltpu.roll(f, 1, 1)

    def south(f):
        return pltpu.roll(f, full - 1, 0)

    def north(f):
        return pltpu.roll(f, 1, 0)

    base = 3 * levels + tracers
    ms[1, 0:rows, 0:cols] = wet[...].astype(F32)
    for i in range(3):
        extend(ms.at[i], base + i, AH)
    for i in range(tracers):
        extend(fs.at[i // each, i % each], 3 * levels + i, OH)
    for level in range(levels):
        extend(us.at[level], level, AH)
        extend(vs.at[level], levels + level, AH)
        extend(hs.at[level], 2 * levels + level, AH)

    w = ms[1]
    k = ms[2]
    we, ww, ws, wn = east(w), west(w), south(w), north(w)
    for step in range(OCEAN_STEPS):
        for i in range(tracers):
            f = fs[i // each, i % each]
            total = we * (east(f) - f)
            total = total + ww * (west(f) - f)
            total = total + ws * (south(f) - f)
            total = total + wn * (north(f) - f)
            f = f + k * (w * total)
            if step < OCEAN_STEPS - 1:
                fs[i // each, i % each] = f
            else:
                f = f[0:rows, 0:cols]
                ocean_buf[i // each, i % each] = f + SEA_GAIN * sea_flux if i == 0 else f
    used = len(copies)
    copies = [pltpu.make_async_copy(ocean_buf, ocean_out, sems.at[used])]
    copies[0].start()

    d = ms[0]
    chunk = max(1, levels // 4)
    for step in range(ACOUSTIC):
        for level in range(levels):
            u, v, h = us[level], vs[level], hs[level]
            column_speed = speed[level] * d
            hs[level] = h - column_speed * ((east(u) - west(u)) * 0.5 + (south(v) - north(v)) * 0.5)
        for level in range(levels):
            u, v, h = us[level], vs[level], hs[level]
            u = u - (east(h) - west(h)) * 0.5
            v = v - (south(h) - north(h)) * 0.5
            if step < ACOUSTIC - 1:
                us[level], vs[level] = u, v
            else:
                h = h[0:rows, 0:cols]
                atm_buf[0, level] = u[0:rows, 0:cols]
                atm_buf[1, level] = v[0:rows, 0:cols]
                atm_buf[2, level] = h - ATM_GAIN * atm_flux if level == levels - 1 else h
                if (level + 1) % chunk == 0:
                    where = pl.ds(level + 1 - chunk, chunk)
                    copies.append(
                        pltpu.make_async_copy(
                            atm_buf.at[:, where], atm_out.at[:, where], sems.at[used + len(copies)]
                        )
                    )
                    copies[-1].start()
    for copy in copies:
        copy.wait()


def on_device(
    tile_count,
    atm_state,
    air_temp,
    depth,
    wave_speed,
    ocean_state,
    wet_mask,
    diffusivity,
    xg_atm_cell,
    xg_dest,
    xg_ocean_cell,
    xg_weight,
):
    levels = atm_state.shape[1]
    rows, cols = atm_state.shape[2:]
    tracers = ocean_state.shape[0] * ocean_state.shape[1]
    cells = xg_weight.shape[-1]
    _, lanes = lane_slots(levels, tracers)
    _, _, _, message_rows = row_slots(levels, tracers)
    vmem = pl.BlockSpec(memory_space=pltpu.VMEM)
    hbm = pl.BlockSpec(memory_space=pltpu.HBM)
    whole = pltpu.CompilerParams(vmem_limit_bytes=64 * 1024 * 1024)
    full = rows + 2 * AH

    def shape(*dims):
        return jax.ShapeDtypeStruct(dims, F32)

    fields = (atm_state, ocean_state, depth, wet_mask, diffusivity)
    up, down, left, right = pl.pallas_call(
        pack_kernel,
        out_shape=[shape(message_rows, cols)] * 2 + [shape(rows, lanes)] * 2,
        in_specs=[hbm] * 5,
        out_specs=[vmem] * 4,
        scratch_shapes=[pltpu.VMEM(x.shape, x.dtype) for x in fields] + [pltpu.SemaphoreType.DMA((5,))],
        compiler_params=whole,
        name="pack",
    )(*fields)
    atm_cell = xg_atm_cell.reshape(1, cells)
    dest = xg_dest.reshape(1, cells)
    sea_cell = xg_ocean_cell.reshape(1, cells)
    weight = xg_weight.reshape(1, cells)

    column_axes = ("sub", "comp")
    column_count = lax.axis_size("sub") * lax.axis_size("comp")

    def shift(value, axes, count, by):
        return lax.ppermute(value, axes, [(i, (i + by) % count) for i in range(count)])

    from_right = shift(left, column_axes, column_count, -1)
    from_left = shift(right, column_axes, column_count, 1)
    from_down = shift(up, "tile", tile_count, -1)
    from_up = shift(down, "tile", tile_count, 1)

    by_shift = tile_count <= 4
    sums = [shape(3 * rows, cols)] * tile_count if by_shift else [shape(tile_count, 3 * rows, cols)]
    *messages, wair = pl.pallas_call(
        functools.partial(send_kernel, tile_count),
        out_shape=sums + [shape(1, cells)],
        in_specs=[hbm] * 6,
        out_specs=[vmem] * (len(sums) + 1),
        scratch_shapes=[pltpu.VMEM((rows, cols), F32)] * 2
        + [pltpu.VMEM((1, cells), jnp.int32)] * 3
        + [pltpu.VMEM((1, cells), F32), pltpu.SemaphoreType.DMA((6,))],
        compiler_params=whole,
        cost_estimate=pl.CostEstimate(flops=0, bytes_accessed=200_000_000, transcendentals=0),
        name="exchange_send",
    )(air_temp, ocean_state, atm_cell, dest, sea_cell, weight)
    near = {}
    for s, low in ((1, rows - AH), (tile_count - 1, 0)):
        near[s] = [
            ref[low : low + AH, i * cols : (i + 1) * cols]
            for ref in (from_left, from_right)
            for i in range(lanes // cols)
        ]
    if by_shift:
        got = messages[:1]
        for s in range(1, tile_count):
            joined = jnp.concatenate([messages[s]] + near[s]) if s in near else messages[s]
            got.append(shift(joined, "tile", tile_count, s))
    else:
        corners = jnp.zeros((tile_count, 2 * AH * (lanes // cols), cols), F32)
        for s in near:
            corners = corners.at[(lax.axis_index("tile") + s) % tile_count].set(jnp.concatenate(near[s]))
        joined = jnp.concatenate([messages[0], corners], axis=1)
        got = [lax.all_to_all(joined, "tile", split_axis=0, concat_axis=0, tiled=True)]

    operands = (wave_speed, atm_state, ocean_state, depth, diffusivity)
    operands += (wet_mask, atm_cell, dest, sea_cell, weight, wair, from_up, from_down, from_left, from_right, *got)
    return tuple(
        pl.pallas_call(
            functools.partial(final_kernel, tile_count, len(got)),
            out_shape=[shape(*atm_state.shape), shape(*ocean_state.shape)],
            in_specs=[hbm] * len(operands),
            out_specs=[hbm] * 2,
            scratch_shapes=[pltpu.SMEM(wave_speed.shape, F32)]
            + [pltpu.VMEM((levels, full, 2 * cols), F32)] * 3
            + [
                pltpu.VMEM((*ocean_state.shape[:2], full, 2 * cols), F32),
                pltpu.VMEM((3, full, 2 * cols), F32),
            ]
            + [pltpu.VMEM(x.shape, x.dtype) for x in operands[5:]]
            + [
                pltpu.VMEM((2 * (lanes // cols), 2 * AH, cols), F32),
                pltpu.VMEM(atm_state.shape, F32),
                pltpu.VMEM(ocean_state.shape, F32),
                pltpu.SemaphoreType.DMA((len(operands) + 10,)),
            ],
            compiler_params=whole,
            name="steps",
        )(*operands)
    )


def solution(mesh):
    grid = P(("member", "tile"), ("sub", "comp"))
    state = P(None, None, ("member", "tile"), ("sub", "comp"))
    cells = P(("member", "tile"), ("sub", "comp"), None)
    return jax.shard_map(
        functools.partial(on_device, mesh.shape["tile"]),
        mesh=mesh,
        in_specs=(
            state,
            grid,
            grid,
            P(),
            state,
            grid,
            grid,
            cells,
            P(("member", "tile"), ("sub", "comp"), None, None),
            cells,
            cells,
        ),
        out_specs=(state, state),
        check_vma=False,
    )
```

```python
import functools

import jax
import jax.numpy as jnp
from jax import lax
from jax.experimental import pallas as pl
from jax.experimental.pallas import tpu as pltpu
from jax.sharding import PartitionSpec as P

ACOUSTIC = 2
OCEAN_STEPS = 2
AH = 2 * ACOUSTIC
OH = OCEAN_STEPS

ATM_GAIN = 0.5
SEA_GAIN = 0.5

F32 = jnp.float32
BF16 = jnp.bfloat16


def lane_slots(levels, tracers):
    slots = [AH * i for i in range(3 * levels)]
    base = AH * 3 * levels
    slots += [base + OH * i for i in range(tracers)]
    base += OH * tracers
    slots += [base + AH * i for i in range(3)]
    total = base + 3 * AH
    return slots, -(-total // 128) * 128


def row_slots(levels, tracers):
    per = 3 * AH - 2
    base = per * levels
    misc = base + OH * tracers
    return per, base, misc, misc + AH + 2 * OH


def pack_kernel(*refs):
    sources, (up, down, left, right), held, sems = refs[:5], refs[5:9], refs[9:14], refs[14]
    atm, ocean, depth, wet, kappa = held
    copies = [
        pltpu.make_async_copy(source, target, sems.at[i])
        for i, (source, target) in enumerate(zip(sources, held))
    ]
    for copy in copies:
        copy.start()
    levels = atm.shape[1]
    rows, cols = atm.shape[2:]
    tracers = ocean.shape[0] * ocean.shape[1]
    each = ocean.shape[1]
    per, obase, mbase, _ = row_slots(levels, tracers)
    slots, _ = lane_slots(levels, tracers)
    for copy in copies:
        copy.wait()
    wetness = wet[...].astype(F32)

    lane = lax.broadcasted_iota(jnp.int32, (rows, cols), 1)
    fields = [(atm, (k, l), AH) for k in range(3) for l in range(levels)]
    fields += [(ocean, (i // each, i % each), OH) for i in range(tracers)]
    fields += [(depth, None, AH), (None, None, AH), (kappa, None, AH)]
    packed = {}
    for (ref, at, width), slot in zip(fields, slots):
        value = wetness if ref is None else (ref[...] if at is None else ref[at[0], at[1]])
        tile, offset = slot // cols, slot % cols
        mask = (lane >= offset) & (lane < offset + width)
        first = pltpu.roll(value, offset, 1) if offset else value
        turn = (offset + width) % cols
        last = pltpu.roll(value, turn, 1) if turn else value
        if tile in packed:
            a, b = packed[tile]
            packed[tile] = (jnp.where(mask, first, a), jnp.where(mask, last, b))
        else:
            packed[tile] = (first, last)
    for tile, (a, b) in packed.items():
        where = slice(tile * cols, (tile + 1) * cols)
        left[:, where] = a
        right[:, where] = b

    for level in range(levels):
        base = per * level
        for at, which, width in ((0, 1, AH), (AH, 0, AH - 1), (2 * AH - 1, 2, AH - 1)):
            up[base + at : base + at + width, :] = atm[which, level, 0:width, :]
            down[base + at : base + at + width, :] = atm[which, level, rows - width : rows, :]
    for i in range(tracers):
        at = obase + OH * i
        up[at : at + OH, :] = ocean[i // each, i % each, 0:OH, :]
        down[at : at + OH, :] = ocean[i // each, i % each, rows - OH : rows, :]
    for at, value, width in (
        (mbase, depth[...], AH),
        (mbase + AH, wetness, OH),
        (mbase + AH + OH, kappa[...], OH),
    ):
        up[at : at + width, :] = value[0:width]
        down[at : at + width, :] = value[rows - width : rows]


def split3(value):
    hi = value.astype(BF16)
    rest = value - hi.astype(F32)
    mid = rest.astype(BF16)
    low = (rest - mid.astype(F32)).astype(BF16)
    return hi, mid, low


def one_hot(index, size):
    shape = (size, index.shape[-1])
    return lax.broadcasted_iota(jnp.int32, shape, 0) == index


def gather_rows(table, hot_rows, hot_cols):
    r = table.shape[0]
    parts = jnp.concatenate(split3(table), axis=0)
    g = jnp.dot(parts, hot_cols, preferred_element_type=F32)
    g = g[0:r] + g[r : 2 * r] + g[2 * r : 3 * r]
    return jnp.sum(jnp.where(hot_rows, g, 0.0), axis=0, keepdims=True)


def scatter_rows(values, hot_rows, hot_cols):
    r = hot_rows.shape[0]
    parts = []
    for value in values:
        for part in split3(value):
            parts.append(jnp.where(hot_rows, part.astype(F32), 0.0).astype(BF16))
    s = lax.dot_general(
        jnp.concatenate(parts, axis=0),
        hot_cols,
        (((1,), (1,)), ((), ())),
        preferred_element_type=F32,
    )
    out = []
    for i in range(len(values)):
        base = 3 * r * i
        out.append(s[base : base + r] + s[base + r : base + 2 * r] + s[base + 2 * r : base + 3 * r])
    return out


def send_kernel(*refs):
    sources, (sums, wair_out), held, sems = refs[:5], refs[5:7], refs[7:12], refs[12]
    air, atm_cell, dest, sea_cell, weight = held
    copies = [
        pltpu.make_async_copy(source, target, sems.at[i])
        for i, (source, target) in enumerate(zip(sources, held))
    ]
    for copy in copies:
        copy.start()
    for copy in copies:
        copy.wait()
    rows, cols = air.shape
    cell = atm_cell[...]
    hot_atm = jnp.where(one_hot(cell % cols, cols), 1.0, 0.0).astype(BF16)
    airx = gather_rows(air[...], one_hot(cell // cols, rows), hot_atm)
    w = weight[...]
    wair = w * airx
    wair_out[...] = wair
    cell = sea_cell[...]
    hot_sea = jnp.where(one_hot(cell % cols, cols), 1.0, 0.0).astype(BF16)
    row = dest[...] * rows + cell // cols
    for tile in range(sums.shape[0]):
        s1, s2 = scatter_rows([wair, w], one_hot(row - tile * rows, rows), hot_sea)
        sums[tile, 0:rows, :] = s1
        sums[tile, rows : 2 * rows, :] = s2


def strips(cols, slot, width, left_part, right_part):
    low_half = lax.broadcasted_iota(jnp.int32, (1, cols), 1) < cols // 2
    offset = slot % cols
    a, b = right_part(slot // cols), left_part(slot // cols)
    if offset:
        a = pltpu.roll(a, cols - offset, 1)
    turn = (cols - width - offset) % cols
    if turn:
        b = pltpu.roll(b, turn, 1)
    return jnp.where(low_half, a, b)


def row_slices(levels, tracers):
    per, obase, mbase, _ = row_slots(levels, tracers)
    out = [(per * level + AH, AH - 1) for level in range(levels)]
    out += [(per * level, AH) for level in range(levels)]
    out += [(per * level + 2 * AH - 1, AH - 1) for level in range(levels)]
    out += [(obase + OH * i, OH) for i in range(tracers)]
    return out + [(mbase, AH), (mbase + AH, OH), (mbase + AH + OH, OH)]


def final_kernel(*refs):
    speed_in, atm_in, ocean_in, depth_in, kappa_in, left_all, right_all = refs[:7]
    sources, rest = refs[7:19], refs[19:]
    atm_out, ocean_out, speed, us, vs, hs, fs, ms = rest[:8]
    held, (far, edge, atm_buf, ocean_buf, sems) = rest[8:20], rest[20:]
    wet, atm_cell, dest, sea_cell, weight, wair, sst, sums, from_up, from_down, from_left, from_right = held
    tiles = sst.shape[0]
    me = lax.axis_index("tile")
    above, below = lax.rem(me + tiles - 1, tiles), lax.rem(me + 1, tiles)
    levels = us.shape[0]
    each = ocean_out.shape[1]
    tracers = ocean_out.shape[0] * each
    rows, cols = atm_out.shape[2:]
    slots, lanes = lane_slots(levels, tracers)
    slices = row_slices(levels, tracers)
    full = rows + 2 * AH
    block = (slice(None), slice(0, rows), slice(0, cols))
    pairs = list(zip(sources, held)) + [(speed_in, speed)]
    pairs += [(atm_in.at[i], ref.at[block]) for i, ref in enumerate((us, vs, hs))]
    pairs += [(ocean_in.at[i], fs.at[(i, *block)]) for i in range(ocean_out.shape[0])]
    pairs += [(ref, ms.at[(i, *block[1:])]) for i, ref in ((0, depth_in), (2, kappa_in))]
    part = far.shape[2]
    for i, ref in enumerate((left_all, right_all)):
        pairs += [(ref.at[below, 0:part], far.at[i, 0]), (ref.at[above, rows - part : rows], far.at[i, 1])]
    copies = [pltpu.make_async_copy(source, target, sems.at[i]) for i, (source, target) in enumerate(pairs)]
    for copy in copies:
        copy.start()
    for copy in copies:
        copy.wait()

    surface = fs[0, 0, 0:rows, 0:cols]
    cell = sea_cell[...]
    hot_sea = jnp.where(one_hot(cell % cols, cols), 1.0, 0.0).astype(BF16)
    row = dest[...] * rows + cell // cols
    sstx = jnp.zeros(cell.shape, F32)
    for tile in range(tiles):
        sstx = sstx + gather_rows(sst[tile], one_hot(row - tile * rows, rows), hot_sea)
    sea_flux = sums[0:rows, :] - surface * sums[rows : 2 * rows, :]
    flux = wair[...] - weight[...] * sstx
    cell = atm_cell[...]
    hot_atm = jnp.where(one_hot(cell % cols, cols), 1.0, 0.0).astype(BF16)
    (atm_flux,) = scatter_rows([flux], one_hot(cell // cols, rows), hot_atm)

    half = lanes // cols
    for i in range(2 * half):
        where = slice(i % half * cols, (i % half + 1) * cols)
        edge[i, 0:AH, :] = far[i // half, 0, 0:AH, where]
        edge[i, AH : 2 * AH, :] = far[i // half, 1, part - AH : part, where]

    def extend(view, field, width):
        at, high = slices[field]
        slot = slots[field]
        view[rows : rows + high, 0:cols] = from_down[at : at + high, :]
        view[full - high : full, 0:cols] = from_up[at : at + high, :]
        view[0:rows, cols : 2 * cols] = strips(
            cols,
            slot,
            width,
            lambda t: from_left[:, t * cols : (t + 1) * cols],
            lambda t: from_right[:, t * cols : (t + 1) * cols],
        )
        view[rows:full, cols : 2 * cols] = strips(cols, slot, width, lambda t: edge[t], lambda t: edge[half + t])

    def east(f):
        return pltpu.roll(f, 2 * cols - 1, 1)

    def west(f):
        return pltpu.roll(f, 1, 1)

    def south(f):
        return pltpu.roll(f, full - 1, 0)

    def north(f):
        return pltpu.roll(f, 1, 0)

    base = 3 * levels + tracers
    ms[1, 0:rows, 0:cols] = wet[...].astype(F32)
    for i in range(3):
        extend(ms.at[i], base + i, AH)
    for i in range(tracers):
        extend(fs.at[i // each, i % each], 3 * levels + i, OH)
    for level in range(levels):
        extend(us.at[level], level, AH)
        extend(vs.at[level], levels + level, AH)
        extend(hs.at[level], 2 * levels + level, AH)

    w = ms[1]
    k = ms[2]
    we, ww, ws, wn = east(w), west(w), south(w), north(w)
    for step in range(OCEAN_STEPS):
        for i in range(tracers):
            f = fs[i // each, i % each]
            total = we * (east(f) - f)
            total = total + ww * (west(f) - f)
            total = total + ws * (south(f) - f)
            total = total + wn * (north(f) - f)
            f = f + k * (w * total)
            if step < OCEAN_STEPS - 1:
                fs[i // each, i % each] = f
            else:
                f = f[0:rows, 0:cols]
                ocean_buf[i // each, i % each] = f + SEA_GAIN * sea_flux if i == 0 else f
    used = len(copies)
    copies = [pltpu.make_async_copy(ocean_buf, ocean_out, sems.at[used])]
    copies[0].start()

    d = ms[0]
    chunk = max(1, levels // 4)
    for step in range(ACOUSTIC):
        for level in range(levels):
            u, v, h = us[level], vs[level], hs[level]
            column_speed = speed[level] * d
            hs[level] = h - column_speed * ((east(u) - west(u)) * 0.5 + (south(v) - north(v)) * 0.5)
        for level in range(levels):
            u, v, h = us[level], vs[level], hs[level]
            u = u - (east(h) - west(h)) * 0.5
            v = v - (south(h) - north(h)) * 0.5
            if step < ACOUSTIC - 1:
                us[level], vs[level] = u, v
            else:
                h = h[0:rows, 0:cols]
                atm_buf[0, level] = u[0:rows, 0:cols]
                atm_buf[1, level] = v[0:rows, 0:cols]
                atm_buf[2, level] = h - ATM_GAIN * atm_flux if level == levels - 1 else h
                if (level + 1) % chunk == 0:
                    where = pl.ds(level + 1 - chunk, chunk)
                    copies.append(
                        pltpu.make_async_copy(
                            atm_buf.at[:, where], atm_out.at[:, where], sems.at[used + len(copies)]
                        )
                    )
                    copies[-1].start()
    for copy in copies:
        copy.wait()


def on_device(
    tile_count,
    atm_state,
    air_temp,
    depth,
    wave_speed,
    ocean_state,
    wet_mask,
    diffusivity,
    xg_atm_cell,
    xg_dest,
    xg_ocean_cell,
    xg_weight,
):
    levels = atm_state.shape[1]
    rows, cols = atm_state.shape[2:]
    tracers = ocean_state.shape[0] * ocean_state.shape[1]
    cells = xg_weight.shape[-1]
    _, lanes = lane_slots(levels, tracers)
    _, _, _, message_rows = row_slots(levels, tracers)
    vmem = pl.BlockSpec(memory_space=pltpu.VMEM)
    hbm = pl.BlockSpec(memory_space=pltpu.HBM)
    whole = pltpu.CompilerParams(vmem_limit_bytes=64 * 1024 * 1024)
    full = rows + 2 * AH

    def shape(*dims):
        return jax.ShapeDtypeStruct(dims, F32)

    fields = (atm_state, ocean_state, depth, wet_mask, diffusivity)
    up, down, left, right = pl.pallas_call(
        pack_kernel,
        out_shape=[shape(message_rows, cols)] * 2 + [shape(rows, lanes)] * 2,
        in_specs=[hbm] * 5,
        out_specs=[vmem] * 4,
        scratch_shapes=[pltpu.VMEM(x.shape, x.dtype) for x in fields] + [pltpu.SemaphoreType.DMA((5,))],
        compiler_params=whole,
        name="pack",
    )(*fields)
    atm_cell = xg_atm_cell.reshape(1, cells)
    dest = xg_dest.reshape(1, cells)
    sea_cell = xg_ocean_cell.reshape(1, cells)
    weight = xg_weight.reshape(1, cells)

    column_axes = ("sub", "comp")
    column_count = lax.axis_size("sub") * lax.axis_size("comp")

    def shift(value, axes, count, by):
        return lax.ppermute(value, axes, [(i, (i + by) % count) for i in range(count)])

    from_right = shift(left, column_axes, column_count, -1)
    from_left = shift(right, column_axes, column_count, 1)
    from_down = shift(up, "tile", tile_count, -1)
    from_up = shift(down, "tile", tile_count, 1)

    sums, wair = pl.pallas_call(
        send_kernel,
        out_shape=[shape(tile_count, 2 * rows, cols), shape(1, cells)],
        in_specs=[hbm] * 5,
        out_specs=[vmem] * 2,
        scratch_shapes=[pltpu.VMEM((rows, cols), F32)]
        + [pltpu.VMEM((1, cells), jnp.int32)] * 3
        + [pltpu.VMEM((1, cells), F32), pltpu.SemaphoreType.DMA((5,))],
        compiler_params=whole,
        cost_estimate=pl.CostEstimate(flops=0, bytes_accessed=20_000_000, transcendentals=0),
        name="exchange_send",
    )(air_temp, atm_cell, dest, sea_cell, weight)
    sums = lax.psum_scatter(sums, "tile", scatter_dimension=0)
    sst = lax.all_gather(ocean_state[0, 0], "tile")
    left_all = lax.all_gather(from_left, "tile")
    right_all = lax.all_gather(from_right, "tile")

    moved = (wave_speed, atm_state, ocean_state, depth, diffusivity, left_all, right_all)
    kept = (wet_mask, atm_cell, dest, sea_cell, weight, wair, sst, sums, from_up, from_down, from_left, from_right)
    return tuple(
        pl.pallas_call(
            final_kernel,
            out_shape=[shape(*atm_state.shape), shape(*ocean_state.shape)],
            in_specs=[hbm] * (len(moved) + len(kept)),
            out_specs=[hbm] * 2,
            scratch_shapes=[pltpu.SMEM(wave_speed.shape, F32)]
            + [pltpu.VMEM((levels, full, 2 * cols), F32)] * 3
            + [
                pltpu.VMEM((*ocean_state.shape[:2], full, 2 * cols), F32),
                pltpu.VMEM((3, full, 2 * cols), F32),
            ]
            + [pltpu.VMEM(x.shape, x.dtype) for x in kept]
            + [
                pltpu.VMEM((2, 2, 8, lanes), F32),
                pltpu.VMEM((2 * (lanes // cols), 2 * AH, cols), F32),
                pltpu.VMEM(atm_state.shape, F32),
                pltpu.VMEM(ocean_state.shape, F32),
                pltpu.SemaphoreType.DMA((len(moved) + len(kept) + 20,)),
            ],
            compiler_params=whole,
            name="steps",
        )(*moved, *kept)
    )


def solution(mesh):
    grid = P(("member", "tile"), ("sub", "comp"))
    state = P(None, None, ("member", "tile"), ("sub", "comp"))
    cells = P(("member", "tile"), ("sub", "comp"), None)
    return jax.shard_map(
        functools.partial(on_device, mesh.shape["tile"]),
        mesh=mesh,
        in_specs=(
            state,
            grid,
            grid,
            P(),
            state,
            grid,
            grid,
            cells,
            P(("member", "tile"), ("sub", "comp"), None, None),
            cells,
            cells,
        ),
        out_specs=(state, state),
        check_vma=False,
    )
```

```python
import functools

import jax
import jax.numpy as jnp
from jax import lax
from jax.experimental import pallas as pl
from jax.experimental.pallas import tpu as pltpu
from jax.sharding import PartitionSpec as P

ACOUSTIC = 2
OCEAN_STEPS = 2
AH = 2 * ACOUSTIC
OH = OCEAN_STEPS

ATM_GAIN = 0.5
SEA_GAIN = 0.5

F32 = jnp.float32
BF16 = jnp.bfloat16


def lane_slots(levels, tracers):
    slots = [AH * i for i in range(3 * levels)]
    base = AH * 3 * levels
    slots += [base + OH * i for i in range(tracers)]
    base += OH * tracers
    slots += [base + AH * i for i in range(3)]
    total = base + 3 * AH
    return slots, -(-total // 128) * 128


def row_slots(levels, tracers):
    per = 3 * AH - 2
    base = per * levels
    misc = base + OH * tracers
    return per, base, misc, misc + AH + 2 * OH


def split3(value):
    hi = value.astype(BF16)
    rest = value - hi.astype(F32)
    mid = rest.astype(BF16)
    low = (rest - mid.astype(F32)).astype(BF16)
    return hi, mid, low


def one_hot(index, size):
    shape = (size, index.shape[-1])
    return lax.broadcasted_iota(jnp.int32, shape, 0) == index


def gather_rows(table, hot_rows, hot_cols):
    r = table.shape[0]
    parts = jnp.concatenate(split3(table), axis=0)
    g = jnp.dot(parts, hot_cols, preferred_element_type=F32)
    g = g[0:r] + g[r : 2 * r] + g[2 * r : 3 * r]
    return jnp.sum(jnp.where(hot_rows, g, 0.0), axis=0, keepdims=True)


def scatter_rows(values, hot_rows, hot_cols):
    r = hot_rows.shape[0]
    parts = []
    for value in values:
        for part in split3(value):
            parts.append(jnp.where(hot_rows, part.astype(F32), 0.0).astype(BF16))
    s = lax.dot_general(
        jnp.concatenate(parts, axis=0),
        hot_cols,
        (((1,), (1,)), ((), ())),
        preferred_element_type=F32,
    )
    out = []
    for i in range(len(values)):
        base = 3 * r * i
        out.append(s[base : base + r] + s[base + r : base + 2 * r] + s[base + 2 * r : base + 3 * r])
    return out


def tile_at(shift, tiles):
    return lax.rem(lax.axis_index("tile") + shift % tiles, tiles)


def first_kernel(tiles, *refs):
    sources, (left_out, right_out, up_out, down_out, wair_out, *sums_out) = refs[:10], refs[10:-17]
    held, (up, down, left, right, wair_buf, sums, sems) = refs[-17:-7], refs[-7:]
    atm, ocean, depth, wet, kappa, air, atm_cell, dest, sea_cell, weight = held
    used = []

    def copy(source, target):
        used.append(pltpu.make_async_copy(source, target, sems.at[len(used)]))
        used[-1].start()

    for source, target in zip(sources, held):
        copy(source, target)
    levels = atm.shape[1]
    rows, cols = atm.shape[2:]
    tracers = ocean.shape[0] * ocean.shape[1]
    each = ocean.shape[1]
    per, obase, mbase, _ = row_slots(levels, tracers)
    slots, _ = lane_slots(levels, tracers)
    for one in used:
        one.wait()
    arrived = len(used)
    wetness = wet[...].astype(F32)

    lane = lax.broadcasted_iota(jnp.int32, (rows, cols), 1)
    fields = [(atm, (k, l), AH) for k in range(3) for l in range(levels)]
    fields += [(ocean, (i // each, i % each), OH) for i in range(tracers)]
    fields += [(depth, None, AH), (None, None, AH), (kappa, None, AH)]
    packed = {}
    for (ref, at, width), slot in zip(fields, slots):
        value = wetness if ref is None else (ref[...] if at is None else ref[at[0], at[1]])
        tile, offset = slot // cols, slot % cols
        mask = (lane >= offset) & (lane < offset + width)
        first = pltpu.roll(value, offset, 1) if offset else value
        turn = (offset + width) % cols
        last = pltpu.roll(value, turn, 1) if turn else value
        if tile in packed:
            a, b = packed[tile]
            packed[tile] = (jnp.where(mask, first, a), jnp.where(mask, last, b))
        else:
            packed[tile] = (first, last)
    for tile, (a, b) in packed.items():
        where = slice(tile * cols, (tile + 1) * cols)
        left[:, where] = a
        right[:, where] = b

    copy(left, left_out)
    copy(right, right_out)

    for level in range(levels):
        base = per * level
        for at, which, width in ((0, 1, AH), (AH, 0, AH - 1), (2 * AH - 1, 2, AH - 1)):
            up[base + at : base + at + width, :] = atm[which, level, 0:width, :]
            down[base + at : base + at + width, :] = atm[which, level, rows - width : rows, :]
    for i in range(tracers):
        at = obase + OH * i
        up[at : at + OH, :] = ocean[i // each, i % each, 0:OH, :]
        down[at : at + OH, :] = ocean[i // each, i % each, rows - OH : rows, :]
    for at, value, width in (
        (mbase, depth[...], AH),
        (mbase + AH, wetness, OH),
        (mbase + AH + OH, kappa[...], OH),
    ):
        up[at : at + width, :] = value[0:width]
        down[at : at + width, :] = value[rows - width : rows]
    halo = up.shape[0]
    copy(up, up_out.at[0:halo])
    copy(down, down_out.at[0:halo])

    cell = atm_cell[...]
    hot_atm = jnp.where(one_hot(cell % cols, cols), 1.0, 0.0).astype(BF16)
    airx = gather_rows(air[...], one_hot(cell // cols, rows), hot_atm)
    w = weight[...]
    wair = w * airx
    wair_buf[...] = wair
    copy(wair_buf, wair_out)
    cell = sea_cell[...]
    hot_sea = jnp.where(one_hot(cell % cols, cols), 1.0, 0.0).astype(BF16)
    row = dest[...] * rows + cell // cols
    for shift in range(tiles):
        target = tile_at(shift, tiles)
        s1, s2 = scatter_rows([wair, w], one_hot(row - target * rows, rows), hot_sea)
        sums[shift, 0:rows, :] = s1
        sums[shift, rows : 2 * rows, :] = s2
        sums[shift, 2 * rows : 3 * rows, :] = ocean[0, 0]
        if len(sums_out) == 1:
            copy(sums.at[shift], sums_out[0].at[target])
        elif shift == 1:
            copy(sums.at[shift], down_out.at[halo : halo + 3 * rows])
        elif shift == tiles - 1:
            copy(sums.at[shift], up_out.at[halo : halo + 3 * rows])
        else:
            copy(sums.at[shift], sums_out[max(shift - 1, 0)])
    for one in used[arrived:]:
        one.wait()


def strips(cols, slot, width, left_part, right_part):
    low_half = lax.broadcasted_iota(jnp.int32, (1, cols), 1) < cols // 2
    offset = slot % cols
    a, b = right_part(slot // cols), left_part(slot // cols)
    if offset:
        a = pltpu.roll(a, cols - offset, 1)
    turn = (cols - width - offset) % cols
    if turn:
        b = pltpu.roll(b, turn, 1)
    return jnp.where(low_half, a, b)


def row_slices(levels, tracers):
    per, obase, mbase, _ = row_slots(levels, tracers)
    out = [(per * level + AH, AH - 1) for level in range(levels)]
    out += [(per * level, AH) for level in range(levels)]
    out += [(per * level + 2 * AH - 1, AH - 1) for level in range(levels)]
    out += [(obase + OH * i, OH) for i in range(tracers)]
    return out + [(mbase, AH), (mbase + AH, OH), (mbase + AH + OH, OH)]


def final_kernel(tiles, *refs):
    speed_in, atm_in, ocean_in, depth_in, kappa_in = refs[:5]
    kept = (len(refs) - 5 - 8 - 4) // 2
    sources, rest = refs[5 : 5 + kept], refs[5 + kept :]
    atm_out, ocean_out, speed, us, vs, hs, fs, ms = rest[:8]
    held, (edge, atm_buf, ocean_buf, sems) = rest[8 : 8 + kept], rest[8 + kept :]
    wet, atm_cell, dest, sea_cell, weight, wair, from_up, from_down, from_left, from_right, from_below, from_above = held[:12]
    messages = held[12:]
    levels = us.shape[0]
    each = ocean_out.shape[1]
    tracers = ocean_out.shape[0] * each
    rows, cols = atm_out.shape[2:]
    slots, lanes = lane_slots(levels, tracers)
    slices = row_slices(levels, tracers)
    full = rows + 2 * AH
    block = (slice(None), slice(0, rows), slice(0, cols))
    pairs = list(zip(sources, held)) + [(speed_in, speed)]
    pairs += [(atm_in.at[i], ref.at[block]) for i, ref in enumerate((us, vs, hs))]
    pairs += [(ocean_in.at[i], fs.at[(i, *block)]) for i in range(ocean_out.shape[0])]
    pairs += [(ref, ms.at[(i, *block[1:])]) for i, ref in ((0, depth_in), (2, kappa_in))]
    copies = [pltpu.make_async_copy(source, target, sems.at[i]) for i, (source, target) in enumerate(pairs)]
    for copy in copies:
        copy.start()
    for copy in copies:
        copy.wait()

    halo = row_slots(levels, tracers)[3]

    def message(shift, part):
        where = slice(part * rows, (part + 1) * rows)
        if len(messages) == 1:
            return messages[0][tile_at(-shift, tiles), where, :]
        if shift in (1, tiles - 1):
            return (from_up if shift == 1 else from_down)[halo + part * rows : halo + (part + 1) * rows, :]
        return messages[max(shift - 1, 0)][where, :]

    surface = fs[0, 0, 0:rows, 0:cols]
    cell = sea_cell[...]
    hot_sea = jnp.where(one_hot(cell % cols, cols), 1.0, 0.0).astype(BF16)
    row = dest[...] * rows + cell // cols
    s1, s2 = message(0, 0), message(0, 1)
    sstx = jnp.zeros(cell.shape, F32)
    for shift in range(tiles):
        if shift:
            s1 = s1 + message(shift, 0)
            s2 = s2 + message(shift, 1)
        sstx = sstx + gather_rows(message(shift, 2), one_hot(row - tile_at(-shift, tiles) * rows, rows), hot_sea)
    sea_flux = s1 - surface * s2
    flux = wair[...] - weight[...] * sstx
    cell = atm_cell[...]
    hot_atm = jnp.where(one_hot(cell % cols, cols), 1.0, 0.0).astype(BF16)
    (atm_flux,) = scatter_rows([flux], one_hot(cell // cols, rows), hot_atm)

    half = lanes // cols
    for i in range(2 * half):
        at, where = i // half * AH, slice(i % half * cols, (i % half + 1) * cols)
        edge[i, 0:AH, :] = from_below[at : at + AH, where]
        edge[i, AH : 2 * AH, :] = from_above[at : at + AH, where]

    def extend(view, field, width):
        at, high = slices[field]
        slot = slots[field]
        view[rows : rows + high, 0:cols] = from_down[at : at + high, :]
        view[full - high : full, 0:cols] = from_up[at : at + high, :]
        view[0:rows, cols : 2 * cols] = strips(
            cols,
            slot,
            width,
            lambda t: from_left[:, t * cols : (t + 1) * cols],
            lambda t: from_right[:, t * cols : (t + 1) * cols],
        )
        view[rows:full, cols : 2 * cols] = strips(cols, slot, width, lambda t: edge[t], lambda t: edge[half + t])

    def east(f):
        return pltpu.roll(f, 2 * cols - 1, 1)

    def west(f):
        return pltpu.roll(f, 1, 1)

    def south(f):
        return pltpu.roll(f, full - 1, 0)

    def north(f):
        return pltpu.roll(f, 1, 0)

    base = 3 * levels + tracers
    ms[1, 0:rows, 0:cols] = wet[...].astype(F32)
    for i in range(3):
        extend(ms.at[i], base + i, AH)
    for i in range(tracers):
        extend(fs.at[i // each, i % each], 3 * levels + i, OH)
    for level in range(levels):
        extend(us.at[level], level, AH)
        extend(vs.at[level], levels + level, AH)
        extend(hs.at[level], 2 * levels + level, AH)

    w = ms[1]
    k = ms[2]
    we, ww, ws, wn = east(w), west(w), south(w), north(w)
    for step in range(OCEAN_STEPS):
        for i in range(tracers):
            f = fs[i // each, i % each]
            total = we * (east(f) - f)
            total = total + ww * (west(f) - f)
            total = total + ws * (south(f) - f)
            total = total + wn * (north(f) - f)
            f = f + k * (w * total)
            if step < OCEAN_STEPS - 1:
                fs[i // each, i % each] = f
            else:
                f = f[0:rows, 0:cols]
                ocean_buf[i // each, i % each] = f + SEA_GAIN * sea_flux if i == 0 else f
    used = len(copies)
    copies = [pltpu.make_async_copy(ocean_buf, ocean_out, sems.at[used])]
    copies[0].start()

    d = ms[0]
    chunk = max(1, levels // 4)
    for step in range(ACOUSTIC):
        for level in range(levels):
            u, v, h = us[level], vs[level], hs[level]
            column_speed = speed[level] * d
            hs[level] = h - column_speed * ((east(u) - west(u)) * 0.5 + (south(v) - north(v)) * 0.5)
        for level in range(levels):
            u, v, h = us[level], vs[level], hs[level]
            u = u - (east(h) - west(h)) * 0.5
            v = v - (south(h) - north(h)) * 0.5
            if step < ACOUSTIC - 1:
                us[level], vs[level] = u, v
            else:
                h = h[0:rows, 0:cols]
                atm_buf[0, level] = u[0:rows, 0:cols]
                atm_buf[1, level] = v[0:rows, 0:cols]
                atm_buf[2, level] = h - ATM_GAIN * atm_flux if level == levels - 1 else h
                if (level + 1) % chunk == 0:
                    where = pl.ds(level + 1 - chunk, chunk)
                    copies.append(
                        pltpu.make_async_copy(
                            atm_buf.at[:, where], atm_out.at[:, where], sems.at[used + len(copies)]
                        )
                    )
                    copies[-1].start()
    for copy in copies:
        copy.wait()


def on_device(
    tile_count,
    atm_state,
    air_temp,
    depth,
    wave_speed,
    ocean_state,
    wet_mask,
    diffusivity,
    xg_atm_cell,
    xg_dest,
    xg_ocean_cell,
    xg_weight,
):
    levels = atm_state.shape[1]
    rows, cols = atm_state.shape[2:]
    tracers = ocean_state.shape[0] * ocean_state.shape[1]
    cells = xg_weight.shape[-1]
    _, lanes = lane_slots(levels, tracers)
    _, _, _, halo = row_slots(levels, tracers)
    message_rows = halo
    vmem = pl.BlockSpec(memory_space=pltpu.VMEM)
    hbm = pl.BlockSpec(memory_space=pltpu.HBM)
    whole = pltpu.CompilerParams(vmem_limit_bytes=64 * 1024 * 1024)
    full = rows + 2 * AH

    def shape(*dims):
        return jax.ShapeDtypeStruct(dims, F32)

    by_shift = tile_count <= 4
    if by_shift:
        message_rows += 3 * rows
        sums = [shape(3 * rows, cols)] * (tile_count - 2)
    else:
        sums = [shape(tile_count, 3 * rows, cols)]
    atm_cell = xg_atm_cell.reshape(1, cells)
    dest = xg_dest.reshape(1, cells)
    sea_cell = xg_ocean_cell.reshape(1, cells)
    weight = xg_weight.reshape(1, cells)
    operands = (atm_state, ocean_state, depth, wet_mask, diffusivity, air_temp, atm_cell, dest, sea_cell, weight)
    left, right, up, down, wair, *messages = pl.pallas_call(
        functools.partial(first_kernel, tile_count),
        out_shape=[shape(rows, lanes)] * 2 + [shape(message_rows, cols)] * 2 + [shape(1, cells)] + sums,
        in_specs=[hbm] * 10,
        out_specs=[hbm] * (5 + len(sums)),
        scratch_shapes=[pltpu.VMEM(x.shape, x.dtype) for x in operands]
        + [pltpu.VMEM((halo, cols), F32)] * 2
        + [pltpu.VMEM((rows, lanes), F32)] * 2
        + [
            pltpu.VMEM((1, cells), F32),
            pltpu.VMEM((tile_count, 3 * rows, cols), F32),
            pltpu.SemaphoreType.DMA((15 + tile_count,)),
        ],
        compiler_params=whole,
        name="first",
    )(*operands)

    column_axes = ("sub", "comp")
    column_count = lax.axis_size("sub") * lax.axis_size("comp")

    def shift(value, axes, count, by):
        return lax.ppermute(value, axes, [(i, (i + by) % count) for i in range(count)])

    from_right = shift(left, column_axes, column_count, -1)
    from_left = shift(right, column_axes, column_count, 1)
    from_down = shift(up, "tile", tile_count, -1)
    from_up = shift(down, "tile", tile_count, 1)

    from_below = shift(jnp.concatenate([from_left[0:AH], from_right[0:AH]]), "tile", tile_count, -1)
    from_above = shift(jnp.concatenate([from_left[rows - AH :], from_right[rows - AH :]]), "tile", tile_count, 1)
    if by_shift:
        got = messages[:1] + [shift(messages[s - 1], "tile", tile_count, s) for s in range(2, tile_count - 1)]
    else:
        got = [lax.all_to_all(messages[0], "tile", split_axis=0, concat_axis=0, tiled=True)]

    operands = (wave_speed, atm_state, ocean_state, depth, diffusivity)
    operands += (wet_mask, atm_cell, dest, sea_cell, weight, wair, from_up, from_down, from_left, from_right)
    operands += (from_below, from_above, *got)
    return tuple(
        pl.pallas_call(
            functools.partial(final_kernel, tile_count),
            out_shape=[shape(*atm_state.shape), shape(*ocean_state.shape)],
            in_specs=[hbm] * len(operands),
            out_specs=[hbm] * 2,
            scratch_shapes=[pltpu.SMEM(wave_speed.shape, F32)]
            + [pltpu.VMEM((levels, full, 2 * cols), F32)] * 3
            + [
                pltpu.VMEM((*ocean_state.shape[:2], full, 2 * cols), F32),
                pltpu.VMEM((3, full, 2 * cols), F32),
            ]
            + [pltpu.VMEM(x.shape, x.dtype) for x in operands[5:]]
            + [
                pltpu.VMEM((2 * (lanes // cols), 2 * AH, cols), F32),
                pltpu.VMEM(atm_state.shape, F32),
                pltpu.VMEM(ocean_state.shape, F32),
                pltpu.SemaphoreType.DMA((len(operands) + 10,)),
            ],
            compiler_params=whole,
            name="steps",
        )(*operands)
    )


def solution(mesh):
    grid = P(("member", "tile"), ("sub", "comp"))
    state = P(None, None, ("member", "tile"), ("sub", "comp"))
    cells = P(("member", "tile"), ("sub", "comp"), None)
    return jax.shard_map(
        functools.partial(on_device, mesh.shape["tile"]),
        mesh=mesh,
        in_specs=(
            state,
            grid,
            grid,
            P(),
            state,
            grid,
            grid,
            cells,
            P(("member", "tile"), ("sub", "comp"), None, None),
            cells,
            cells,
        ),
        out_specs=(state, state),
        check_vma=False,
    )
```

```python
import functools

import jax
import jax.numpy as jnp
from jax import lax
from jax.experimental import pallas as pl
from jax.experimental.pallas import tpu as pltpu
from jax.sharding import PartitionSpec as P

ACOUSTIC = 2
OCEAN_STEPS = 2
AH = 2 * ACOUSTIC
OH = OCEAN_STEPS

ATM_GAIN = 0.5
SEA_GAIN = 0.5

F32 = jnp.float32
BF16 = jnp.bfloat16


def lane_slots(levels, tracers):
    slots = [AH * i for i in range(3 * levels)]
    base = AH * 3 * levels
    slots += [base + OH * i for i in range(tracers)]
    base += OH * tracers
    slots += [base + AH * i for i in range(3)]
    total = base + 3 * AH
    return slots, -(-total // 128) * 128


def row_slots(levels, tracers):
    per = 3 * AH - 2
    base = per * levels
    misc = base + OH * tracers
    return per, base, misc, misc + AH + 2 * OH


def split3(value):
    hi = value.astype(BF16)
    rest = value - hi.astype(F32)
    mid = rest.astype(BF16)
    low = (rest - mid.astype(F32)).astype(BF16)
    return hi, mid, low


def one_hot(index, size):
    shape = (size, index.shape[-1])
    return lax.broadcasted_iota(jnp.int32, shape, 0) == index


def gather_rows(table, hot_rows, hot_cols):
    r = table.shape[0]
    parts = jnp.concatenate(split3(table), axis=0)
    g = jnp.dot(parts, hot_cols, preferred_element_type=F32)
    g = g[0:r] + g[r : 2 * r] + g[2 * r : 3 * r]
    return jnp.sum(jnp.where(hot_rows, g, 0.0), axis=0, keepdims=True)


def scatter_rows(values, hot_rows, hot_cols):
    r = hot_rows.shape[0]
    parts = []
    for value in values:
        for part in split3(value):
            parts.append(jnp.where(hot_rows, part.astype(F32), 0.0).astype(BF16))
    s = lax.dot_general(
        jnp.concatenate(parts, axis=0),
        hot_cols,
        (((1,), (1,)), ((), ())),
        preferred_element_type=F32,
    )
    out = []
    for i in range(len(values)):
        base = 3 * r * i
        out.append(s[base : base + r] + s[base + r : base + 2 * r] + s[base + 2 * r : base + 3 * r])
    return out


def tile_at(shift, tiles):
    return lax.rem(lax.axis_index("tile") + shift % tiles, tiles)


def first_kernel(tiles, *refs):
    sources, (left_out, right_out, up_out, down_out, wair_out, *sums_out) = refs[:10], refs[10:-17]
    held, (up, down, left, right, wair_buf, sums, sems) = refs[-17:-7], refs[-7:]
    atm, ocean, depth, wet, kappa, air, atm_cell, dest, sea_cell, weight = held
    used = []

    def copy(source, target):
        used.append(pltpu.make_async_copy(source, target, sems.at[len(used)]))
        used[-1].start()

    for source, target in zip(sources, held):
        copy(source, target)
    levels = atm.shape[1]
    rows, cols = atm.shape[2:]
    tracers = ocean.shape[0] * ocean.shape[1]
    each = ocean.shape[1]
    per, obase, mbase, _ = row_slots(levels, tracers)
    slots, _ = lane_slots(levels, tracers)
    for one in used:
        one.wait()
    arrived = len(used)
    wetness = wet[...].astype(F32)

    lane = lax.broadcasted_iota(jnp.int32, (rows, cols), 1)
    fields = [(atm, (k, l), AH) for k in range(3) for l in range(levels)]
    fields += [(ocean, (i // each, i % each), OH) for i in range(tracers)]
    fields += [(depth, None, AH), (None, None, AH), (kappa, None, AH)]
    packed = {}
    for (ref, at, width), slot in zip(fields, slots):
        value = wetness if ref is None else (ref[...] if at is None else ref[at[0], at[1]])
        tile, offset = slot // cols, slot % cols
        mask = (lane >= offset) & (lane < offset + width)
        first = pltpu.roll(value, offset, 1) if offset else value
        turn = (offset + width) % cols
        last = pltpu.roll(value, turn, 1) if turn else value
        if tile in packed:
            a, b = packed[tile]
            packed[tile] = (jnp.where(mask, first, a), jnp.where(mask, last, b))
        else:
            packed[tile] = (first, last)
    for tile, (a, b) in packed.items():
        where = slice(tile * cols, (tile + 1) * cols)
        left[:, where] = a
        right[:, where] = b

    copy(left, left_out)
    copy(right, right_out)

    for level in range(levels):
        base = per * level
        for at, which, width in ((0, 1, AH), (AH, 0, AH - 1), (2 * AH - 1, 2, AH - 1)):
            up[base + at : base + at + width, :] = atm[which, level, 0:width, :]
            down[base + at : base + at + width, :] = atm[which, level, rows - width : rows, :]
    for i in range(tracers):
        at = obase + OH * i
        up[at : at + OH, :] = ocean[i // each, i % each, 0:OH, :]
        down[at : at + OH, :] = ocean[i // each, i % each, rows - OH : rows, :]
    for at, value, width in (
        (mbase, depth[...], AH),
        (mbase + AH, wetness, OH),
        (mbase + AH + OH, kappa[...], OH),
    ):
        up[at : at + width, :] = value[0:width]
        down[at : at + width, :] = value[rows - width : rows]
    halo = up.shape[0]
    copy(up, up_out.at[0:halo])
    copy(down, down_out.at[0:halo])

    cell = atm_cell[...]
    hot_atm = jnp.where(one_hot(cell % cols, cols), 1.0, 0.0).astype(BF16)
    airx = gather_rows(air[...], one_hot(cell // cols, rows), hot_atm)
    w = weight[...]
    wair = w * airx
    wair_buf[...] = wair
    copy(wair_buf, wair_out)
    cell = sea_cell[...]
    hot_sea = jnp.where(one_hot(cell % cols, cols), 1.0, 0.0).astype(BF16)
    row = dest[...] * rows + cell // cols
    for shift in range(tiles):
        target = tile_at(shift, tiles)
        s1, s2 = scatter_rows([wair, w], one_hot(row - target * rows, rows), hot_sea)
        sums[shift, 0:rows, :] = s1
        sums[shift, rows : 2 * rows, :] = s2
        sums[shift, 2 * rows : 3 * rows, :] = ocean[0, 0]
        if len(sums_out) == 1:
            copy(sums.at[shift], sums_out[0].at[target])
        elif shift == 1:
            copy(sums.at[shift], down_out.at[halo : halo + 3 * rows])
        elif shift == tiles - 1:
            copy(sums.at[shift], up_out.at[halo : halo + 3 * rows])
        else:
            copy(sums.at[shift], sums_out[max(shift - 1, 0)])
    for one in used[arrived:]:
        one.wait()


def strips(cols, slot, width, left_part, right_part):
    low_half = lax.broadcasted_iota(jnp.int32, (1, cols), 1) < cols // 2
    offset = slot % cols
    a, b = right_part(slot // cols), left_part(slot // cols)
    if offset:
        a = pltpu.roll(a, cols - offset, 1)
    turn = (cols - width - offset) % cols
    if turn:
        b = pltpu.roll(b, turn, 1)
    return jnp.where(low_half, a, b)


def row_slices(levels, tracers):
    per, obase, mbase, _ = row_slots(levels, tracers)
    out = [(per * level + AH, AH - 1) for level in range(levels)]
    out += [(per * level, AH) for level in range(levels)]
    out += [(per * level + 2 * AH - 1, AH - 1) for level in range(levels)]
    out += [(obase + OH * i, OH) for i in range(tracers)]
    return out + [(mbase, AH), (mbase + AH, OH), (mbase + AH + OH, OH)]


def final_kernel(tiles, *refs):
    speed_in, atm_in, ocean_in, depth_in, kappa_in = refs[:5]
    kept = (len(refs) - 5 - 8 - 4) // 2
    sources, rest = refs[5 : 5 + kept], refs[5 + kept :]
    atm_out, ocean_out, speed, us, vs, hs, fs, ms = rest[:8]
    held, (edge, atm_buf, ocean_buf, sems) = rest[8 : 8 + kept], rest[8 + kept :]
    wet, atm_cell, dest, sea_cell, weight, wair, from_up, from_down, from_left, from_right, from_below, from_above = held[:12]
    messages = held[12:]
    levels = us.shape[0]
    each = ocean_out.shape[1]
    tracers = ocean_out.shape[0] * each
    rows, cols = atm_out.shape[2:]
    slots, lanes = lane_slots(levels, tracers)
    slices = row_slices(levels, tracers)
    full = rows + 2 * AH
    block = (slice(None), slice(0, rows), slice(0, cols))
    pairs = list(zip(sources, held)) + [(speed_in, speed)]
    pairs += [(atm_in.at[i], ref.at[block]) for i, ref in enumerate((us, vs, hs))]
    pairs += [(ocean_in.at[i], fs.at[(i, *block)]) for i in range(ocean_out.shape[0])]
    pairs += [(ref, ms.at[(i, *block[1:])]) for i, ref in ((0, depth_in), (2, kappa_in))]
    copies = [pltpu.make_async_copy(source, target, sems.at[i]) for i, (source, target) in enumerate(pairs)]
    for copy in copies:
        copy.start()
    for copy in copies:
        copy.wait()

    halo = row_slots(levels, tracers)[3]

    def message(shift, part):
        where = slice(part * rows, (part + 1) * rows)
        if len(messages) == 1:
            return messages[0][tile_at(-shift, tiles), where, :]
        if shift in (1, tiles - 1):
            return (from_up if shift == 1 else from_down)[halo + part * rows : halo + (part + 1) * rows, :]
        return messages[max(shift - 1, 0)][where, :]

    surface = fs[0, 0, 0:rows, 0:cols]
    cell = sea_cell[...]
    hot_sea = jnp.where(one_hot(cell % cols, cols), 1.0, 0.0).astype(BF16)
    row = dest[...] * rows + cell // cols
    s1, s2 = message(0, 0), message(0, 1)
    sstx = jnp.zeros(cell.shape, F32)
    for shift in range(tiles):
        if shift:
            s1 = s1 + message(shift, 0)
            s2 = s2 + message(shift, 1)
        sstx = sstx + gather_rows(message(shift, 2), one_hot(row - tile_at(-shift, tiles) * rows, rows), hot_sea)
    sea_flux = s1 - surface * s2
    flux = wair[...] - weight[...] * sstx
    cell = atm_cell[...]
    hot_atm = jnp.where(one_hot(cell % cols, cols), 1.0, 0.0).astype(BF16)
    (atm_flux,) = scatter_rows([flux], one_hot(cell // cols, rows), hot_atm)

    half = lanes // cols
    for i in range(2 * half):
        at, where = i // half * AH, slice(i % half * cols, (i % half + 1) * cols)
        edge[i, 0:AH, :] = from_below[at : at + AH, where]
        edge[i, AH : 2 * AH, :] = from_above[at : at + AH, where]

    def extend(view, field, width):
        at, high = slices[field]
        slot = slots[field]
        view[rows : rows + high, 0:cols] = from_down[at : at + high, :]
        view[full - high : full, 0:cols] = from_up[at : at + high, :]
        view[0:rows, cols : 2 * cols] = strips(
            cols,
            slot,
            width,
            lambda t: from_left[:, t * cols : (t + 1) * cols],
            lambda t: from_right[:, t * cols : (t + 1) * cols],
        )
        view[rows:full, cols : 2 * cols] = strips(cols, slot, width, lambda t: edge[t], lambda t: edge[half + t])

    def east(f):
        return pltpu.roll(f, 2 * cols - 1, 1)

    def west(f):
        return pltpu.roll(f, 1, 1)

    def south(f):
        return pltpu.roll(f, full - 1, 0)

    def north(f):
        return pltpu.roll(f, 1, 0)

    base = 3 * levels + tracers
    ms[1, 0:rows, 0:cols] = wet[...].astype(F32)
    for i in range(3):
        extend(ms.at[i], base + i, AH)
    for i in range(tracers):
        extend(fs.at[i // each, i % each], 3 * levels + i, OH)
    for level in range(levels):
        extend(us.at[level], level, AH)
        extend(vs.at[level], levels + level, AH)
        extend(hs.at[level], 2 * levels + level, AH)

    w = ms[1]
    k = ms[2]
    we, ww, ws, wn = east(w), west(w), south(w), north(w)
    for step in range(OCEAN_STEPS):
        for i in range(tracers):
            f = fs[i // each, i % each]
            total = we * (east(f) - f)
            total = total + ww * (west(f) - f)
            total = total + ws * (south(f) - f)
            total = total + wn * (north(f) - f)
            f = f + k * (w * total)
            if step < OCEAN_STEPS - 1:
                fs[i // each, i % each] = f
            else:
                f = f[0:rows, 0:cols]
                ocean_buf[i // each, i % each] = f + SEA_GAIN * sea_flux if i == 0 else f
    used = len(copies)
    copies = [pltpu.make_async_copy(ocean_buf, ocean_out, sems.at[used])]
    copies[0].start()

    d = ms[0]
    chunk = max(1, levels // 4)
    for step in range(ACOUSTIC):
        for level in range(levels):
            u, v, h = us[level], vs[level], hs[level]
            column_speed = speed[level] * d
            hs[level] = h - column_speed * ((east(u) - west(u)) * 0.5 + (south(v) - north(v)) * 0.5)
        for level in range(levels):
            u, v, h = us[level], vs[level], hs[level]
            u = u - (east(h) - west(h)) * 0.5
            v = v - (south(h) - north(h)) * 0.5
            if step < ACOUSTIC - 1:
                us[level], vs[level] = u, v
            else:
                h = h[0:rows, 0:cols]
                atm_buf[0, level] = u[0:rows, 0:cols]
                atm_buf[1, level] = v[0:rows, 0:cols]
                atm_buf[2, level] = h - ATM_GAIN * atm_flux if level == levels - 1 else h
                if (level + 1) % chunk == 0:
                    where = pl.ds(level + 1 - chunk, chunk)
                    copies.append(
                        pltpu.make_async_copy(
                            atm_buf.at[:, where], atm_out.at[:, where], sems.at[used + len(copies)]
                        )
                    )
                    copies[-1].start()
    for copy in copies:
        copy.wait()


def on_device(
    tile_count,
    atm_state,
    air_temp,
    depth,
    wave_speed,
    ocean_state,
    wet_mask,
    diffusivity,
    xg_atm_cell,
    xg_dest,
    xg_ocean_cell,
    xg_weight,
):
    levels = atm_state.shape[1]
    rows, cols = atm_state.shape[2:]
    tracers = ocean_state.shape[0] * ocean_state.shape[1]
    cells = xg_weight.shape[-1]
    _, lanes = lane_slots(levels, tracers)
    _, _, _, halo = row_slots(levels, tracers)
    message_rows = halo
    vmem = pl.BlockSpec(memory_space=pltpu.VMEM)
    hbm = pl.BlockSpec(memory_space=pltpu.HBM)
    whole = pltpu.CompilerParams(vmem_limit_bytes=64 * 1024 * 1024)
    full = rows + 2 * AH

    def shape(*dims):
        return jax.ShapeDtypeStruct(dims, F32)

    by_shift = tile_count <= 4
    if by_shift:
        message_rows += 3 * rows
        sums = [shape(3 * rows, cols)] * (tile_count - 2)
    else:
        sums = [shape(tile_count, 3 * rows, cols)]
    atm_cell = xg_atm_cell.reshape(1, cells)
    dest = xg_dest.reshape(1, cells)
    sea_cell = xg_ocean_cell.reshape(1, cells)
    weight = xg_weight.reshape(1, cells)
    operands = (atm_state, ocean_state, depth, wet_mask, diffusivity, air_temp, atm_cell, dest, sea_cell, weight)
    left, right, up, down, wair, *messages = pl.pallas_call(
        functools.partial(first_kernel, tile_count),
        out_shape=[shape(rows, lanes)] * 2 + [shape(message_rows, cols)] * 2 + [shape(1, cells)] + sums,
        in_specs=[hbm] * 10,
        out_specs=[hbm] * (5 + len(sums)),
        scratch_shapes=[pltpu.VMEM(x.shape, x.dtype) for x in operands]
        + [pltpu.VMEM((halo, cols), F32)] * 2
        + [pltpu.VMEM((rows, lanes), F32)] * 2
        + [
            pltpu.VMEM((1, cells), F32),
            pltpu.VMEM((tile_count, 3 * rows, cols), F32),
            pltpu.SemaphoreType.DMA((15 + tile_count,)),
        ],
        compiler_params=whole,
        name="first",
    )(*operands)

    column_axes = ("sub", "comp")
    column_count = lax.axis_size("sub") * lax.axis_size("comp")

    def shift(value, axes, count, by):
        return lax.ppermute(value, axes, [(i, (i + by) % count) for i in range(count)])

    from_right = shift(left, column_axes, column_count, -1)
    from_left = shift(right, column_axes, column_count, 1)
    from_down = shift(up, "tile", tile_count, -1)
    from_up = shift(down, "tile", tile_count, 1)

    from_below = shift(jnp.concatenate([from_left[0:AH], from_right[0:AH]]), "tile", tile_count, -1)
    from_above = shift(jnp.concatenate([from_left[rows - AH :], from_right[rows - AH :]]), "tile", tile_count, 1)
    if by_shift:
        *messages, from_left = lax.optimization_barrier((*messages, from_left))
        got = messages[:1] + [shift(messages[s - 1], "tile", tile_count, s) for s in range(2, tile_count - 1)]
    else:
        got = [lax.all_to_all(messages[0], "tile", split_axis=0, concat_axis=0, tiled=True)]

    operands = (wave_speed, atm_state, ocean_state, depth, diffusivity)
    operands += (wet_mask, atm_cell, dest, sea_cell, weight, wair, from_up, from_down, from_left, from_right)
    operands += (from_below, from_above, *got)
    return tuple(
        pl.pallas_call(
            functools.partial(final_kernel, tile_count),
            out_shape=[shape(*atm_state.shape), shape(*ocean_state.shape)],
            in_specs=[hbm] * len(operands),
            out_specs=[hbm] * 2,
            scratch_shapes=[pltpu.SMEM(wave_speed.shape, F32)]
            + [pltpu.VMEM((levels, full, 2 * cols), F32)] * 3
            + [
                pltpu.VMEM((*ocean_state.shape[:2], full, 2 * cols), F32),
                pltpu.VMEM((3, full, 2 * cols), F32),
            ]
            + [pltpu.VMEM(x.shape, x.dtype) for x in operands[5:]]
            + [
                pltpu.VMEM((2 * (lanes // cols), 2 * AH, cols), F32),
                pltpu.VMEM(atm_state.shape, F32),
                pltpu.VMEM(ocean_state.shape, F32),
                pltpu.SemaphoreType.DMA((len(operands) + 10,)),
            ],
            compiler_params=whole,
            name="steps",
        )(*operands)
    )


def solution(mesh):
    grid = P(("member", "tile"), ("sub", "comp"))
    state = P(None, None, ("member", "tile"), ("sub", "comp"))
    cells = P(("member", "tile"), ("sub", "comp"), None)
    return jax.shard_map(
        functools.partial(on_device, mesh.shape["tile"]),
        mesh=mesh,
        in_specs=(
            state,
            grid,
            grid,
            P(),
            state,
            grid,
            grid,
            cells,
            P(("member", "tile"), ("sub", "comp"), None, None),
            cells,
            cells,
        ),
        out_specs=(state, state),
        check_vma=False,
    )
```

```python
import functools

import jax
import jax.numpy as jnp
from jax import lax
from jax.experimental import pallas as pl
from jax.experimental.pallas import tpu as pltpu
from jax.sharding import PartitionSpec as P

ACOUSTIC = 2
OCEAN_STEPS = 2
AH = 2 * ACOUSTIC
OH = OCEAN_STEPS

ATM_GAIN = 0.5
SEA_GAIN = 0.5

F32 = jnp.float32
BF16 = jnp.bfloat16


def lane_slots(levels, tracers):
    slots = [AH * i for i in range(3 * levels)]
    base = AH * 3 * levels
    slots += [base + OH * i for i in range(tracers)]
    base += OH * tracers
    slots += [base + AH * i for i in range(3)]
    total = base + 3 * AH
    return slots, -(-total // 128) * 128


def row_slots(levels, tracers):
    tracer = 5 * levels
    misc = tracer + OH * tracers
    own = misc + AH + 2 * OH
    _, lanes = lane_slots(levels, tracers)
    return tracer, misc, own, own + 2 * AH * (lanes // 128)


def near_rows(u, v, h, speed, rows, cols):
    east_west = (pltpu.roll(u, cols - 1, 1) - pltpu.roll(u, 1, 1)) * 0.5
    south_north = (pltpu.roll(v, rows - 1, 0) - pltpu.roll(v, 1, 0)) * 0.5
    h1 = h - speed * (east_west + south_north)
    out = []
    for near, turn in ((0, 1), (rows - 1, -1)):
        at = [slice(near + turn * i, near + turn * i + 1) for i in range(3)]
        out.append(
            (
                u[at[0]],
                v[at[0]],
                h[at[0]] - (0.5 * turn) * speed[at[0]] * v[at[1]],
                h1[at[1]],
                h1[at[2]] - (2.0 * turn) * v[at[1]],
            )
        )
    return out


def split3(value):
    hi = value.astype(BF16)
    rest = value - hi.astype(F32)
    mid = rest.astype(BF16)
    low = (rest - mid.astype(F32)).astype(BF16)
    return hi, mid, low


def one_hot(index, size):
    shape = (size, index.shape[-1])
    return lax.broadcasted_iota(jnp.int32, shape, 0) == index


def gather_rows(table, hot_rows, hot_cols):
    r = table.shape[0]
    parts = jnp.concatenate(split3(table), axis=0)
    g = jnp.dot(parts, hot_cols, preferred_element_type=F32)
    g = g[0:r] + g[r : 2 * r] + g[2 * r : 3 * r]
    return jnp.sum(jnp.where(hot_rows, g, 0.0), axis=0, keepdims=True)


def scatter_rows(values, hot_rows, hot_cols):
    r = hot_rows.shape[0]
    parts = []
    for value in values:
        for part in split3(value):
            parts.append(jnp.where(hot_rows, part.astype(F32), 0.0).astype(BF16))
    s = lax.dot_general(
        jnp.concatenate(parts, axis=0),
        hot_cols,
        (((1,), (1,)), ((), ())),
        preferred_element_type=F32,
    )
    out = []
    for i in range(len(values)):
        base = 3 * r * i
        out.append(s[base : base + r] + s[base + r : base + 2 * r] + s[base + 2 * r : base + 3 * r])
    return out


def tile_at(shift, tiles):
    return lax.rem(lax.axis_index("tile") + shift % tiles, tiles)


def first_kernel(tiles, *refs):
    sources, (left_out, right_out, up_out, down_out, wair_out, *sums_out) = refs[:11], refs[11:-18]
    held, (up, down, left, right, wair_buf, sums, sems) = refs[-18:-7], refs[-7:]
    atm, ocean, depth, wet, kappa, air, atm_cell, dest, sea_cell, weight, wave_speed = held
    used = []

    def copy(source, target):
        used.append(pltpu.make_async_copy(source, target, sems.at[len(used)]))
        used[-1].start()

    for source, target in zip(sources, held):
        copy(source, target)
    levels = atm.shape[1]
    rows, cols = atm.shape[2:]
    tracers = ocean.shape[0] * ocean.shape[1]
    each = ocean.shape[1]
    obase, mbase, own, halo = row_slots(levels, tracers)
    slots, _ = lane_slots(levels, tracers)
    for one in used:
        one.wait()
    arrived = len(used)
    wetness = wet[...].astype(F32)

    lane = lax.broadcasted_iota(jnp.int32, (rows, cols), 1)
    fields = [(atm, (k, l), AH) for k in range(3) for l in range(levels)]
    fields += [(ocean, (i // each, i % each), OH) for i in range(tracers)]
    fields += [(depth, None, AH), (None, None, AH), (kappa, None, AH)]
    packed = {}
    for (ref, at, width), slot in zip(fields, slots):
        value = wetness if ref is None else (ref[...] if at is None else ref[at[0], at[1]])
        tile, offset = slot // cols, slot % cols
        mask = (lane >= offset) & (lane < offset + width)
        first = pltpu.roll(value, offset, 1) if offset else value
        turn = (offset + width) % cols
        last = pltpu.roll(value, turn, 1) if turn else value
        if tile in packed:
            a, b = packed[tile]
            packed[tile] = (jnp.where(mask, first, a), jnp.where(mask, last, b))
        else:
            packed[tile] = (first, last)
    for tile, (a, b) in packed.items():
        where = slice(tile * cols, (tile + 1) * cols)
        left[:, where] = a
        right[:, where] = b

    copy(left, left_out)
    copy(right, right_out)

    for level in range(levels):
        speed = wave_speed[level] * depth[...]
        both = near_rows(atm[0, level], atm[1, level], atm[2, level], speed, rows, cols)
        for ref, values in zip((up, down), both):
            for i, value in enumerate(values):
                at = i * levels + level
                ref[at : at + 1, :] = value
    at = own
    for strip in (left, right):
        for i in range(strip.shape[1] // cols):
            where = slice(i * cols, (i + 1) * cols)
            up[at : at + AH, :] = strip[0:AH, where]
            down[at : at + AH, :] = strip[rows - AH : rows, where]
            at += AH
    for i in range(tracers):
        at = obase + OH * i
        up[at : at + OH, :] = ocean[i // each, i % each, 0:OH, :]
        down[at : at + OH, :] = ocean[i // each, i % each, rows - OH : rows, :]
    for at, value, width in (
        (mbase, depth[...], AH),
        (mbase + AH, wetness, OH),
        (mbase + AH + OH, kappa[...], OH),
    ):
        up[at : at + width, :] = value[0:width]
        down[at : at + width, :] = value[rows - width : rows]
    copy(up, up_out.at[0:halo])
    copy(down, down_out.at[0:halo])

    cell = atm_cell[...]
    hot_atm = jnp.where(one_hot(cell % cols, cols), 1.0, 0.0).astype(BF16)
    airx = gather_rows(air[...], one_hot(cell // cols, rows), hot_atm)
    w = weight[...]
    wair = w * airx
    wair_buf[...] = wair
    copy(wair_buf, wair_out)
    cell = sea_cell[...]
    hot_sea = jnp.where(one_hot(cell % cols, cols), 1.0, 0.0).astype(BF16)
    row = dest[...] * rows + cell // cols
    for shift in range(tiles):
        target = tile_at(shift, tiles)
        s1, s2 = scatter_rows([wair, w], one_hot(row - target * rows, rows), hot_sea)
        sums[shift, 0:rows, :] = s1
        sums[shift, rows : 2 * rows, :] = s2
        sums[shift, 2 * rows : 3 * rows, :] = ocean[0, 0]
        if len(sums_out) == 1:
            copy(sums.at[shift], sums_out[0].at[target])
        elif shift == 1:
            copy(sums.at[shift], down_out.at[halo : halo + 3 * rows])
        elif shift == tiles - 1:
            copy(sums.at[shift], up_out.at[halo : halo + 3 * rows])
        else:
            copy(sums.at[shift], sums_out[max(shift - 1, 0)])
    for one in used[arrived:]:
        one.wait()


def strips(cols, slot, width, left_part, right_part):
    low_half = lax.broadcasted_iota(jnp.int32, (1, cols), 1) < cols // 2
    offset = slot % cols
    a, b = right_part(slot // cols), left_part(slot // cols)
    if offset:
        a = pltpu.roll(a, cols - offset, 1)
    turn = (cols - width - offset) % cols
    if turn:
        b = pltpu.roll(b, turn, 1)
    return jnp.where(low_half, a, b)


def final_kernel(tiles, *refs):
    speed_in, atm_in, ocean_in, depth_in, kappa_in = refs[:5]
    kept = (len(refs) - 5 - 8 - 4) // 2
    sources, rest = refs[5 : 5 + kept], refs[5 + kept :]
    atm_out, ocean_out, speed, us, vs, hs, fs, ms = rest[:8]
    held, (edge, atm_buf, ocean_buf, sems) = rest[8 : 8 + kept], rest[8 + kept :]
    wet, atm_cell, dest, sea_cell, weight, wair, from_up, from_down, from_left, from_right, from_below, from_above = held[:12]
    messages = held[12:]
    levels = us.shape[0]
    each = ocean_out.shape[1]
    tracers = ocean_out.shape[0] * each
    rows, cols = atm_out.shape[2:]
    slots, lanes = lane_slots(levels, tracers)
    obase, mbase, own, halo = row_slots(levels, tracers)
    full = rows + 2 * AH
    block = (slice(None), slice(0, rows), slice(0, cols))
    pairs = list(zip(sources, held)) + [(speed_in, speed)]
    pairs += [(atm_in.at[i], ref.at[block]) for i, ref in enumerate((us, vs, hs))]
    pairs += [(ocean_in.at[i], fs.at[(i, *block)]) for i in range(ocean_out.shape[0])]
    pairs += [(ref, ms.at[(i, *block[1:])]) for i, ref in ((0, depth_in), (2, kappa_in))]
    copies = [pltpu.make_async_copy(source, target, sems.at[i]) for i, (source, target) in enumerate(pairs)]
    for copy in copies:
        copy.start()
    for copy in copies:
        copy.wait()

    def message(shift, part):
        where = slice(part * rows, (part + 1) * rows)
        if len(messages) == 1:
            return messages[0][tile_at(-shift, tiles), where, :]
        if shift in (1, tiles - 1):
            return (from_up if shift == 1 else from_down)[halo + part * rows : halo + (part + 1) * rows, :]
        return messages[max(shift - 1, 0)][where, :]

    surface = fs[0, 0, 0:rows, 0:cols]
    cell = sea_cell[...]
    hot_sea = jnp.where(one_hot(cell % cols, cols), 1.0, 0.0).astype(BF16)
    row = dest[...] * rows + cell // cols
    s1, s2 = message(0, 0), message(0, 1)
    sstx = jnp.zeros(cell.shape, F32)
    for shift in range(tiles):
        if shift:
            s1 = s1 + message(shift, 0)
            s2 = s2 + message(shift, 1)
        sstx = sstx + gather_rows(message(shift, 2), one_hot(row - tile_at(-shift, tiles) * rows, rows), hot_sea)
    sea_flux = s1 - surface * s2
    flux = wair[...] - weight[...] * sstx
    cell = atm_cell[...]
    hot_atm = jnp.where(one_hot(cell % cols, cols), 1.0, 0.0).astype(BF16)
    (atm_flux,) = scatter_rows([flux], one_hot(cell // cols, rows), hot_atm)

    half = lanes // cols
    for i in range(2 * half):
        at, where = i // half * AH, slice(i % half * cols, (i % half + 1) * cols)
        edge[i, 0:AH, :] = from_below[at : at + AH, where]
        edge[i, AH : 2 * AH, :] = from_above[at : at + AH, where]
        at = own + AH * i
        edge[2 * half + i, 0:AH, :] = from_down[at : at + AH, :]
        edge[2 * half + i, AH : 2 * AH, :] = from_up[at : at + AH, :]

    def extend(view, field, width):
        slot = slots[field]
        view[0:rows, cols : 2 * cols] = strips(
            cols,
            slot,
            width,
            lambda t: from_left[:, t * cols : (t + 1) * cols],
            lambda t: from_right[:, t * cols : (t + 1) * cols],
        )
        view[rows:full, cols : 2 * cols] = strips(cols, slot, width, lambda t: edge[t], lambda t: edge[half + t])

    def extend_rows(view, at, high):
        view[rows : rows + high, 0:cols] = from_down[at : at + high, :]
        view[full - high : full, 0:cols] = from_up[at : at + high, :]

    lane = lax.broadcasted_iota(jnp.int32, (2 * AH, cols), 1)
    line = lax.broadcasted_iota(jnp.int32, (2 * AH, cols), 0)
    whole_strip = (lane < AH) | (lane >= cols - AH)
    outer = (lane < AH - 1) | (lane > cols - AH)

    def near(which, level):
        at = which * levels + level
        return from_down[at : at + 1, :], from_up[at : at + 1, :]

    def extend_level(view, which, level):
        strip = strips(cols, slots[which * levels + level], AH, lambda t: edge[3 * half + t], lambda t: edge[2 * half + t])
        below, above = near(which, level)
        inner = jnp.where(line == 0, below, jnp.where(line == 2 * AH - 1, above, 0.0))
        view[rows:full, 0:cols] = jnp.where(whole_strip if which == 0 else outer, strip, inner)

    def new_height_rows(tile, level):
        below, above = near(3, level), near(4, level)
        sent = jnp.where(
            line == 1, below[0], jnp.where(line == 2, above[0], jnp.where(line == 2 * AH - 3, above[1], below[1]))
        )
        here = (line == 1) | (line == 2) | (line == 2 * AH - 3) | (line == 2 * AH - 2)
        return jnp.where(here & jnp.logical_not(outer), sent, tile)

    def east(f):
        return pltpu.roll(f, 2 * cols - 1, 1)

    def west(f):
        return pltpu.roll(f, 1, 1)

    def south(f):
        return pltpu.roll(f, full - 1, 0)

    def north(f):
        return pltpu.roll(f, 1, 0)

    base = 3 * levels + tracers
    ms[1, 0:rows, 0:cols] = wet[...].astype(F32)
    for i, (at, high) in enumerate(((mbase, AH), (mbase + AH, OH), (mbase + AH + OH, OH))):
        extend(ms.at[i], base + i, AH)
        extend_rows(ms.at[i], at, high)
    for i in range(tracers):
        extend(fs.at[i // each, i % each], 3 * levels + i, OH)
        extend_rows(fs.at[i // each, i % each], obase + OH * i, OH)
    for level in range(levels):
        for which, ref in enumerate((us, vs, hs)):
            extend(ref.at[level], which * levels + level, AH)
            extend_level(ref.at[level], which, level)

    w = ms[1]
    k = ms[2]
    we, ww, ws, wn = east(w), west(w), south(w), north(w)
    for step in range(OCEAN_STEPS):
        for i in range(tracers):
            f = fs[i // each, i % each]
            total = we * (east(f) - f)
            total = total + ww * (west(f) - f)
            total = total + ws * (south(f) - f)
            total = total + wn * (north(f) - f)
            f = f + k * (w * total)
            if step < OCEAN_STEPS - 1:
                fs[i // each, i % each] = f
            else:
                f = f[0:rows, 0:cols]
                ocean_buf[i // each, i % each] = f + SEA_GAIN * sea_flux if i == 0 else f
    used = len(copies)
    copies = [pltpu.make_async_copy(ocean_buf, ocean_out, sems.at[used])]
    copies[0].start()

    d = ms[0]
    chunk = max(1, levels // 4)
    for step in range(ACOUSTIC):
        for level in range(levels):
            u, v, h = us[level], vs[level], hs[level]
            column_speed = speed[level] * d
            hs[level] = h - column_speed * ((east(u) - west(u)) * 0.5 + (south(v) - north(v)) * 0.5)
            if step == 0:
                hs[level, rows:full, 0:cols] = new_height_rows(hs[level, rows:full, 0:cols], level)
        for level in range(levels):
            u, v, h = us[level], vs[level], hs[level]
            u = u - (east(h) - west(h)) * 0.5
            v = v - (south(h) - north(h)) * 0.5
            if step < ACOUSTIC - 1:
                us[level], vs[level] = u, v
            else:
                h = h[0:rows, 0:cols]
                atm_buf[0, level] = u[0:rows, 0:cols]
                atm_buf[1, level] = v[0:rows, 0:cols]
                atm_buf[2, level] = h - ATM_GAIN * atm_flux if level == levels - 1 else h
                if (level + 1) % chunk == 0:
                    where = pl.ds(level + 1 - chunk, chunk)
                    copies.append(
                        pltpu.make_async_copy(
                            atm_buf.at[:, where], atm_out.at[:, where], sems.at[used + len(copies)]
                        )
                    )
                    copies[-1].start()
    for copy in copies:
        copy.wait()


def on_device(
    tile_count,
    atm_state,
    air_temp,
    depth,
    wave_speed,
    ocean_state,
    wet_mask,
    diffusivity,
    xg_atm_cell,
    xg_dest,
    xg_ocean_cell,
    xg_weight,
):
    levels = atm_state.shape[1]
    rows, cols = atm_state.shape[2:]
    tracers = ocean_state.shape[0] * ocean_state.shape[1]
    cells = xg_weight.shape[-1]
    _, lanes = lane_slots(levels, tracers)
    _, _, _, halo = row_slots(levels, tracers)
    message_rows = halo
    vmem = pl.BlockSpec(memory_space=pltpu.VMEM)
    hbm = pl.BlockSpec(memory_space=pltpu.HBM)
    whole = pltpu.CompilerParams(vmem_limit_bytes=64 * 1024 * 1024)
    full = rows + 2 * AH

    def shape(*dims):
        return jax.ShapeDtypeStruct(dims, F32)

    by_shift = tile_count <= 4
    if by_shift:
        message_rows += 3 * rows
        sums = [shape(3 * rows, cols)] * (tile_count - 2)
    else:
        sums = [shape(tile_count, 3 * rows, cols)]
    atm_cell = xg_atm_cell.reshape(1, cells)
    dest = xg_dest.reshape(1, cells)
    sea_cell = xg_ocean_cell.reshape(1, cells)
    weight = xg_weight.reshape(1, cells)
    operands = (atm_state, ocean_state, depth, wet_mask, diffusivity, air_temp, atm_cell, dest, sea_cell, weight)
    operands += (wave_speed,)
    left, right, up, down, wair, *messages = pl.pallas_call(
        functools.partial(first_kernel, tile_count),
        out_shape=[shape(rows, lanes)] * 2 + [shape(message_rows, cols)] * 2 + [shape(1, cells)] + sums,
        in_specs=[hbm] * 11,
        out_specs=[hbm] * (5 + len(sums)),
        scratch_shapes=[pltpu.VMEM(x.shape, x.dtype) for x in operands[:-1]]
        + [pltpu.SMEM(wave_speed.shape, F32)]
        + [pltpu.VMEM((halo, cols), F32)] * 2
        + [pltpu.VMEM((rows, lanes), F32)] * 2
        + [
            pltpu.VMEM((1, cells), F32),
            pltpu.VMEM((tile_count, 3 * rows, cols), F32),
            pltpu.SemaphoreType.DMA((16 + tile_count,)),
        ],
        compiler_params=whole,
        name="first",
    )(*operands)

    column_axes = ("sub", "comp")
    column_count = lax.axis_size("sub") * lax.axis_size("comp")

    def shift(value, axes, count, by):
        return lax.ppermute(value, axes, [(i, (i + by) % count) for i in range(count)])

    from_right = shift(left, column_axes, column_count, -1)
    from_left = shift(right, column_axes, column_count, 1)
    from_down = shift(up, "tile", tile_count, -1)
    from_up = shift(down, "tile", tile_count, 1)

    from_below = shift(jnp.concatenate([from_left[0:AH], from_right[0:AH]]), "tile", tile_count, -1)
    from_above = shift(jnp.concatenate([from_left[rows - AH :], from_right[rows - AH :]]), "tile", tile_count, 1)
    if by_shift:
        *messages, from_left = lax.optimization_barrier((*messages, from_left))
        got = messages[:1] + [shift(messages[s - 1], "tile", tile_count, s) for s in range(2, tile_count - 1)]
    else:
        got = [lax.all_to_all(messages[0], "tile", split_axis=0, concat_axis=0, tiled=True)]

    operands = (wave_speed, atm_state, ocean_state, depth, diffusivity)
    operands += (wet_mask, atm_cell, dest, sea_cell, weight, wair, from_up, from_down, from_left, from_right)
    operands += (from_below, from_above, *got)
    return tuple(
        pl.pallas_call(
            functools.partial(final_kernel, tile_count),
            out_shape=[shape(*atm_state.shape), shape(*ocean_state.shape)],
            in_specs=[hbm] * len(operands),
            out_specs=[hbm] * 2,
            scratch_shapes=[pltpu.SMEM(wave_speed.shape, F32)]
            + [pltpu.VMEM((levels, full, 2 * cols), F32)] * 3
            + [
                pltpu.VMEM((*ocean_state.shape[:2], full, 2 * cols), F32),
                pltpu.VMEM((3, full, 2 * cols), F32),
            ]
            + [pltpu.VMEM(x.shape, x.dtype) for x in operands[5:]]
            + [
                pltpu.VMEM((4 * (lanes // cols), 2 * AH, cols), F32),
                pltpu.VMEM(atm_state.shape, F32),
                pltpu.VMEM(ocean_state.shape, F32),
                pltpu.SemaphoreType.DMA((len(operands) + 10,)),
            ],
            compiler_params=whole,
            name="steps",
        )(*operands)
    )


def solution(mesh):
    grid = P(("member", "tile"), ("sub", "comp"))
    state = P(None, None, ("member", "tile"), ("sub", "comp"))
    cells = P(("member", "tile"), ("sub", "comp"), None)
    return jax.shard_map(
        functools.partial(on_device, mesh.shape["tile"]),
        mesh=mesh,
        in_specs=(
            state,
            grid,
            grid,
            P(),
            state,
            grid,
            grid,
            cells,
            P(("member", "tile"), ("sub", "comp"), None, None),
            cells,
            cells,
        ),
        out_specs=(state, state),
        check_vma=False,
    )
```

```python
import functools

import jax
import jax.numpy as jnp
from jax import lax
from jax.experimental import pallas as pl
from jax.experimental.pallas import tpu as pltpu
from jax.sharding import PartitionSpec as P

ACOUSTIC = 2
OCEAN_STEPS = 2
AH = 2 * ACOUSTIC
OH = OCEAN_STEPS

ATM_GAIN = 0.5
SEA_GAIN = 0.5

F32 = jnp.float32
BF16 = jnp.bfloat16


def lane_slots(levels, tracers):
    slots = [AH * i for i in range(3 * levels)]
    base = AH * 3 * levels
    slots += [base + OH * i for i in range(tracers)]
    base += OH * tracers
    slots += [base + AH * i for i in range(3)]
    total = base + 3 * AH
    return slots, -(-total // 128) * 128


def row_slots(levels, tracers):
    tracer = 5 * levels
    misc = tracer + OH * tracers
    own = misc + AH + 2 * OH
    _, lanes = lane_slots(levels, tracers)
    return tracer, misc, own, own + 2 * AH * (lanes // 128)


def near_rows(u, v, h, speed, rows, cols):
    east_west = (pltpu.roll(u, cols - 1, 1) - pltpu.roll(u, 1, 1)) * 0.5
    south_north = (pltpu.roll(v, rows - 1, 0) - pltpu.roll(v, 1, 0)) * 0.5
    h1 = h - speed * (east_west + south_north)
    out = []
    for near, turn in ((0, 1), (rows - 1, -1)):
        at = [slice(near + turn * i, near + turn * i + 1) for i in range(3)]
        out.append(
            (
                u[at[0]],
                v[at[0]],
                h[at[0]] - (0.5 * turn) * speed[at[0]] * v[at[1]],
                h1[at[1]],
                h1[at[2]] - (2.0 * turn) * v[at[1]],
            )
        )
    return out


def split3(value):
    hi = value.astype(BF16)
    rest = value - hi.astype(F32)
    mid = rest.astype(BF16)
    low = (rest - mid.astype(F32)).astype(BF16)
    return hi, mid, low


def one_hot(index, size):
    shape = (size, index.shape[-1])
    return lax.broadcasted_iota(jnp.int32, shape, 0) == index


def gather_rows(table, hot_rows, hot_cols):
    r = table.shape[0]
    parts = jnp.concatenate(split3(table), axis=0)
    g = jnp.dot(parts, hot_cols, preferred_element_type=F32)
    g = g[0:r] + g[r : 2 * r] + g[2 * r : 3 * r]
    return jnp.sum(jnp.where(hot_rows, g, 0.0), axis=0, keepdims=True)


def scatter_rows(values, hot_rows, hot_cols):
    r = hot_rows.shape[0]
    parts = []
    for value in values:
        for part in split3(value):
            parts.append(jnp.where(hot_rows, part.astype(F32), 0.0).astype(BF16))
    s = lax.dot_general(
        jnp.concatenate(parts, axis=0),
        hot_cols,
        (((1,), (1,)), ((), ())),
        preferred_element_type=F32,
    )
    out = []
    for i in range(len(values)):
        base = 3 * r * i
        out.append(s[base : base + r] + s[base + r : base + 2 * r] + s[base + 2 * r : base + 3 * r])
    return out


def tile_at(shift, tiles):
    return lax.rem(lax.axis_index("tile") + shift % tiles, tiles)


def tile_parity():
    return lax.rem(lax.axis_index("tile"), 2)


def column_parity():
    return lax.rem(lax.axis_index(("sub", "comp")), 2)


def first_kernel(tiles, *refs):
    sources, (cols_a, cols_b, rows_a, rows_b, wair_out, *sums_out) = refs[:11], refs[11:-18]
    held, (up, down, left, right, wair_buf, sums, sems) = refs[-18:-7], refs[-7:]
    atm, ocean, depth, wet, kappa, air, atm_cell, dest, sea_cell, weight, wave_speed = held
    used = []

    def copy(source, target):
        used.append(pltpu.make_async_copy(source, target, sems.at[len(used)]))
        used[-1].start()

    def copy_either(parity, source, even, odd):
        choices = [pltpu.make_async_copy(source, target, sems.at[len(used)]) for target in (even, odd)]
        pl.when(parity == 0)(choices[0].start)
        pl.when(parity != 0)(choices[1].start)
        used.append(choices[0])

    column, line = column_parity(), tile_parity()
    for source, target in zip(sources, held):
        copy(source, target)
    levels = atm.shape[1]
    rows, cols = atm.shape[2:]
    tracers = ocean.shape[0] * ocean.shape[1]
    each = ocean.shape[1]
    obase, mbase, own, halo = row_slots(levels, tracers)
    slots, _ = lane_slots(levels, tracers)
    for one in used:
        one.wait()
    arrived = len(used)
    wetness = wet[...].astype(F32)

    lane = lax.broadcasted_iota(jnp.int32, (rows, cols), 1)
    fields = [(atm, (k, l), AH) for k in range(3) for l in range(levels)]
    fields += [(ocean, (i // each, i % each), OH) for i in range(tracers)]
    fields += [(depth, None, AH), (None, None, AH), (kappa, None, AH)]
    packed = {}
    for (ref, at, width), slot in zip(fields, slots):
        value = wetness if ref is None else (ref[...] if at is None else ref[at[0], at[1]])
        tile, offset = slot // cols, slot % cols
        mask = (lane >= offset) & (lane < offset + width)
        first = pltpu.roll(value, offset, 1) if offset else value
        turn = (offset + width) % cols
        last = pltpu.roll(value, turn, 1) if turn else value
        if tile in packed:
            a, b = packed[tile]
            packed[tile] = (jnp.where(mask, first, a), jnp.where(mask, last, b))
        else:
            packed[tile] = (first, last)
    for tile, (a, b) in packed.items():
        where = slice(tile * cols, (tile + 1) * cols)
        left[:, where] = a
        right[:, where] = b

    copy_either(column, right, cols_a, cols_b)
    copy_either(column, left, cols_b, cols_a)

    for level in range(levels):
        speed = wave_speed[level] * depth[...]
        both = near_rows(atm[0, level], atm[1, level], atm[2, level], speed, rows, cols)
        for ref, values in zip((up, down), both):
            for i, value in enumerate(values):
                at = i * levels + level
                ref[at : at + 1, :] = value
    at = own
    for strip in (left, right):
        for i in range(strip.shape[1] // cols):
            where = slice(i * cols, (i + 1) * cols)
            up[at : at + AH, :] = strip[0:AH, where]
            down[at : at + AH, :] = strip[rows - AH : rows, where]
            at += AH
    for i in range(tracers):
        at = obase + OH * i
        up[at : at + OH, :] = ocean[i // each, i % each, 0:OH, :]
        down[at : at + OH, :] = ocean[i // each, i % each, rows - OH : rows, :]
    for at, value, width in (
        (mbase, depth[...], AH),
        (mbase + AH, wetness, OH),
        (mbase + AH + OH, kappa[...], OH),
    ):
        up[at : at + width, :] = value[0:width]
        down[at : at + width, :] = value[rows - width : rows]
    copy_either(line, down, rows_a.at[0:halo], rows_b.at[0:halo])
    copy_either(line, up, rows_b.at[0:halo], rows_a.at[0:halo])

    cell = atm_cell[...]
    hot_atm = jnp.where(one_hot(cell % cols, cols), 1.0, 0.0).astype(BF16)
    airx = gather_rows(air[...], one_hot(cell // cols, rows), hot_atm)
    w = weight[...]
    wair = w * airx
    wair_buf[...] = wair
    copy(wair_buf, wair_out)
    cell = sea_cell[...]
    hot_sea = jnp.where(one_hot(cell % cols, cols), 1.0, 0.0).astype(BF16)
    row = dest[...] * rows + cell // cols
    tail = slice(halo, halo + 3 * rows)
    for shift in range(tiles):
        target = tile_at(shift, tiles)
        s1, s2 = scatter_rows([wair, w], one_hot(row - target * rows, rows), hot_sea)
        sums[shift, 0:rows, :] = s1
        sums[shift, rows : 2 * rows, :] = s2
        sums[shift, 2 * rows : 3 * rows, :] = ocean[0, 0]
        if len(sums_out) == 1:
            copy(sums.at[shift], sums_out[0].at[target])
        elif shift == 1:
            copy_either(line, sums.at[shift], rows_a.at[tail], rows_b.at[tail])
        elif shift == tiles - 1:
            copy_either(line, sums.at[shift], rows_b.at[tail], rows_a.at[tail])
        else:
            copy(sums.at[shift], sums_out[max(shift - 1, 0)])
    for one in used[arrived:]:
        one.wait()


def strips(cols, slot, width, left_part, right_part):
    low_half = lax.broadcasted_iota(jnp.int32, (1, cols), 1) < cols // 2
    offset = slot % cols
    a, b = right_part(slot // cols), left_part(slot // cols)
    if offset:
        a = pltpu.roll(a, cols - offset, 1)
    turn = (cols - width - offset) % cols
    if turn:
        b = pltpu.roll(b, turn, 1)
    return jnp.where(low_half, a, b)


def final_kernel(tiles, *refs):
    speed_in, atm_in, ocean_in, depth_in, kappa_in = refs[:5]
    kept = (len(refs) - 5 - 8 - 4) // 2
    sources, rest = refs[5 : 5 + kept], refs[5 + kept :]
    atm_out, ocean_out, speed, us, vs, hs, fs, ms = rest[:8]
    held, (edge, atm_buf, ocean_buf, sems) = rest[8 : 8 + kept], rest[8 + kept :]
    wet, atm_cell, dest, sea_cell, weight, wair, from_up, from_down, from_left, from_right, from_below, from_above = held[:12]
    messages = held[12:]
    levels = us.shape[0]
    each = ocean_out.shape[1]
    tracers = ocean_out.shape[0] * each
    rows, cols = atm_out.shape[2:]
    slots, lanes = lane_slots(levels, tracers)
    obase, mbase, own, halo = row_slots(levels, tracers)
    full = rows + 2 * AH
    block = (slice(None), slice(0, rows), slice(0, cols))
    rows_a, rows_b, cols_a, cols_b = sources[6:10]
    either = [(tile_parity(), rows_b, rows_a, from_up), (tile_parity(), rows_a, rows_b, from_down)]
    either += [(column_parity(), cols_b, cols_a, from_left), (column_parity(), cols_a, cols_b, from_right)]
    pairs = [pair for i, pair in enumerate(zip(sources, held)) if not 6 <= i < 10] + [(speed_in, speed)]
    pairs += [(atm_in.at[i], ref.at[block]) for i, ref in enumerate((us, vs, hs))]
    pairs += [(ocean_in.at[i], fs.at[(i, *block)]) for i in range(ocean_out.shape[0])]
    pairs += [(ref, ms.at[(i, *block[1:])]) for i, ref in ((0, depth_in), (2, kappa_in))]
    copies = [pltpu.make_async_copy(source, target, sems.at[i]) for i, (source, target) in enumerate(pairs)]
    for copy in copies:
        copy.start()
    for parity, even, odd, target in either:
        choices = [pltpu.make_async_copy(source, target, sems.at[len(copies)]) for source in (even, odd)]
        pl.when(parity == 0)(choices[0].start)
        pl.when(parity != 0)(choices[1].start)
        copies.append(choices[0])
    for copy in copies:
        copy.wait()
    corner_a, corner_b = from_below, from_above
    even_line, even_column = tile_parity() == 0, column_parity() == 0

    def message(shift, part):
        where = slice(part * rows, (part + 1) * rows)
        if len(messages) == 1:
            return messages[0][tile_at(-shift, tiles), where, :]
        if shift in (1, tiles - 1):
            return (from_up if shift == 1 else from_down)[halo + part * rows : halo + (part + 1) * rows, :]
        return messages[max(shift - 1, 0)][where, :]

    surface = fs[0, 0, 0:rows, 0:cols]
    cell = sea_cell[...]
    hot_sea = jnp.where(one_hot(cell % cols, cols), 1.0, 0.0).astype(BF16)
    row = dest[...] * rows + cell // cols
    s1, s2 = message(0, 0), message(0, 1)
    sstx = jnp.zeros(cell.shape, F32)
    for shift in range(tiles):
        if shift:
            s1 = s1 + message(shift, 0)
            s2 = s2 + message(shift, 1)
        sstx = sstx + gather_rows(message(shift, 2), one_hot(row - tile_at(-shift, tiles) * rows, rows), hot_sea)
    sea_flux = s1 - surface * s2
    flux = wair[...] - weight[...] * sstx
    cell = atm_cell[...]
    hot_atm = jnp.where(one_hot(cell % cols, cols), 1.0, 0.0).astype(BF16)
    (atm_flux,) = scatter_rows([flux], one_hot(cell // cols, rows), hot_atm)

    half = lanes // cols
    for i in range(2 * half):
        where = slice(i % half * cols, (i % half + 1) * cols)
        first, second = (slice(AH, 2 * AH), slice(0, AH)) if i < half else (slice(0, AH), slice(AH, 2 * AH))
        a = jnp.where(even_column, corner_a[first, where], corner_a[second, where])
        b = jnp.where(even_column, corner_b[first, where], corner_b[second, where])
        edge[i, 0:AH, :] = jnp.where(even_line, a, b)
        edge[i, AH : 2 * AH, :] = jnp.where(even_line, b, a)
        at = own + AH * i
        edge[2 * half + i, 0:AH, :] = from_down[at : at + AH, :]
        edge[2 * half + i, AH : 2 * AH, :] = from_up[at : at + AH, :]

    def extend(view, field, width):
        slot = slots[field]
        view[0:rows, cols : 2 * cols] = strips(
            cols,
            slot,
            width,
            lambda t: from_left[:, t * cols : (t + 1) * cols],
            lambda t: from_right[:, t * cols : (t + 1) * cols],
        )
        view[rows:full, cols : 2 * cols] = strips(cols, slot, width, lambda t: edge[t], lambda t: edge[half + t])

    def extend_rows(view, at, high):
        view[rows : rows + high, 0:cols] = from_down[at : at + high, :]
        view[full - high : full, 0:cols] = from_up[at : at + high, :]

    lane = lax.broadcasted_iota(jnp.int32, (2 * AH, cols), 1)
    line = lax.broadcasted_iota(jnp.int32, (2 * AH, cols), 0)
    whole_strip = (lane < AH) | (lane >= cols - AH)
    outer = (lane < AH - 1) | (lane > cols - AH)

    def near(which, level):
        at = which * levels + level
        return from_down[at : at + 1, :], from_up[at : at + 1, :]

    def extend_level(view, which, level):
        strip = strips(cols, slots[which * levels + level], AH, lambda t: edge[3 * half + t], lambda t: edge[2 * half + t])
        below, above = near(which, level)
        inner = jnp.where(line == 0, below, jnp.where(line == 2 * AH - 1, above, 0.0))
        view[rows:full, 0:cols] = jnp.where(whole_strip if which == 0 else outer, strip, inner)

    def new_height_rows(tile, level):
        below, above = near(3, level), near(4, level)
        sent = jnp.where(
            line == 1, below[0], jnp.where(line == 2, above[0], jnp.where(line == 2 * AH - 3, above[1], below[1]))
        )
        here = (line == 1) | (line == 2) | (line == 2 * AH - 3) | (line == 2 * AH - 2)
        return jnp.where(here & jnp.logical_not(outer), sent, tile)

    def east(f):
        return pltpu.roll(f, 2 * cols - 1, 1)

    def west(f):
        return pltpu.roll(f, 1, 1)

    def south(f):
        return pltpu.roll(f, full - 1, 0)

    def north(f):
        return pltpu.roll(f, 1, 0)

    base = 3 * levels + tracers
    ms[1, 0:rows, 0:cols] = wet[...].astype(F32)
    for i, (at, high) in enumerate(((mbase, AH), (mbase + AH, OH), (mbase + AH + OH, OH))):
        extend(ms.at[i], base + i, AH)
        extend_rows(ms.at[i], at, high)
    for i in range(tracers):
        extend(fs.at[i // each, i % each], 3 * levels + i, OH)
        extend_rows(fs.at[i // each, i % each], obase + OH * i, OH)
    for level in range(levels):
        for which, ref in enumerate((us, vs, hs)):
            extend(ref.at[level], which * levels + level, AH)
            extend_level(ref.at[level], which, level)

    w = ms[1]
    k = ms[2]
    we, ww, ws, wn = east(w), west(w), south(w), north(w)
    for step in range(OCEAN_STEPS):
        for i in range(tracers):
            f = fs[i // each, i % each]
            total = we * (east(f) - f)
            total = total + ww * (west(f) - f)
            total = total + ws * (south(f) - f)
            total = total + wn * (north(f) - f)
            f = f + k * (w * total)
            if step < OCEAN_STEPS - 1:
                fs[i // each, i % each] = f
            else:
                f = f[0:rows, 0:cols]
                ocean_buf[i // each, i % each] = f + SEA_GAIN * sea_flux if i == 0 else f
    used = len(copies)
    copies = [pltpu.make_async_copy(ocean_buf, ocean_out, sems.at[used])]
    copies[0].start()

    d = ms[0]
    chunk = max(1, levels // 4)
    for step in range(ACOUSTIC):
        for level in range(levels):
            u, v, h = us[level], vs[level], hs[level]
            column_speed = speed[level] * d
            hs[level] = h - column_speed * ((east(u) - west(u)) * 0.5 + (south(v) - north(v)) * 0.5)
            if step == 0:
                hs[level, rows:full, 0:cols] = new_height_rows(hs[level, rows:full, 0:cols], level)
        for level in range(levels):
            u, v, h = us[level], vs[level], hs[level]
            u = u - (east(h) - west(h)) * 0.5
            v = v - (south(h) - north(h)) * 0.5
            if step < ACOUSTIC - 1:
                us[level], vs[level] = u, v
            else:
                h = h[0:rows, 0:cols]
                atm_buf[0, level] = u[0:rows, 0:cols]
                atm_buf[1, level] = v[0:rows, 0:cols]
                atm_buf[2, level] = h - ATM_GAIN * atm_flux if level == levels - 1 else h
                if (level + 1) % chunk == 0:
                    where = pl.ds(level + 1 - chunk, chunk)
                    copies.append(
                        pltpu.make_async_copy(
                            atm_buf.at[:, where], atm_out.at[:, where], sems.at[used + len(copies)]
                        )
                    )
                    copies[-1].start()
    for copy in copies:
        copy.wait()


def on_device(
    tile_count,
    atm_state,
    air_temp,
    depth,
    wave_speed,
    ocean_state,
    wet_mask,
    diffusivity,
    xg_atm_cell,
    xg_dest,
    xg_ocean_cell,
    xg_weight,
):
    levels = atm_state.shape[1]
    rows, cols = atm_state.shape[2:]
    tracers = ocean_state.shape[0] * ocean_state.shape[1]
    cells = xg_weight.shape[-1]
    _, lanes = lane_slots(levels, tracers)
    _, _, _, halo = row_slots(levels, tracers)
    message_rows = halo
    vmem = pl.BlockSpec(memory_space=pltpu.VMEM)
    hbm = pl.BlockSpec(memory_space=pltpu.HBM)
    whole = pltpu.CompilerParams(vmem_limit_bytes=64 * 1024 * 1024)
    full = rows + 2 * AH

    def shape(*dims):
        return jax.ShapeDtypeStruct(dims, F32)

    by_shift = tile_count <= 4
    if by_shift:
        message_rows += 3 * rows
        sums = [shape(3 * rows, cols)] * (tile_count - 2)
    else:
        sums = [shape(tile_count, 3 * rows, cols)]
    atm_cell = xg_atm_cell.reshape(1, cells)
    dest = xg_dest.reshape(1, cells)
    sea_cell = xg_ocean_cell.reshape(1, cells)
    weight = xg_weight.reshape(1, cells)
    operands = (atm_state, ocean_state, depth, wet_mask, diffusivity, air_temp, atm_cell, dest, sea_cell, weight)
    operands += (wave_speed,)
    cols_a, cols_b, rows_a, rows_b, wair, *messages = pl.pallas_call(
        functools.partial(first_kernel, tile_count),
        out_shape=[shape(rows, lanes)] * 2 + [shape(message_rows, cols)] * 2 + [shape(1, cells)] + sums,
        in_specs=[hbm] * 11,
        out_specs=[hbm] * (5 + len(sums)),
        scratch_shapes=[pltpu.VMEM(x.shape, x.dtype) for x in operands[:-1]]
        + [pltpu.SMEM(wave_speed.shape, F32)]
        + [pltpu.VMEM((halo, cols), F32)] * 2
        + [pltpu.VMEM((rows, lanes), F32)] * 2
        + [
            pltpu.VMEM((1, cells), F32),
            pltpu.VMEM((tile_count, 3 * rows, cols), F32),
            pltpu.SemaphoreType.DMA((16 + tile_count,)),
        ],
        compiler_params=whole,
        name="first",
    )(*operands)

    column_axes = ("sub", "comp")
    column_count = lax.axis_size("sub") * lax.axis_size("comp")

    def shift(value, axes, count, by):
        return lax.ppermute(value, axes, [(i, (i + by) % count) for i in range(count)])

    def swap(value, axes, count, odd):
        return lax.ppermute(value, axes, [(i, (i + (1 if (i + odd) % 2 == 0 else -1)) % count) for i in range(count)])

    got_a = swap(cols_a, column_axes, column_count, 0)
    got_b = swap(cols_b, column_axes, column_count, 1)
    near_a = swap(rows_a, "tile", tile_count, 0)
    near_b = swap(rows_b, "tile", tile_count, 1)

    low = jnp.where(tile_parity() == 0, rows - AH, 0)
    corner_a, corner_b = [
        jnp.concatenate([lax.dynamic_slice_in_dim(x, at, AH) for x in (got_a, got_b)]) for at in (low, rows - AH - low)
    ]
    corner_a = swap(corner_a, "tile", tile_count, 0)
    corner_b = swap(corner_b, "tile", tile_count, 1)
    if by_shift:
        *messages, got_b = lax.optimization_barrier((*messages, got_b))
        got = messages[:1] + [shift(messages[s - 1], "tile", tile_count, s) for s in range(2, tile_count - 1)]
    else:
        got = [lax.all_to_all(messages[0], "tile", split_axis=0, concat_axis=0, tiled=True)]

    operands = (wave_speed, atm_state, ocean_state, depth, diffusivity)
    operands += (wet_mask, atm_cell, dest, sea_cell, weight, wair, near_a, near_b, got_a, got_b)
    operands += (corner_a, corner_b, *got)
    return tuple(
        pl.pallas_call(
            functools.partial(final_kernel, tile_count),
            out_shape=[shape(*atm_state.shape), shape(*ocean_state.shape)],
            in_specs=[hbm] * len(operands),
            out_specs=[hbm] * 2,
            scratch_shapes=[pltpu.SMEM(wave_speed.shape, F32)]
            + [pltpu.VMEM((levels, full, 2 * cols), F32)] * 3
            + [
                pltpu.VMEM((*ocean_state.shape[:2], full, 2 * cols), F32),
                pltpu.VMEM((3, full, 2 * cols), F32),
            ]
            + [pltpu.VMEM(x.shape, x.dtype) for x in operands[5:]]
            + [
                pltpu.VMEM((4 * (lanes // cols), 2 * AH, cols), F32),
                pltpu.VMEM(atm_state.shape, F32),
                pltpu.VMEM(ocean_state.shape, F32),
                pltpu.SemaphoreType.DMA((len(operands) + 10,)),
            ],
            compiler_params=whole,
            name="steps",
        )(*operands)
    )


def solution(mesh):
    grid = P(("member", "tile"), ("sub", "comp"))
    state = P(None, None, ("member", "tile"), ("sub", "comp"))
    cells = P(("member", "tile"), ("sub", "comp"), None)
    return jax.shard_map(
        functools.partial(on_device, mesh.shape["tile"]),
        mesh=mesh,
        in_specs=(
            state,
            grid,
            grid,
            P(),
            state,
            grid,
            grid,
            cells,
            P(("member", "tile"), ("sub", "comp"), None, None),
            cells,
            cells,
        ),
        out_specs=(state, state),
        check_vma=False,
    )
```

```python
import functools

import jax
import jax.numpy as jnp
from jax import lax
from jax.experimental import pallas as pl
from jax.experimental.pallas import tpu as pltpu
from jax.sharding import PartitionSpec as P

ACOUSTIC = 2
OCEAN_STEPS = 2
AH = 2 * ACOUSTIC
OH = OCEAN_STEPS

ATM_GAIN = 0.5
SEA_GAIN = 0.5

F32 = jnp.float32
BF16 = jnp.bfloat16


def lane_slots(levels, tracers):
    slots = [AH * i for i in range(3 * levels)]
    base = AH * 3 * levels
    slots += [base + OH * i for i in range(tracers)]
    base += OH * tracers
    slots += [base + AH * i for i in range(3)]
    total = base + 3 * AH
    return slots, -(-total // 128) * 128


def row_slots(levels, tracers):
    tracer = 5 * levels
    misc = tracer + OH * tracers
    own = misc + AH + 2 * OH
    _, lanes = lane_slots(levels, tracers)
    return tracer, misc, own, own + 2 * AH * (lanes // 128)


def near_rows(u, v, h, speed, rows, cols):
    east_west = (pltpu.roll(u, cols - 1, 1) - pltpu.roll(u, 1, 1)) * 0.5
    south_north = (pltpu.roll(v, rows - 1, 0) - pltpu.roll(v, 1, 0)) * 0.5
    h1 = h - speed * (east_west + south_north)
    out = []
    for near, turn in ((0, 1), (rows - 1, -1)):
        at = [slice(near + turn * i, near + turn * i + 1) for i in range(3)]
        out.append(
            (
                u[at[0]],
                v[at[0]],
                h[at[0]] - (0.5 * turn) * speed[at[0]] * v[at[1]],
                h1[at[1]],
                h1[at[2]] - (2.0 * turn) * v[at[1]],
            )
        )
    return out


def split3(value):
    hi = value.astype(BF16)
    rest = value - hi.astype(F32)
    mid = rest.astype(BF16)
    low = (rest - mid.astype(F32)).astype(BF16)
    return hi, mid, low


def one_hot(index, size):
    shape = (size, index.shape[-1])
    return lax.broadcasted_iota(jnp.int32, shape, 0) == index


def gather_rows(table, hot_rows, hot_cols):
    r = table.shape[0]
    parts = jnp.concatenate(split3(table), axis=0)
    g = jnp.dot(parts, hot_cols, preferred_element_type=F32)
    g = g[0:r] + g[r : 2 * r] + g[2 * r : 3 * r]
    return jnp.sum(jnp.where(hot_rows, g, 0.0), axis=0, keepdims=True)


def scatter_rows(values, hot_rows, hot_cols):
    r = hot_rows.shape[0]
    parts = []
    for value in values:
        for part in split3(value):
            parts.append(jnp.where(hot_rows, part.astype(F32), 0.0).astype(BF16))
    s = lax.dot_general(
        jnp.concatenate(parts, axis=0),
        hot_cols,
        (((1,), (1,)), ((), ())),
        preferred_element_type=F32,
    )
    out = []
    for i in range(len(values)):
        base = 3 * r * i
        out.append(s[base : base + r] + s[base + r : base + 2 * r] + s[base + 2 * r : base + 3 * r])
    return out


def tile_at(shift, tiles):
    return lax.rem(lax.axis_index("tile") + shift % tiles, tiles)


def tile_parity():
    return lax.rem(lax.axis_index("tile") + 1, 2)


def column_parity():
    return lax.rem(lax.axis_index(("sub", "comp")), 2)


def first_kernel(tiles, *refs):
    sources, (cols_a, cols_b, rows_a, rows_b, wair_out, *sums_out) = refs[:11], refs[11:-18]
    held, (up, down, left, right, wair_buf, sums, sems) = refs[-18:-7], refs[-7:]
    atm, ocean, depth, wet, kappa, air, atm_cell, dest, sea_cell, weight, wave_speed = held
    used = []

    def copy(source, target):
        used.append(pltpu.make_async_copy(source, target, sems.at[len(used)]))
        used[-1].start()

    def copy_either(parity, source, even, odd):
        choices = [pltpu.make_async_copy(source, target, sems.at[len(used)]) for target in (even, odd)]
        pl.when(parity == 0)(choices[0].start)
        pl.when(parity != 0)(choices[1].start)
        used.append(choices[0])

    column, line = column_parity(), tile_parity()
    for source, target in zip(sources, held):
        copy(source, target)
    levels = atm.shape[1]
    rows, cols = atm.shape[2:]
    tracers = ocean.shape[0] * ocean.shape[1]
    each = ocean.shape[1]
    obase, mbase, own, halo = row_slots(levels, tracers)
    slots, _ = lane_slots(levels, tracers)
    for one in used:
        one.wait()
    arrived = len(used)
    wetness = wet[...].astype(F32)

    lane = lax.broadcasted_iota(jnp.int32, (rows, cols), 1)
    fields = [(atm, (k, l), AH) for k in range(3) for l in range(levels)]
    fields += [(ocean, (i // each, i % each), OH) for i in range(tracers)]
    fields += [(depth, None, AH), (None, None, AH), (kappa, None, AH)]
    packed = {}
    for (ref, at, width), slot in zip(fields, slots):
        value = wetness if ref is None else (ref[...] if at is None else ref[at[0], at[1]])
        tile, offset = slot // cols, slot % cols
        mask = (lane >= offset) & (lane < offset + width)
        first = pltpu.roll(value, offset, 1) if offset else value
        turn = (offset + width) % cols
        last = pltpu.roll(value, turn, 1) if turn else value
        if tile in packed:
            a, b = packed[tile]
            packed[tile] = (jnp.where(mask, first, a), jnp.where(mask, last, b))
        else:
            packed[tile] = (first, last)
    for tile, (a, b) in packed.items():
        where = slice(tile * cols, (tile + 1) * cols)
        left[:, where] = a
        right[:, where] = b

    copy_either(column, right, cols_a, cols_b)
    copy_either(column, left, cols_b, cols_a)

    for level in range(levels):
        speed = wave_speed[level] * depth[...]
        both = near_rows(atm[0, level], atm[1, level], atm[2, level], speed, rows, cols)
        for ref, values in zip((up, down), both):
            for i, value in enumerate(values):
                at = i * levels + level
                ref[at : at + 1, :] = value
    at = own
    for strip in (left, right):
        for i in range(strip.shape[1] // cols):
            where = slice(i * cols, (i + 1) * cols)
            up[at : at + AH, :] = strip[0:AH, where]
            down[at : at + AH, :] = strip[rows - AH : rows, where]
            at += AH
    for i in range(tracers):
        at = obase + OH * i
        up[at : at + OH, :] = ocean[i // each, i % each, 0:OH, :]
        down[at : at + OH, :] = ocean[i // each, i % each, rows - OH : rows, :]
    for at, value, width in (
        (mbase, depth[...], AH),
        (mbase + AH, wetness, OH),
        (mbase + AH + OH, kappa[...], OH),
    ):
        up[at : at + width, :] = value[0:width]
        down[at : at + width, :] = value[rows - width : rows]
    copy_either(line, down, rows_a.at[0:halo], rows_b.at[0:halo])
    copy_either(line, up, rows_b.at[0:halo], rows_a.at[0:halo])

    cell = atm_cell[...]
    hot_atm = jnp.where(one_hot(cell % cols, cols), 1.0, 0.0).astype(BF16)
    airx = gather_rows(air[...], one_hot(cell // cols, rows), hot_atm)
    w = weight[...]
    wair = w * airx
    wair_buf[...] = wair
    copy(wair_buf, wair_out)
    cell = sea_cell[...]
    hot_sea = jnp.where(one_hot(cell % cols, cols), 1.0, 0.0).astype(BF16)
    row = dest[...] * rows + cell // cols
    tail = slice(halo, halo + 3 * rows)
    for shift in range(tiles):
        target = tile_at(shift, tiles)
        s1, s2 = scatter_rows([wair, w], one_hot(row - target * rows, rows), hot_sea)
        sums[shift, 0:rows, :] = s1
        sums[shift, rows : 2 * rows, :] = s2
        sums[shift, 2 * rows : 3 * rows, :] = ocean[0, 0]
        if len(sums_out) == 1:
            copy(sums.at[shift], sums_out[0].at[target])
        elif shift == 1:
            copy_either(line, sums.at[shift], rows_a.at[tail], rows_b.at[tail])
        elif shift == tiles - 1:
            copy_either(line, sums.at[shift], rows_b.at[tail], rows_a.at[tail])
        else:
            copy(sums.at[shift], sums_out[max(shift - 1, 0)])
    for one in used[arrived:]:
        one.wait()


def strips(cols, slot, width, left_part, right_part):
    low_half = lax.broadcasted_iota(jnp.int32, (1, cols), 1) < cols // 2
    offset = slot % cols
    a, b = right_part(slot // cols), left_part(slot // cols)
    if offset:
        a = pltpu.roll(a, cols - offset, 1)
    turn = (cols - width - offset) % cols
    if turn:
        b = pltpu.roll(b, turn, 1)
    return jnp.where(low_half, a, b)


def final_kernel(tiles, *refs):
    speed_in, atm_in, ocean_in, depth_in, kappa_in = refs[:5]
    kept = (len(refs) - 5 - 8 - 4) // 2
    sources, rest = refs[5 : 5 + kept], refs[5 + kept :]
    atm_out, ocean_out, speed, us, vs, hs, fs, ms = rest[:8]
    held, (edge, atm_buf, ocean_buf, sems) = rest[8 : 8 + kept], rest[8 + kept :]
    wet, atm_cell, dest, sea_cell, weight, wair, from_up, from_down, from_left, from_right, from_below, from_above = held[:12]
    messages = held[12:]
    levels = us.shape[0]
    each = ocean_out.shape[1]
    tracers = ocean_out.shape[0] * each
    rows, cols = atm_out.shape[2:]
    slots, lanes = lane_slots(levels, tracers)
    obase, mbase, own, halo = row_slots(levels, tracers)
    full = rows + 2 * AH
    block = (slice(None), slice(0, rows), slice(0, cols))
    rows_a, rows_b, cols_a, cols_b = sources[6:10]
    either = [(tile_parity(), rows_b, rows_a, from_up), (tile_parity(), rows_a, rows_b, from_down)]
    either += [(column_parity(), cols_b, cols_a, from_left), (column_parity(), cols_a, cols_b, from_right)]
    pairs = [pair for i, pair in enumerate(zip(sources, held)) if not 6 <= i < 10] + [(speed_in, speed)]
    pairs += [(atm_in.at[i], ref.at[block]) for i, ref in enumerate((us, vs, hs))]
    pairs += [(ocean_in.at[i], fs.at[(i, *block)]) for i in range(ocean_out.shape[0])]
    pairs += [(ref, ms.at[(i, *block[1:])]) for i, ref in ((0, depth_in), (2, kappa_in))]
    copies = [pltpu.make_async_copy(source, target, sems.at[i]) for i, (source, target) in enumerate(pairs)]
    for copy in copies:
        copy.start()
    for parity, even, odd, target in either:
        choices = [pltpu.make_async_copy(source, target, sems.at[len(copies)]) for source in (even, odd)]
        pl.when(parity == 0)(choices[0].start)
        pl.when(parity != 0)(choices[1].start)
        copies.append(choices[0])
    for copy in copies:
        copy.wait()
    corner_a, corner_b = from_below, from_above
    even_line, even_column = tile_parity() == 0, column_parity() == 0

    def message(shift, part):
        where = slice(part * rows, (part + 1) * rows)
        if len(messages) == 1:
            return messages[0][tile_at(-shift, tiles), where, :]
        if shift in (1, tiles - 1):
            return (from_up if shift == 1 else from_down)[halo + part * rows : halo + (part + 1) * rows, :]
        return messages[max(shift - 1, 0)][where, :]

    surface = fs[0, 0, 0:rows, 0:cols]
    cell = sea_cell[...]
    hot_sea = jnp.where(one_hot(cell % cols, cols), 1.0, 0.0).astype(BF16)
    row = dest[...] * rows + cell // cols
    s1, s2 = message(0, 0), message(0, 1)
    sstx = jnp.zeros(cell.shape, F32)
    for shift in range(tiles):
        if shift:
            s1 = s1 + message(shift, 0)
            s2 = s2 + message(shift, 1)
        sstx = sstx + gather_rows(message(shift, 2), one_hot(row - tile_at(-shift, tiles) * rows, rows), hot_sea)
    sea_flux = s1 - surface * s2
    flux = wair[...] - weight[...] * sstx
    cell = atm_cell[...]
    hot_atm = jnp.where(one_hot(cell % cols, cols), 1.0, 0.0).astype(BF16)
    (atm_flux,) = scatter_rows([flux], one_hot(cell // cols, rows), hot_atm)

    half = lanes // cols
    for i in range(2 * half):
        where = slice(i % half * cols, (i % half + 1) * cols)
        first, second = (slice(AH, 2 * AH), slice(0, AH)) if i < half else (slice(0, AH), slice(AH, 2 * AH))
        a = jnp.where(even_column, corner_a[first, where], corner_a[second, where])
        b = jnp.where(even_column, corner_b[first, where], corner_b[second, where])
        edge[i, 0:AH, :] = jnp.where(even_line, a, b)
        edge[i, AH : 2 * AH, :] = jnp.where(even_line, b, a)
        at = own + AH * i
        edge[2 * half + i, 0:AH, :] = from_down[at : at + AH, :]
        edge[2 * half + i, AH : 2 * AH, :] = from_up[at : at + AH, :]

    def extend(view, field, width):
        slot = slots[field]
        view[0:rows, cols : 2 * cols] = strips(
            cols,
            slot,
            width,
            lambda t: from_left[:, t * cols : (t + 1) * cols],
            lambda t: from_right[:, t * cols : (t + 1) * cols],
        )
        view[rows:full, cols : 2 * cols] = strips(cols, slot, width, lambda t: edge[t], lambda t: edge[half + t])

    def extend_rows(view, at, high):
        view[rows : rows + high, 0:cols] = from_down[at : at + high, :]
        view[full - high : full, 0:cols] = from_up[at : at + high, :]

    lane = lax.broadcasted_iota(jnp.int32, (2 * AH, cols), 1)
    line = lax.broadcasted_iota(jnp.int32, (2 * AH, cols), 0)
    whole_strip = (lane < AH) | (lane >= cols - AH)
    outer = (lane < AH - 1) | (lane > cols - AH)

    def near(which, level):
        at = which * levels + level
        return from_down[at : at + 1, :], from_up[at : at + 1, :]

    def extend_level(view, which, level):
        strip = strips(cols, slots[which * levels + level], AH, lambda t: edge[3 * half + t], lambda t: edge[2 * half + t])
        below, above = near(which, level)
        inner = jnp.where(line == 0, below, jnp.where(line == 2 * AH - 1, above, 0.0))
        view[rows:full, 0:cols] = jnp.where(whole_strip if which == 0 else outer, strip, inner)

    def new_height_rows(tile, level):
        below, above = near(3, level), near(4, level)
        sent = jnp.where(
            line == 1, below[0], jnp.where(line == 2, above[0], jnp.where(line == 2 * AH - 3, above[1], below[1]))
        )
        here = (line == 1) | (line == 2) | (line == 2 * AH - 3) | (line == 2 * AH - 2)
        return jnp.where(here & jnp.logical_not(outer), sent, tile)

    def east(f):
        return pltpu.roll(f, 2 * cols - 1, 1)

    def west(f):
        return pltpu.roll(f, 1, 1)

    def south(f):
        return pltpu.roll(f, full - 1, 0)

    def north(f):
        return pltpu.roll(f, 1, 0)

    base = 3 * levels + tracers
    ms[1, 0:rows, 0:cols] = wet[...].astype(F32)
    for i, (at, high) in enumerate(((mbase, AH), (mbase + AH, OH), (mbase + AH + OH, OH))):
        extend(ms.at[i], base + i, AH)
        extend_rows(ms.at[i], at, high)
    for i in range(tracers):
        extend(fs.at[i // each, i % each], 3 * levels + i, OH)
        extend_rows(fs.at[i // each, i % each], obase + OH * i, OH)
    for level in range(levels):
        for which, ref in enumerate((us, vs, hs)):
            extend(ref.at[level], which * levels + level, AH)
            extend_level(ref.at[level], which, level)

    w = ms[1]
    k = ms[2]
    we, ww, ws, wn = east(w), west(w), south(w), north(w)
    for step in range(OCEAN_STEPS):
        for i in range(tracers):
            f = fs[i // each, i % each]
            total = we * (east(f) - f)
            total = total + ww * (west(f) - f)
            total = total + ws * (south(f) - f)
            total = total + wn * (north(f) - f)
            f = f + k * (w * total)
            if step < OCEAN_STEPS - 1:
                fs[i // each, i % each] = f
            else:
                f = f[0:rows, 0:cols]
                ocean_buf[i // each, i % each] = f + SEA_GAIN * sea_flux if i == 0 else f
    used = len(copies)
    copies = [pltpu.make_async_copy(ocean_buf, ocean_out, sems.at[used])]
    copies[0].start()

    d = ms[0]
    chunk = max(1, levels // 4)
    for step in range(ACOUSTIC):
        for level in range(levels):
            u, v, h = us[level], vs[level], hs[level]
            column_speed = speed[level] * d
            hs[level] = h - column_speed * ((east(u) - west(u)) * 0.5 + (south(v) - north(v)) * 0.5)
            if step == 0:
                hs[level, rows:full, 0:cols] = new_height_rows(hs[level, rows:full, 0:cols], level)
        for level in range(levels):
            u, v, h = us[level], vs[level], hs[level]
            u = u - (east(h) - west(h)) * 0.5
            v = v - (south(h) - north(h)) * 0.5
            if step < ACOUSTIC - 1:
                us[level], vs[level] = u, v
            else:
                h = h[0:rows, 0:cols]
                atm_buf[0, level] = u[0:rows, 0:cols]
                atm_buf[1, level] = v[0:rows, 0:cols]
                atm_buf[2, level] = h - ATM_GAIN * atm_flux if level == levels - 1 else h
                if (level + 1) % chunk == 0:
                    where = pl.ds(level + 1 - chunk, chunk)
                    copies.append(
                        pltpu.make_async_copy(
                            atm_buf.at[:, where], atm_out.at[:, where], sems.at[used + len(copies)]
                        )
                    )
                    copies[-1].start()
    for copy in copies:
        copy.wait()


def on_device(
    tile_count,
    atm_state,
    air_temp,
    depth,
    wave_speed,
    ocean_state,
    wet_mask,
    diffusivity,
    xg_atm_cell,
    xg_dest,
    xg_ocean_cell,
    xg_weight,
):
    levels = atm_state.shape[1]
    rows, cols = atm_state.shape[2:]
    tracers = ocean_state.shape[0] * ocean_state.shape[1]
    cells = xg_weight.shape[-1]
    _, lanes = lane_slots(levels, tracers)
    _, _, _, halo = row_slots(levels, tracers)
    message_rows = halo
    vmem = pl.BlockSpec(memory_space=pltpu.VMEM)
    hbm = pl.BlockSpec(memory_space=pltpu.HBM)
    whole = pltpu.CompilerParams(vmem_limit_bytes=64 * 1024 * 1024)
    full = rows + 2 * AH

    def shape(*dims):
        return jax.ShapeDtypeStruct(dims, F32)

    by_shift = tile_count <= 4
    if by_shift:
        message_rows += 3 * rows
        sums = [shape(3 * rows, cols)] * (tile_count - 2)
    else:
        sums = [shape(tile_count, 3 * rows, cols)]
    atm_cell = xg_atm_cell.reshape(1, cells)
    dest = xg_dest.reshape(1, cells)
    sea_cell = xg_ocean_cell.reshape(1, cells)
    weight = xg_weight.reshape(1, cells)
    operands = (atm_state, ocean_state, depth, wet_mask, diffusivity, air_temp, atm_cell, dest, sea_cell, weight)
    operands += (wave_speed,)
    cols_a, cols_b, rows_a, rows_b, wair, *messages = pl.pallas_call(
        functools.partial(first_kernel, tile_count),
        out_shape=[shape(rows, lanes)] * 2 + [shape(message_rows, cols)] * 2 + [shape(1, cells)] + sums,
        in_specs=[hbm] * 11,
        out_specs=[hbm] * (5 + len(sums)),
        scratch_shapes=[pltpu.VMEM(x.shape, x.dtype) for x in operands[:-1]]
        + [pltpu.SMEM(wave_speed.shape, F32)]
        + [pltpu.VMEM((halo, cols), F32)] * 2
        + [pltpu.VMEM((rows, lanes), F32)] * 2
        + [
            pltpu.VMEM((1, cells), F32),
            pltpu.VMEM((tile_count, 3 * rows, cols), F32),
            pltpu.SemaphoreType.DMA((16 + tile_count,)),
        ],
        compiler_params=whole,
        name="first",
    )(*operands)

    column_axes = ("sub", "comp")
    column_count = lax.axis_size("sub") * lax.axis_size("comp")

    def shift(value, axes, count, by):
        return lax.ppermute(value, axes, [(i, (i + by) % count) for i in range(count)])

    def swap(value, axes, count, odd):
        return lax.ppermute(value, axes, [(i, (i + (1 if (i + odd) % 2 == 0 else -1)) % count) for i in range(count)])

    got_a = swap(cols_a, column_axes, column_count, 0)
    got_b = swap(cols_b, column_axes, column_count, 1)
    near_a = swap(rows_a, "tile", tile_count, 1)
    near_b = swap(rows_b, "tile", tile_count, 0)

    low = jnp.where(tile_parity() == 0, rows - AH, 0)
    corner_a, corner_b = [
        jnp.concatenate([lax.dynamic_slice_in_dim(x, at, AH) for x in (got_a, got_b)]) for at in (low, rows - AH - low)
    ]
    corner_a = swap(corner_a, "tile", tile_count, 1)
    corner_b = swap(corner_b, "tile", tile_count, 0)
    if by_shift:
        *messages, got_b = lax.optimization_barrier((*messages, got_b))
        got = messages[:1] + [shift(messages[s - 1], "tile", tile_count, s) for s in range(2, tile_count - 1)]
    else:
        got = [lax.all_to_all(messages[0], "tile", split_axis=0, concat_axis=0, tiled=True)]

    operands = (wave_speed, atm_state, ocean_state, depth, diffusivity)
    operands += (wet_mask, atm_cell, dest, sea_cell, weight, wair, near_a, near_b, got_a, got_b)
    operands += (corner_a, corner_b, *got)
    return tuple(
        pl.pallas_call(
            functools.partial(final_kernel, tile_count),
            out_shape=[shape(*atm_state.shape), shape(*ocean_state.shape)],
            in_specs=[hbm] * len(operands),
            out_specs=[hbm] * 2,
            scratch_shapes=[pltpu.SMEM(wave_speed.shape, F32)]
            + [pltpu.VMEM((levels, full, 2 * cols), F32)] * 3
            + [
                pltpu.VMEM((*ocean_state.shape[:2], full, 2 * cols), F32),
                pltpu.VMEM((3, full, 2 * cols), F32),
            ]
            + [pltpu.VMEM(x.shape, x.dtype) for x in operands[5:]]
            + [
                pltpu.VMEM((4 * (lanes // cols), 2 * AH, cols), F32),
                pltpu.VMEM(atm_state.shape, F32),
                pltpu.VMEM(ocean_state.shape, F32),
                pltpu.SemaphoreType.DMA((len(operands) + 10,)),
            ],
            compiler_params=whole,
            name="steps",
        )(*operands)
    )


def solution(mesh):
    grid = P(("member", "tile"), ("sub", "comp"))
    state = P(None, None, ("member", "tile"), ("sub", "comp"))
    cells = P(("member", "tile"), ("sub", "comp"), None)
    return jax.shard_map(
        functools.partial(on_device, mesh.shape["tile"]),
        mesh=mesh,
        in_specs=(
            state,
            grid,
            grid,
            P(),
            state,
            grid,
            grid,
            cells,
            P(("member", "tile"), ("sub", "comp"), None, None),
            cells,
            cells,
        ),
        out_specs=(state, state),
        check_vma=False,
    )
```

```python
import functools

import jax
import jax.numpy as jnp
from jax import lax
from jax.experimental import pallas as pl
from jax.experimental.pallas import tpu as pltpu
from jax.sharding import PartitionSpec as P

ACOUSTIC = 2
OCEAN_STEPS = 2
AH = 2 * ACOUSTIC
OH = OCEAN_STEPS

ATM_GAIN = 0.5
SEA_GAIN = 0.5

F32 = jnp.float32
BF16 = jnp.bfloat16


def lane_slots(levels, tracers):
    slots = [AH * i for i in range(3 * levels)]
    base = AH * 3 * levels
    slots += [base + OH * i for i in range(tracers)]
    base += OH * tracers
    slots += [base + AH * i for i in range(3)]
    total = base + 3 * AH
    return slots, -(-total // 128) * 128


def row_slots(levels, tracers):
    tracer = 5 * levels
    misc = tracer + OH * tracers
    own = misc + AH + 2 * OH
    _, lanes = lane_slots(levels, tracers)
    return tracer, misc, own, own + 2 * AH * (lanes // 128)


def near_rows(u, v, h, speed, rows, cols):
    east_west = (pltpu.roll(u, cols - 1, 1) - pltpu.roll(u, 1, 1)) * 0.5
    south_north = (pltpu.roll(v, rows - 1, 0) - pltpu.roll(v, 1, 0)) * 0.5
    h1 = h - speed * (east_west + south_north)
    out = []
    for near, turn in ((0, 1), (rows - 1, -1)):
        at = [slice(near + turn * i, near + turn * i + 1) for i in range(3)]
        out.append(
            (
                u[at[0]],
                v[at[0]],
                h[at[0]] - (0.5 * turn) * speed[at[0]] * v[at[1]],
                h1[at[1]],
                h1[at[2]] - (2.0 * turn) * v[at[1]],
            )
        )
    return out


def split3(value):
    hi = value.astype(BF16)
    rest = value - hi.astype(F32)
    mid = rest.astype(BF16)
    low = (rest - mid.astype(F32)).astype(BF16)
    return hi, mid, low


def one_hot(index, size):
    shape = (size, index.shape[-1])
    return lax.broadcasted_iota(jnp.int32, shape, 0) == index


def gather_rows(table, hot_rows, hot_cols):
    r = table.shape[0]
    parts = jnp.concatenate(split3(table), axis=0)
    g = jnp.dot(parts, hot_cols, preferred_element_type=F32)
    g = g[0:r] + g[r : 2 * r] + g[2 * r : 3 * r]
    return jnp.sum(jnp.where(hot_rows, g, 0.0), axis=0, keepdims=True)


def scatter_rows(values, hot_rows, hot_cols):
    r = hot_rows.shape[0]
    hot = jnp.where(hot_rows, 1.0, 0.0).astype(BF16)
    parts = [hot * part for value in values for part in split3(value)]
    s = lax.dot_general(
        jnp.concatenate(parts, axis=0),
        hot_cols,
        (((1,), (1,)), ((), ())),
        preferred_element_type=F32,
    )
    out = []
    for i in range(len(values)):
        base = 3 * r * i
        out.append(s[base : base + r] + s[base + r : base + 2 * r] + s[base + 2 * r : base + 3 * r])
    return out


def tile_at(shift, tiles):
    return lax.rem(lax.axis_index("tile") + shift % tiles, tiles)


def tile_parity():
    return lax.rem(lax.axis_index("tile") + 1, 2)


def column_parity():
    return lax.rem(lax.axis_index(("sub", "comp")), 2)


def first_kernel(tiles, *refs):
    sources, (cols_a, cols_b, rows_a, rows_b, wair_out, *sums_out) = refs[:11], refs[11:-18]
    held, (up, down, left, right, wair_buf, sums, sems) = refs[-18:-7], refs[-7:]
    atm, ocean, depth, wet, kappa, air, atm_cell, dest, sea_cell, weight, wave_speed = held
    used = []

    def copy(source, target):
        used.append(pltpu.make_async_copy(source, target, sems.at[len(used)]))
        used[-1].start()

    def copy_either(parity, source, even, odd):
        choices = [pltpu.make_async_copy(source, target, sems.at[len(used)]) for target in (even, odd)]
        pl.when(parity == 0)(choices[0].start)
        pl.when(parity != 0)(choices[1].start)
        used.append(choices[0])

    column, line = column_parity(), tile_parity()
    for source, target in zip(sources, held):
        copy(source, target)
    levels = atm.shape[1]
    rows, cols = atm.shape[2:]
    tracers = ocean.shape[0] * ocean.shape[1]
    each = ocean.shape[1]
    obase, mbase, own, halo = row_slots(levels, tracers)
    slots, _ = lane_slots(levels, tracers)
    for one in used:
        one.wait()
    arrived = len(used)
    wetness = wet[...].astype(F32)

    lane = lax.broadcasted_iota(jnp.int32, (rows, cols), 1)
    fields = [(atm, (k, l), AH) for k in range(3) for l in range(levels)]
    fields += [(ocean, (i // each, i % each), OH) for i in range(tracers)]
    fields += [(depth, None, AH), (None, None, AH), (kappa, None, AH)]
    packed = {}
    for (ref, at, width), slot in zip(fields, slots):
        value = wetness if ref is None else (ref[...] if at is None else ref[at[0], at[1]])
        tile, offset = slot // cols, slot % cols
        mask = (lane >= offset) & (lane < offset + width)
        first = pltpu.roll(value, offset, 1) if offset else value
        turn = (offset + width) % cols
        last = pltpu.roll(value, turn, 1) if turn else value
        if tile in packed:
            a, b = packed[tile]
            packed[tile] = (jnp.where(mask, first, a), jnp.where(mask, last, b))
        else:
            packed[tile] = (first, last)
    for tile, (a, b) in packed.items():
        where = slice(tile * cols, (tile + 1) * cols)
        left[:, where] = a
        right[:, where] = b

    copy_either(column, right, cols_a, cols_b)
    copy_either(column, left, cols_b, cols_a)

    for level in range(levels):
        speed = wave_speed[level] * depth[...]
        both = near_rows(atm[0, level], atm[1, level], atm[2, level], speed, rows, cols)
        for ref, values in zip((up, down), both):
            for i, value in enumerate(values):
                at = i * levels + level
                ref[at : at + 1, :] = value
    at = own
    for strip in (left, right):
        for i in range(strip.shape[1] // cols):
            where = slice(i * cols, (i + 1) * cols)
            up[at : at + AH, :] = strip[0:AH, where]
            down[at : at + AH, :] = strip[rows - AH : rows, where]
            at += AH
    for i in range(tracers):
        at = obase + OH * i
        up[at : at + OH, :] = ocean[i // each, i % each, 0:OH, :]
        down[at : at + OH, :] = ocean[i // each, i % each, rows - OH : rows, :]
    for at, value, width in (
        (mbase, depth[...], AH),
        (mbase + AH, wetness, OH),
        (mbase + AH + OH, kappa[...], OH),
    ):
        up[at : at + width, :] = value[0:width]
        down[at : at + width, :] = value[rows - width : rows]
    copy_either(line, down, rows_a.at[0:halo], rows_b.at[0:halo])
    copy_either(line, up, rows_b.at[0:halo], rows_a.at[0:halo])

    cell = atm_cell[...]
    hot_atm = jnp.where(one_hot(cell % cols, cols), 1.0, 0.0).astype(BF16)
    airx = gather_rows(air[...], one_hot(cell // cols, rows), hot_atm)
    w = weight[...]
    wair = w * airx
    wair_buf[...] = wair
    copy(wair_buf, wair_out)
    cell = sea_cell[...]
    hot_sea = jnp.where(one_hot(cell % cols, cols), 1.0, 0.0).astype(BF16)
    row = dest[...] * rows + cell // cols
    tail = slice(halo, halo + 3 * rows)
    for shift in range(tiles):
        target = tile_at(shift, tiles)
        s1, s2 = scatter_rows([wair, w], one_hot(row - target * rows, rows), hot_sea)
        sums[shift, 0:rows, :] = s1
        sums[shift, rows : 2 * rows, :] = s2
        sums[shift, 2 * rows : 3 * rows, :] = ocean[0, 0]
        if len(sums_out) == 1:
            copy(sums.at[shift], sums_out[0].at[target])
        elif shift == 1:
            copy_either(line, sums.at[shift], rows_a.at[tail], rows_b.at[tail])
        elif shift == tiles - 1:
            copy_either(line, sums.at[shift], rows_b.at[tail], rows_a.at[tail])
        else:
            copy(sums.at[shift], sums_out[max(shift - 1, 0)])
    for one in used[arrived:]:
        one.wait()


def strips(cols, slot, width, left_part, right_part):
    low_half = lax.broadcasted_iota(jnp.int32, (1, cols), 1) < cols // 2
    offset = slot % cols
    a, b = right_part(slot // cols), left_part(slot // cols)
    if offset:
        a = pltpu.roll(a, cols - offset, 1)
    turn = (cols - width - offset) % cols
    if turn:
        b = pltpu.roll(b, turn, 1)
    return jnp.where(low_half, a, b)


def final_kernel(tiles, *refs):
    speed_in, atm_in, ocean_in, depth_in, kappa_in = refs[:5]
    kept = (len(refs) - 5 - 8 - 4) // 2
    sources, rest = refs[5 : 5 + kept], refs[5 + kept :]
    atm_out, ocean_out, speed, us, vs, hs, fs, ms = rest[:8]
    held, (edge, atm_buf, ocean_buf, sems) = rest[8 : 8 + kept], rest[8 + kept :]
    wet, atm_cell, dest, sea_cell, weight, wair, from_up, from_down, from_left, from_right, from_below, from_above = held[:12]
    messages = held[12:]
    levels = us.shape[0]
    each = ocean_out.shape[1]
    tracers = ocean_out.shape[0] * each
    rows, cols = atm_out.shape[2:]
    slots, lanes = lane_slots(levels, tracers)
    obase, mbase, own, halo = row_slots(levels, tracers)
    full = rows + 2 * AH
    block = (slice(None), slice(0, rows), slice(0, cols))
    rows_a, rows_b, cols_a, cols_b = sources[6:10]
    either = [(tile_parity(), rows_b, rows_a, from_up), (tile_parity(), rows_a, rows_b, from_down)]
    either += [(column_parity(), cols_b, cols_a, from_left), (column_parity(), cols_a, cols_b, from_right)]
    pairs = [pair for i, pair in enumerate(zip(sources, held)) if not 6 <= i < 10] + [(speed_in, speed)]
    pairs += [(atm_in.at[i], ref.at[block]) for i, ref in enumerate((us, vs, hs))]
    pairs += [(ocean_in.at[i], fs.at[(i, *block)]) for i in range(ocean_out.shape[0])]
    pairs += [(ref, ms.at[(i, *block[1:])]) for i, ref in ((0, depth_in), (2, kappa_in))]
    copies = [pltpu.make_async_copy(source, target, sems.at[i]) for i, (source, target) in enumerate(pairs)]
    for copy in copies:
        copy.start()
    for parity, even, odd, target in either:
        choices = [pltpu.make_async_copy(source, target, sems.at[len(copies)]) for source in (even, odd)]
        pl.when(parity == 0)(choices[0].start)
        pl.when(parity != 0)(choices[1].start)
        copies.append(choices[0])
    for copy in copies:
        copy.wait()
    corner_a, corner_b = from_below, from_above
    even_line, even_column = tile_parity() == 0, column_parity() == 0

    def message(shift, part):
        where = slice(part * rows, (part + 1) * rows)
        if len(messages) == 1:
            return messages[0][tile_at(-shift, tiles), where, :]
        if shift in (1, tiles - 1):
            return (from_up if shift == 1 else from_down)[halo + part * rows : halo + (part + 1) * rows, :]
        return messages[max(shift - 1, 0)][where, :]

    surface = fs[0, 0, 0:rows, 0:cols]
    cell = sea_cell[...]
    hot_sea = jnp.where(one_hot(cell % cols, cols), 1.0, 0.0).astype(BF16)
    row = dest[...] * rows + cell // cols
    s1, s2 = message(0, 0), message(0, 1)
    sstx = jnp.zeros(cell.shape, F32)
    for shift in range(tiles):
        if shift:
            s1 = s1 + message(shift, 0)
            s2 = s2 + message(shift, 1)
        sstx = sstx + gather_rows(message(shift, 2), one_hot(row - tile_at(-shift, tiles) * rows, rows), hot_sea)
    sea_flux = s1 - surface * s2
    flux = wair[...] - weight[...] * sstx
    cell = atm_cell[...]
    hot_atm = jnp.where(one_hot(cell % cols, cols), 1.0, 0.0).astype(BF16)
    (atm_flux,) = scatter_rows([flux], one_hot(cell // cols, rows), hot_atm)

    half = lanes // cols
    for i in range(2 * half):
        where = slice(i % half * cols, (i % half + 1) * cols)
        first, second = (slice(AH, 2 * AH), slice(0, AH)) if i < half else (slice(0, AH), slice(AH, 2 * AH))
        a = jnp.where(even_column, corner_a[first, where], corner_a[second, where])
        b = jnp.where(even_column, corner_b[first, where], corner_b[second, where])
        edge[i, 0:AH, :] = jnp.where(even_line, a, b)
        edge[i, AH : 2 * AH, :] = jnp.where(even_line, b, a)
        at = own + AH * i
        edge[2 * half + i, 0:AH, :] = from_down[at : at + AH, :]
        edge[2 * half + i, AH : 2 * AH, :] = from_up[at : at + AH, :]

    def extend(view, field, width):
        slot = slots[field]
        view[0:rows, cols : 2 * cols] = strips(
            cols,
            slot,
            width,
            lambda t: from_left[:, t * cols : (t + 1) * cols],
            lambda t: from_right[:, t * cols : (t + 1) * cols],
        )
        view[rows:full, cols : 2 * cols] = strips(cols, slot, width, lambda t: edge[t], lambda t: edge[half + t])

    def extend_rows(view, at, high):
        view[rows : rows + high, 0:cols] = from_down[at : at + high, :]
        view[full - high : full, 0:cols] = from_up[at : at + high, :]

    lane = lax.broadcasted_iota(jnp.int32, (2 * AH, cols), 1)
    line = lax.broadcasted_iota(jnp.int32, (2 * AH, cols), 0)
    whole_strip = (lane < AH) | (lane >= cols - AH)
    outer = (lane < AH - 1) | (lane > cols - AH)

    def near(which, level):
        at = which * levels + level
        return from_down[at : at + 1, :], from_up[at : at + 1, :]

    def extend_level(view, which, level):
        strip = strips(cols, slots[which * levels + level], AH, lambda t: edge[3 * half + t], lambda t: edge[2 * half + t])
        below, above = near(which, level)
        inner = jnp.where(line == 0, below, jnp.where(line == 2 * AH - 1, above, 0.0))
        view[rows:full, 0:cols] = jnp.where(whole_strip if which == 0 else outer, strip, inner)

    def new_height_rows(tile, level):
        below, above = near(3, level), near(4, level)
        sent = jnp.where(
            line == 1, below[0], jnp.where(line == 2, above[0], jnp.where(line == 2 * AH - 3, above[1], below[1]))
        )
        here = (line == 1) | (line == 2) | (line == 2 * AH - 3) | (line == 2 * AH - 2)
        return jnp.where(here & jnp.logical_not(outer), sent, tile)

    def east(f):
        return pltpu.roll(f, 2 * cols - 1, 1)

    def west(f):
        return pltpu.roll(f, 1, 1)

    def south(f):
        return pltpu.roll(f, full - 1, 0)

    def north(f):
        return pltpu.roll(f, 1, 0)

    base = 3 * levels + tracers
    ms[1, 0:rows, 0:cols] = wet[...].astype(F32)
    for i, (at, high) in enumerate(((mbase, AH), (mbase + AH, OH), (mbase + AH + OH, OH))):
        extend(ms.at[i], base + i, AH)
        extend_rows(ms.at[i], at, high)
    for i in range(tracers):
        extend(fs.at[i // each, i % each], 3 * levels + i, OH)
        extend_rows(fs.at[i // each, i % each], obase + OH * i, OH)
    for level in range(levels):
        for which, ref in enumerate((us, vs, hs)):
            extend(ref.at[level], which * levels + level, AH)
            extend_level(ref.at[level], which, level)

    w = ms[1]
    k = ms[2]
    kw = k * w
    ce, cw, cs, cn = kw * east(w), kw * west(w), kw * south(w), kw * north(w)
    center = 1.0 - (ce + cw + cs + cn)
    for step in range(OCEAN_STEPS):
        for i in range(tracers):
            f = fs[i // each, i % each]
            f = center * f + ce * east(f) + cw * west(f) + cs * south(f) + cn * north(f)
            if step < OCEAN_STEPS - 1:
                fs[i // each, i % each] = f
            else:
                f = f[0:rows, 0:cols]
                ocean_buf[i // each, i % each] = f + SEA_GAIN * sea_flux if i == 0 else f
    used = len(copies)
    copies = [pltpu.make_async_copy(ocean_buf, ocean_out, sems.at[used])]
    copies[0].start()

    d = 0.5 * ms[0]
    chunk = max(1, levels // 4)
    for step in range(ACOUSTIC):
        for level in range(levels):
            u, v, h = us[level], vs[level], hs[level]
            hs[level] = h - (speed[level] * d) * ((east(u) - west(u)) + (south(v) - north(v)))
            if step == 0:
                hs[level, rows:full, 0:cols] = new_height_rows(hs[level, rows:full, 0:cols], level)
        for level in range(levels):
            u, v, h = us[level], vs[level], hs[level]
            u = u - (east(h) - west(h)) * 0.5
            v = v - (south(h) - north(h)) * 0.5
            if step < ACOUSTIC - 1:
                us[level], vs[level] = u, v
            else:
                h = h[0:rows, 0:cols]
                atm_buf[0, level] = u[0:rows, 0:cols]
                atm_buf[1, level] = v[0:rows, 0:cols]
                atm_buf[2, level] = h - ATM_GAIN * atm_flux if level == levels - 1 else h
                if (level + 1) % chunk == 0:
                    where = pl.ds(level + 1 - chunk, chunk)
                    copies.append(
                        pltpu.make_async_copy(
                            atm_buf.at[:, where], atm_out.at[:, where], sems.at[used + len(copies)]
                        )
                    )
                    copies[-1].start()
    for copy in copies:
        copy.wait()


def on_device(
    tile_count,
    atm_state,
    air_temp,
    depth,
    wave_speed,
    ocean_state,
    wet_mask,
    diffusivity,
    xg_atm_cell,
    xg_dest,
    xg_ocean_cell,
    xg_weight,
):
    levels = atm_state.shape[1]
    rows, cols = atm_state.shape[2:]
    tracers = ocean_state.shape[0] * ocean_state.shape[1]
    cells = xg_weight.shape[-1]
    _, lanes = lane_slots(levels, tracers)
    _, _, _, halo = row_slots(levels, tracers)
    message_rows = halo
    vmem = pl.BlockSpec(memory_space=pltpu.VMEM)
    hbm = pl.BlockSpec(memory_space=pltpu.HBM)
    whole = pltpu.CompilerParams(vmem_limit_bytes=64 * 1024 * 1024)
    full = rows + 2 * AH

    def shape(*dims):
        return jax.ShapeDtypeStruct(dims, F32)

    by_shift = tile_count <= 4
    if by_shift:
        message_rows += 3 * rows
        sums = [shape(3 * rows, cols)] * (tile_count - 2)
    else:
        sums = [shape(tile_count, 3 * rows, cols)]
    atm_cell = xg_atm_cell.reshape(1, cells)
    dest = xg_dest.reshape(1, cells)
    sea_cell = xg_ocean_cell.reshape(1, cells)
    weight = xg_weight.reshape(1, cells)
    operands = (atm_state, ocean_state, depth, wet_mask, diffusivity, air_temp, atm_cell, dest, sea_cell, weight)
    operands += (wave_speed,)
    cols_a, cols_b, rows_a, rows_b, wair, *messages = pl.pallas_call(
        functools.partial(first_kernel, tile_count),
        out_shape=[shape(rows, lanes)] * 2 + [shape(message_rows, cols)] * 2 + [shape(1, cells)] + sums,
        in_specs=[hbm] * 11,
        out_specs=[hbm] * (5 + len(sums)),
        scratch_shapes=[pltpu.VMEM(x.shape, x.dtype) for x in operands[:-1]]
        + [pltpu.SMEM(wave_speed.shape, F32)]
        + [pltpu.VMEM((halo, cols), F32)] * 2
        + [pltpu.VMEM((rows, lanes), F32)] * 2
        + [
            pltpu.VMEM((1, cells), F32),
            pltpu.VMEM((tile_count, 3 * rows, cols), F32),
            pltpu.SemaphoreType.DMA((16 + tile_count,)),
        ],
        compiler_params=whole,
        name="first",
    )(*operands)

    column_axes = ("sub", "comp")
    column_count = lax.axis_size("sub") * lax.axis_size("comp")

    def shift(value, axes, count, by):
        return lax.ppermute(value, axes, [(i, (i + by) % count) for i in range(count)])

    def swap(value, axes, count, odd):
        return lax.ppermute(value, axes, [(i, (i + (1 if (i + odd) % 2 == 0 else -1)) % count) for i in range(count)])

    got_a = swap(cols_a, column_axes, column_count, 0)
    got_b = swap(cols_b, column_axes, column_count, 1)
    near_a = swap(rows_a, "tile", tile_count, 1)
    near_b = swap(rows_b, "tile", tile_count, 0)

    low = jnp.where(tile_parity() == 0, rows - AH, 0)
    corner_a, corner_b = [
        jnp.concatenate([lax.dynamic_slice_in_dim(x, at, AH) for x in (got_a, got_b)]) for at in (low, rows - AH - low)
    ]
    corner_a = swap(corner_a, "tile", tile_count, 1)
    corner_b = swap(corner_b, "tile", tile_count, 0)
    if by_shift:
        got = messages[:1] + [shift(messages[s - 1], "tile", tile_count, s) for s in range(2, tile_count - 1)]
    else:
        got = [lax.all_to_all(messages[0], "tile", split_axis=0, concat_axis=0, tiled=True)]

    operands = (wave_speed, atm_state, ocean_state, depth, diffusivity)
    operands += (wet_mask, atm_cell, dest, sea_cell, weight, wair, near_a, near_b, got_a, got_b)
    operands += (corner_a, corner_b, *got)
    return tuple(
        pl.pallas_call(
            functools.partial(final_kernel, tile_count),
            out_shape=[shape(*atm_state.shape), shape(*ocean_state.shape)],
            in_specs=[hbm] * len(operands),
            out_specs=[hbm] * 2,
            scratch_shapes=[pltpu.SMEM(wave_speed.shape, F32)]
            + [pltpu.VMEM((levels, full, 2 * cols), F32)] * 3
            + [
                pltpu.VMEM((*ocean_state.shape[:2], full, 2 * cols), F32),
                pltpu.VMEM((3, full, 2 * cols), F32),
            ]
            + [pltpu.VMEM(x.shape, x.dtype) for x in operands[5:]]
            + [
                pltpu.VMEM((4 * (lanes // cols), 2 * AH, cols), F32),
                pltpu.VMEM(atm_state.shape, F32),
                pltpu.VMEM(ocean_state.shape, F32),
                pltpu.SemaphoreType.DMA((len(operands) + 10,)),
            ],
            compiler_params=whole,
            name="steps",
        )(*operands)
    )


def solution(mesh):
    grid = P(("member", "tile"), ("sub", "comp"))
    state = P(None, None, ("member", "tile"), ("sub", "comp"))
    cells = P(("member", "tile"), ("sub", "comp"), None)
    return jax.shard_map(
        functools.partial(on_device, mesh.shape["tile"]),
        mesh=mesh,
        in_specs=(
            state,
            grid,
            grid,
            P(),
            state,
            grid,
            grid,
            cells,
            P(("member", "tile"), ("sub", "comp"), None, None),
            cells,
            cells,
        ),
        out_specs=(state, state),
        check_vma=False,
    )
```

```python
import functools

import jax
import jax.numpy as jnp
from jax import lax
from jax.experimental import pallas as pl
from jax.experimental.pallas import tpu as pltpu
from jax.sharding import PartitionSpec as P

ACOUSTIC = 2
OCEAN_STEPS = 2
AH = 2 * ACOUSTIC
OH = OCEAN_STEPS

ATM_GAIN = 0.5
SEA_GAIN = 0.5

F32 = jnp.float32
BF16 = jnp.bfloat16


def lane_slots(levels, tracers):
    slots = [AH * i for i in range(3 * levels)]
    base = AH * 3 * levels
    slots += [base + OH * i for i in range(tracers)]
    base += OH * tracers
    slots += [base + AH * i for i in range(3)]
    total = base + 3 * AH
    return slots, -(-total // 128) * 128


def row_slots(levels, tracers):
    tracer = 5 * levels
    misc = tracer + OH * tracers
    own = misc + AH + 2 * OH
    _, lanes = lane_slots(levels, tracers)
    return tracer, misc, own, own + 2 * AH * (lanes // 128)


def near_rows(u, v, h, speed, rows, cols):
    east_west = (pltpu.roll(u, cols - 1, 1) - pltpu.roll(u, 1, 1)) * 0.5
    south_north = (pltpu.roll(v, rows - 1, 0) - pltpu.roll(v, 1, 0)) * 0.5
    h1 = h - speed * (east_west + south_north)
    out = []
    for near, turn in ((0, 1), (rows - 1, -1)):
        at = [slice(near + turn * i, near + turn * i + 1) for i in range(3)]
        out.append(
            (
                u[at[0]],
                v[at[0]],
                h[at[0]] - (0.5 * turn) * speed[at[0]] * v[at[1]],
                h1[at[1]],
                h1[at[2]] - (2.0 * turn) * v[at[1]],
            )
        )
    return out


def split3(value):
    hi = value.astype(BF16)
    rest = value - hi.astype(F32)
    mid = rest.astype(BF16)
    low = (rest - mid.astype(F32)).astype(BF16)
    return hi, mid, low


def one_hot(index, size):
    shape = (size, index.shape[-1])
    return lax.broadcasted_iota(jnp.int32, shape, 0) == index


def gather_rows(table, hot_rows, hot_cols):
    r = table.shape[0]
    parts = jnp.concatenate(split3(table), axis=0)
    g = jnp.dot(parts, hot_cols, preferred_element_type=F32)
    g = g[0:r] + g[r : 2 * r] + g[2 * r : 3 * r]
    return jnp.sum(jnp.where(hot_rows, g, 0.0), axis=0, keepdims=True)


def scatter_rows(values, hot_rows, hot_cols):
    r = hot_rows.shape[0]
    hot = jnp.where(hot_rows, 1.0, 0.0).astype(BF16)
    parts = [hot * part for value in values for part in split3(value)]
    s = lax.dot_general(
        jnp.concatenate(parts, axis=0),
        hot_cols,
        (((1,), (1,)), ((), ())),
        preferred_element_type=F32,
    )
    out = []
    for i in range(len(values)):
        base = 3 * r * i
        out.append(s[base : base + r] + s[base + r : base + 2 * r] + s[base + 2 * r : base + 3 * r])
    return out


def tile_at(shift, tiles):
    return lax.rem(lax.axis_index("tile") + shift % tiles, tiles)


def tile_parity():
    return lax.rem(lax.axis_index("tile") + 1, 2)


def column_parity():
    return lax.rem(lax.axis_index(("sub", "comp")), 2)


def first_kernel(tiles, *refs):
    sources, (cols_a, cols_b, rows_a, rows_b, wair_out, *sums_out) = refs[:11], refs[11:-18]
    held, (up, down, left, right, wair_buf, sums, sems) = refs[-18:-7], refs[-7:]
    atm, ocean, depth, wet, kappa, air, atm_cell, dest, sea_cell, weight, wave_speed = held
    used = []

    def copy(source, target):
        used.append(pltpu.make_async_copy(source, target, sems.at[len(used)]))
        used[-1].start()

    def copy_either(parity, source, even, odd):
        choices = [pltpu.make_async_copy(source, target, sems.at[len(used)]) for target in (even, odd)]
        pl.when(parity == 0)(choices[0].start)
        pl.when(parity != 0)(choices[1].start)
        used.append(choices[0])

    column, line = column_parity(), tile_parity()
    for source, target in zip(sources, held):
        copy(source, target)
    levels = atm.shape[1]
    rows, cols = atm.shape[2:]
    tracers = ocean.shape[0] * ocean.shape[1]
    each = ocean.shape[1]
    obase, mbase, own, halo = row_slots(levels, tracers)
    slots, _ = lane_slots(levels, tracers)
    for one in used:
        one.wait()
    arrived = len(used)
    wetness = wet[...].astype(F32)

    lane = lax.broadcasted_iota(jnp.int32, (rows, cols), 1)
    fields = [(atm, (k, l), AH) for k in range(3) for l in range(levels)]
    fields += [(ocean, (i // each, i % each), OH) for i in range(tracers)]
    fields += [(depth, None, AH), (None, None, AH), (kappa, None, AH)]
    packed = {}
    for (ref, at, width), slot in zip(fields, slots):
        value = wetness if ref is None else (ref[...] if at is None else ref[at[0], at[1]])
        tile, offset = slot // cols, slot % cols
        mask = (lane >= offset) & (lane < offset + width)
        first = pltpu.roll(value, offset, 1) if offset else value
        turn = (offset + width) % cols
        last = pltpu.roll(value, turn, 1) if turn else value
        if tile in packed:
            a, b = packed[tile]
            packed[tile] = (jnp.where(mask, first, a), jnp.where(mask, last, b))
        else:
            packed[tile] = (first, last)
    for tile, (a, b) in packed.items():
        where = slice(tile * cols, (tile + 1) * cols)
        left[:, where] = a
        right[:, where] = b

    copy_either(column, right, cols_a, cols_b)
    copy_either(column, left, cols_b, cols_a)

    for level in range(levels):
        speed = wave_speed[level] * depth[...]
        both = near_rows(atm[0, level], atm[1, level], atm[2, level], speed, rows, cols)
        for ref, values in zip((up, down), both):
            for i, value in enumerate(values):
                at = i * levels + level
                ref[at : at + 1, :] = value
    at = own
    for strip in (left, right):
        for i in range(strip.shape[1] // cols):
            where = slice(i * cols, (i + 1) * cols)
            up[at : at + AH, :] = strip[0:AH, where]
            down[at : at + AH, :] = strip[rows - AH : rows, where]
            at += AH
    for i in range(tracers):
        at = obase + OH * i
        up[at : at + OH, :] = ocean[i // each, i % each, 0:OH, :]
        down[at : at + OH, :] = ocean[i // each, i % each, rows - OH : rows, :]
    for at, value, width in (
        (mbase, depth[...], AH),
        (mbase + AH, wetness, OH),
        (mbase + AH + OH, kappa[...], OH),
    ):
        up[at : at + width, :] = value[0:width]
        down[at : at + width, :] = value[rows - width : rows]
    copy_either(line, down, rows_a.at[0:halo], rows_b.at[0:halo])
    copy_either(line, up, rows_b.at[0:halo], rows_a.at[0:halo])

    cell = atm_cell[...]
    hot_atm = jnp.where(one_hot(cell % cols, cols), 1.0, 0.0).astype(BF16)
    airx = gather_rows(air[...], one_hot(cell // cols, rows), hot_atm)
    w = weight[...]
    wair = w * airx
    wair_buf[...] = wair
    copy(wair_buf, wair_out)
    cell = sea_cell[...]
    hot_sea = jnp.where(one_hot(cell % cols, cols), 1.0, 0.0).astype(BF16)
    row = dest[...] * rows + cell // cols
    tail = slice(halo, halo + 3 * rows)
    for shift in range(tiles):
        target = tile_at(shift, tiles)
        s1, s2 = scatter_rows([wair, w], one_hot(row - target * rows, rows), hot_sea)
        sums[shift, 0:rows, :] = s1
        sums[shift, rows : 2 * rows, :] = s2
        sums[shift, 2 * rows : 3 * rows, :] = ocean[0, 0]
        if len(sums_out) == 1:
            copy(sums.at[shift], sums_out[0].at[target])
        elif shift == 1:
            copy_either(line, sums.at[shift], rows_a.at[tail], rows_b.at[tail])
        elif shift == tiles - 1:
            copy_either(line, sums.at[shift], rows_b.at[tail], rows_a.at[tail])
        else:
            copy(sums.at[shift], sums_out[max(shift - 1, 0)])
    for one in used[arrived:]:
        one.wait()


def corner_kernel(got_a, got_b, corner_a, corner_b):
    rows = got_a.shape[0]
    first = tile_parity() == 0
    for i, ref in enumerate((got_a, got_b)):
        low, high = ref[0:AH, :], ref[rows - AH : rows, :]
        corner_a[i * AH : (i + 1) * AH, :] = jnp.where(first, high, low)
        corner_b[i * AH : (i + 1) * AH, :] = jnp.where(first, low, high)


def strips(cols, slot, width, left_part, right_part):
    low_half = lax.broadcasted_iota(jnp.int32, (1, cols), 1) < cols // 2
    offset = slot % cols
    a, b = right_part(slot // cols), left_part(slot // cols)
    if offset:
        a = pltpu.roll(a, cols - offset, 1)
    turn = (cols - width - offset) % cols
    if turn:
        b = pltpu.roll(b, turn, 1)
    return jnp.where(low_half, a, b)


def final_kernel(tiles, *refs):
    speed_in, atm_in, ocean_in, depth_in, kappa_in = refs[:5]
    kept = (len(refs) - 5 - 8 - 4) // 2
    sources, rest = refs[5 : 5 + kept], refs[5 + kept :]
    atm_out, ocean_out, speed, us, vs, hs, fs, ms = rest[:8]
    held, (edge, atm_buf, ocean_buf, sems) = rest[8 : 8 + kept], rest[8 + kept :]
    wet, atm_cell, dest, sea_cell, weight, wair, from_up, from_down, from_left, from_right, from_below, from_above = held[:12]
    messages = held[12:]
    levels = us.shape[0]
    each = ocean_out.shape[1]
    tracers = ocean_out.shape[0] * each
    rows, cols = atm_out.shape[2:]
    slots, lanes = lane_slots(levels, tracers)
    obase, mbase, own, halo = row_slots(levels, tracers)
    full = rows + 2 * AH
    block = (slice(None), slice(0, rows), slice(0, cols))
    rows_a, rows_b, cols_a, cols_b = sources[6:10]
    either = [(tile_parity(), rows_b, rows_a, from_up), (tile_parity(), rows_a, rows_b, from_down)]
    either += [(column_parity(), cols_b, cols_a, from_left), (column_parity(), cols_a, cols_b, from_right)]
    pairs = [pair for i, pair in enumerate(zip(sources, held)) if not 6 <= i < 10] + [(speed_in, speed)]
    pairs += [(atm_in.at[i], ref.at[block]) for i, ref in enumerate((us, vs, hs))]
    pairs += [(ocean_in.at[i], fs.at[(i, *block)]) for i in range(ocean_out.shape[0])]
    pairs += [(ref, ms.at[(i, *block[1:])]) for i, ref in ((0, depth_in), (2, kappa_in))]
    copies = [pltpu.make_async_copy(source, target, sems.at[i]) for i, (source, target) in enumerate(pairs)]
    for copy in copies:
        copy.start()
    for parity, even, odd, target in either:
        choices = [pltpu.make_async_copy(source, target, sems.at[len(copies)]) for source in (even, odd)]
        pl.when(parity == 0)(choices[0].start)
        pl.when(parity != 0)(choices[1].start)
        copies.append(choices[0])
    for copy in copies:
        copy.wait()
    corner_a, corner_b = from_below, from_above
    even_line, even_column = tile_parity() == 0, column_parity() == 0

    def message(shift, part):
        where = slice(part * rows, (part + 1) * rows)
        if len(messages) == 1:
            return messages[0][tile_at(-shift, tiles), where, :]
        if shift in (1, tiles - 1):
            return (from_up if shift == 1 else from_down)[halo + part * rows : halo + (part + 1) * rows, :]
        return messages[max(shift - 1, 0)][where, :]

    surface = fs[0, 0, 0:rows, 0:cols]
    cell = sea_cell[...]
    hot_sea = jnp.where(one_hot(cell % cols, cols), 1.0, 0.0).astype(BF16)
    row = dest[...] * rows + cell // cols
    s1, s2 = message(0, 0), message(0, 1)
    sstx = jnp.zeros(cell.shape, F32)
    for shift in range(tiles):
        if shift:
            s1 = s1 + message(shift, 0)
            s2 = s2 + message(shift, 1)
        sstx = sstx + gather_rows(message(shift, 2), one_hot(row - tile_at(-shift, tiles) * rows, rows), hot_sea)
    sea_flux = s1 - surface * s2
    flux = wair[...] - weight[...] * sstx
    cell = atm_cell[...]
    hot_atm = jnp.where(one_hot(cell % cols, cols), 1.0, 0.0).astype(BF16)
    (atm_flux,) = scatter_rows([flux], one_hot(cell // cols, rows), hot_atm)

    half = lanes // cols
    for i in range(2 * half):
        where = slice(i % half * cols, (i % half + 1) * cols)
        first, second = (slice(AH, 2 * AH), slice(0, AH)) if i < half else (slice(0, AH), slice(AH, 2 * AH))
        a = jnp.where(even_column, corner_a[first, where], corner_a[second, where])
        b = jnp.where(even_column, corner_b[first, where], corner_b[second, where])
        edge[i, 0:AH, :] = jnp.where(even_line, a, b)
        edge[i, AH : 2 * AH, :] = jnp.where(even_line, b, a)
        at = own + AH * i
        edge[2 * half + i, 0:AH, :] = from_down[at : at + AH, :]
        edge[2 * half + i, AH : 2 * AH, :] = from_up[at : at + AH, :]

    def extend(view, field, width):
        slot = slots[field]
        view[0:rows, cols : 2 * cols] = strips(
            cols,
            slot,
            width,
            lambda t: from_left[:, t * cols : (t + 1) * cols],
            lambda t: from_right[:, t * cols : (t + 1) * cols],
        )
        view[rows:full, cols : 2 * cols] = strips(cols, slot, width, lambda t: edge[t], lambda t: edge[half + t])

    def extend_rows(view, at, high):
        view[rows : rows + high, 0:cols] = from_down[at : at + high, :]
        view[full - high : full, 0:cols] = from_up[at : at + high, :]

    lane = lax.broadcasted_iota(jnp.int32, (2 * AH, cols), 1)
    line = lax.broadcasted_iota(jnp.int32, (2 * AH, cols), 0)
    whole_strip = (lane < AH) | (lane >= cols - AH)
    outer = (lane < AH - 1) | (lane > cols - AH)

    def near(which, level):
        at = which * levels + level
        return from_down[at : at + 1, :], from_up[at : at + 1, :]

    def extend_level(view, which, level):
        strip = strips(cols, slots[which * levels + level], AH, lambda t: edge[3 * half + t], lambda t: edge[2 * half + t])
        below, above = near(which, level)
        inner = jnp.where(line == 0, below, jnp.where(line == 2 * AH - 1, above, 0.0))
        view[rows:full, 0:cols] = jnp.where(whole_strip if which == 0 else outer, strip, inner)

    def new_height_rows(tile, level):
        below, above = near(3, level), near(4, level)
        sent = jnp.where(
            line == 1, below[0], jnp.where(line == 2, above[0], jnp.where(line == 2 * AH - 3, above[1], below[1]))
        )
        here = (line == 1) | (line == 2) | (line == 2 * AH - 3) | (line == 2 * AH - 2)
        return jnp.where(here & jnp.logical_not(outer), sent, tile)

    def east(f):
        return pltpu.roll(f, 2 * cols - 1, 1)

    def west(f):
        return pltpu.roll(f, 1, 1)

    def south(f):
        return pltpu.roll(f, full - 1, 0)

    def north(f):
        return pltpu.roll(f, 1, 0)

    base = 3 * levels + tracers
    ms[1, 0:rows, 0:cols] = wet[...].astype(F32)
    for i, (at, high) in enumerate(((mbase, AH), (mbase + AH, OH), (mbase + AH + OH, OH))):
        extend(ms.at[i], base + i, AH)
        extend_rows(ms.at[i], at, high)
    for i in range(tracers):
        extend(fs.at[i // each, i % each], 3 * levels + i, OH)
        extend_rows(fs.at[i // each, i % each], obase + OH * i, OH)
    for level in range(levels):
        for which, ref in enumerate((us, vs, hs)):
            extend(ref.at[level], which * levels + level, AH)
            extend_level(ref.at[level], which, level)

    w = ms[1]
    k = ms[2]
    kw = k * w
    ce, cw, cs, cn = kw * east(w), kw * west(w), kw * south(w), kw * north(w)
    center = 1.0 - (ce + cw + cs + cn)
    for step in range(OCEAN_STEPS):
        for i in range(tracers):
            f = fs[i // each, i % each]
            f = center * f + ce * east(f) + cw * west(f) + cs * south(f) + cn * north(f)
            if step < OCEAN_STEPS - 1:
                fs[i // each, i % each] = f
            else:
                f = f[0:rows, 0:cols]
                ocean_buf[i // each, i % each] = f + SEA_GAIN * sea_flux if i == 0 else f
    used = len(copies)
    copies = [pltpu.make_async_copy(ocean_buf, ocean_out, sems.at[used])]
    copies[0].start()

    d = 0.5 * ms[0]
    chunk = max(1, levels // 4)
    for step in range(ACOUSTIC):
        for level in range(levels):
            u, v, h = us[level], vs[level], hs[level]
            hs[level] = h - (speed[level] * d) * ((east(u) - west(u)) + (south(v) - north(v)))
            if step == 0:
                hs[level, rows:full, 0:cols] = new_height_rows(hs[level, rows:full, 0:cols], level)
        for level in range(levels):
            u, v, h = us[level], vs[level], hs[level]
            u = u - (east(h) - west(h)) * 0.5
            v = v - (south(h) - north(h)) * 0.5
            if step < ACOUSTIC - 1:
                us[level], vs[level] = u, v
            else:
                h = h[0:rows, 0:cols]
                atm_buf[0, level] = u[0:rows, 0:cols]
                atm_buf[1, level] = v[0:rows, 0:cols]
                atm_buf[2, level] = h - ATM_GAIN * atm_flux if level == levels - 1 else h
                if (level + 1) % chunk == 0:
                    where = pl.ds(level + 1 - chunk, chunk)
                    copies.append(
                        pltpu.make_async_copy(
                            atm_buf.at[:, where], atm_out.at[:, where], sems.at[used + len(copies)]
                        )
                    )
                    copies[-1].start()
    for copy in copies:
        copy.wait()


def on_device(
    tile_count,
    atm_state,
    air_temp,
    depth,
    wave_speed,
    ocean_state,
    wet_mask,
    diffusivity,
    xg_atm_cell,
    xg_dest,
    xg_ocean_cell,
    xg_weight,
):
    levels = atm_state.shape[1]
    rows, cols = atm_state.shape[2:]
    tracers = ocean_state.shape[0] * ocean_state.shape[1]
    cells = xg_weight.shape[-1]
    _, lanes = lane_slots(levels, tracers)
    _, _, _, halo = row_slots(levels, tracers)
    message_rows = halo
    vmem = pl.BlockSpec(memory_space=pltpu.VMEM)
    hbm = pl.BlockSpec(memory_space=pltpu.HBM)
    whole = pltpu.CompilerParams(vmem_limit_bytes=64 * 1024 * 1024)
    full = rows + 2 * AH

    def shape(*dims):
        return jax.ShapeDtypeStruct(dims, F32)

    by_shift = tile_count <= 4
    if by_shift:
        message_rows += 3 * rows
        sums = [shape(3 * rows, cols)] * (tile_count - 2)
    else:
        sums = [shape(tile_count, 3 * rows, cols)]
    atm_cell = xg_atm_cell.reshape(1, cells)
    dest = xg_dest.reshape(1, cells)
    sea_cell = xg_ocean_cell.reshape(1, cells)
    weight = xg_weight.reshape(1, cells)
    operands = (atm_state, ocean_state, depth, wet_mask, diffusivity, air_temp, atm_cell, dest, sea_cell, weight)
    operands += (wave_speed,)
    cols_a, cols_b, rows_a, rows_b, wair, *messages = pl.pallas_call(
        functools.partial(first_kernel, tile_count),
        out_shape=[shape(rows, lanes)] * 2 + [shape(message_rows, cols)] * 2 + [shape(1, cells)] + sums,
        in_specs=[hbm] * 11,
        out_specs=[hbm] * (5 + len(sums)),
        scratch_shapes=[pltpu.VMEM(x.shape, x.dtype) for x in operands[:-1]]
        + [pltpu.SMEM(wave_speed.shape, F32)]
        + [pltpu.VMEM((halo, cols), F32)] * 2
        + [pltpu.VMEM((rows, lanes), F32)] * 2
        + [
            pltpu.VMEM((1, cells), F32),
            pltpu.VMEM((tile_count, 3 * rows, cols), F32),
            pltpu.SemaphoreType.DMA((16 + tile_count,)),
        ],
        compiler_params=whole,
        name="first",
    )(*operands)

    column_axes = ("sub", "comp")
    column_count = lax.axis_size("sub") * lax.axis_size("comp")

    def shift(value, axes, count, by):
        return lax.ppermute(value, axes, [(i, (i + by) % count) for i in range(count)])

    def swap(value, axes, count, odd):
        return lax.ppermute(value, axes, [(i, (i + (1 if (i + odd) % 2 == 0 else -1)) % count) for i in range(count)])

    got_a = swap(cols_a, column_axes, column_count, 0)
    got_b = swap(cols_b, column_axes, column_count, 1)
    near_a = swap(rows_a, "tile", tile_count, 1)
    near_b = swap(rows_b, "tile", tile_count, 0)

    corner_a, corner_b = pl.pallas_call(
        corner_kernel,
        out_shape=[shape(2 * AH, lanes)] * 2,
        in_specs=[vmem] * 2,
        out_specs=[vmem] * 2,
        compiler_params=pltpu.CompilerParams(vmem_limit_bytes=4 * 1024 * 1024),
        cost_estimate=pl.CostEstimate(flops=0, bytes_accessed=100000, transcendentals=0),
        name="corners",
    )(got_a, got_b)
    corner_a = swap(corner_a, "tile", tile_count, 1)
    corner_b = swap(corner_b, "tile", tile_count, 0)
    if by_shift:
        got = messages[:1] + [shift(messages[s - 1], "tile", tile_count, s) for s in range(2, tile_count - 1)]
    else:
        got = [lax.all_to_all(messages[0], "tile", split_axis=0, concat_axis=0, tiled=True)]

    operands = (wave_speed, atm_state, ocean_state, depth, diffusivity)
    operands += (wet_mask, atm_cell, dest, sea_cell, weight, wair, near_a, near_b, got_a, got_b)
    operands += (corner_a, corner_b, *got)
    return tuple(
        pl.pallas_call(
            functools.partial(final_kernel, tile_count),
            out_shape=[shape(*atm_state.shape), shape(*ocean_state.shape)],
            in_specs=[hbm] * len(operands),
            out_specs=[hbm] * 2,
            scratch_shapes=[pltpu.SMEM(wave_speed.shape, F32)]
            + [pltpu.VMEM((levels, full, 2 * cols), F32)] * 3
            + [
                pltpu.VMEM((*ocean_state.shape[:2], full, 2 * cols), F32),
                pltpu.VMEM((3, full, 2 * cols), F32),
            ]
            + [pltpu.VMEM(x.shape, x.dtype) for x in operands[5:]]
            + [
                pltpu.VMEM((4 * (lanes // cols), 2 * AH, cols), F32),
                pltpu.VMEM(atm_state.shape, F32),
                pltpu.VMEM(ocean_state.shape, F32),
                pltpu.SemaphoreType.DMA((len(operands) + 10,)),
            ],
            compiler_params=whole,
            name="steps",
        )(*operands)
    )


def solution(mesh):
    grid = P(("member", "tile"), ("sub", "comp"))
    state = P(None, None, ("member", "tile"), ("sub", "comp"))
    cells = P(("member", "tile"), ("sub", "comp"), None)
    return jax.shard_map(
        functools.partial(on_device, mesh.shape["tile"]),
        mesh=mesh,
        in_specs=(
            state,
            grid,
            grid,
            P(),
            state,
            grid,
            grid,
            cells,
            P(("member", "tile"), ("sub", "comp"), None, None),
            cells,
            cells,
        ),
        out_specs=(state, state),
        check_vma=False,
    )
```

```python
import functools

import jax
import jax.numpy as jnp
from jax import lax
from jax.experimental import pallas as pl
from jax.experimental.pallas import tpu as pltpu
from jax.sharding import PartitionSpec as P

ACOUSTIC = 2
OCEAN_STEPS = 2
AH = 2 * ACOUSTIC
OH = OCEAN_STEPS

ATM_GAIN = 0.5
SEA_GAIN = 0.5

F32 = jnp.float32
BF16 = jnp.bfloat16


def lane_slots(levels, tracers):
    slots = [AH * i for i in range(3 * levels)]
    base = AH * 3 * levels
    slots += [base + OH * i for i in range(tracers)]
    base += OH * tracers
    slots += [base + AH * i for i in range(3)]
    total = base + 3 * AH
    return slots, -(-total // 128) * 128


def row_slots(levels, tracers):
    tracer = 5 * levels
    misc = tracer + OH * tracers
    own = misc + AH + 2 * OH
    _, lanes = lane_slots(levels, tracers)
    return tracer, misc, own, own + 2 * AH * (lanes // 128)


def near_rows(u, v, h, speed, rows, cols):
    east_west = (pltpu.roll(u, cols - 1, 1) - pltpu.roll(u, 1, 1)) * 0.5
    south_north = (pltpu.roll(v, rows - 1, 0) - pltpu.roll(v, 1, 0)) * 0.5
    h1 = h - speed * (east_west + south_north)
    out = []
    for near, turn in ((0, 1), (rows - 1, -1)):
        at = [slice(near + turn * i, near + turn * i + 1) for i in range(3)]
        out.append(
            (
                u[at[0]],
                v[at[0]],
                h[at[0]] - (0.5 * turn) * speed[at[0]] * v[at[1]],
                h1[at[1]],
                h1[at[2]] - (2.0 * turn) * v[at[1]],
            )
        )
    return out


def split3(value):
    hi = value.astype(BF16)
    rest = value - hi.astype(F32)
    mid = rest.astype(BF16)
    low = (rest - mid.astype(F32)).astype(BF16)
    return hi, mid, low


def one_hot(index, size):
    shape = (size, index.shape[-1])
    return lax.broadcasted_iota(jnp.int32, shape, 0) == index


def gather_rows(table, hot_rows, hot_cols):
    r = table.shape[0]
    parts = jnp.concatenate(split3(table), axis=0)
    g = jnp.dot(parts, hot_cols, preferred_element_type=F32)
    g = g[0:r] + g[r : 2 * r] + g[2 * r : 3 * r]
    return jnp.sum(jnp.where(hot_rows, g, 0.0), axis=0, keepdims=True)


def scatter_rows(values, hot_rows, hot_cols):
    r = hot_rows.shape[0]
    hot = jnp.where(hot_rows, 1.0, 0.0).astype(BF16)
    parts = [hot * part for value in values for part in split3(value)]
    s = lax.dot_general(
        jnp.concatenate(parts, axis=0),
        hot_cols,
        (((1,), (1,)), ((), ())),
        preferred_element_type=F32,
    )
    out = []
    for i in range(len(values)):
        base = 3 * r * i
        out.append(s[base : base + r] + s[base + r : base + 2 * r] + s[base + 2 * r : base + 3 * r])
    return out


def tile_at(shift, tiles):
    return lax.rem(lax.axis_index("tile") + shift % tiles, tiles)


def tile_parity():
    return lax.rem(lax.axis_index("tile") + 1, 2)


def column_parity():
    return lax.rem(lax.axis_index(("sub", "comp")), 2)


def first_kernel(tiles, *refs):
    sources, (cols_a, cols_b, rows_a, rows_b, wair_out, *sums_out) = refs[:11], refs[11:-18]
    held, (up, down, left, right, wair_buf, sums, sems) = refs[-18:-7], refs[-7:]
    atm, ocean, depth, wet, kappa, air, atm_cell, dest, sea_cell, weight, wave_speed = held
    used = []

    def copy(source, target):
        used.append(pltpu.make_async_copy(source, target, sems.at[len(used)]))
        used[-1].start()

    def copy_either(parity, source, even, odd):
        choices = [pltpu.make_async_copy(source, target, sems.at[len(used)]) for target in (even, odd)]
        pl.when(parity == 0)(choices[0].start)
        pl.when(parity != 0)(choices[1].start)
        used.append(choices[0])

    column, line = column_parity(), tile_parity()
    for source, target in zip(sources, held):
        copy(source, target)
    levels = atm.shape[1]
    rows, cols = atm.shape[2:]
    tracers = ocean.shape[0] * ocean.shape[1]
    each = ocean.shape[1]
    obase, mbase, own, halo = row_slots(levels, tracers)
    slots, _ = lane_slots(levels, tracers)
    for one in used:
        one.wait()
    arrived = len(used)
    wetness = wet[...].astype(F32)

    lane = lax.broadcasted_iota(jnp.int32, (rows, cols), 1)
    fields = [(atm, (k, l), AH) for k in range(3) for l in range(levels)]
    fields += [(ocean, (i // each, i % each), OH) for i in range(tracers)]
    fields += [(depth, None, AH), (None, None, AH), (kappa, None, AH)]
    packed = {}
    for (ref, at, width), slot in zip(fields, slots):
        value = wetness if ref is None else (ref[...] if at is None else ref[at[0], at[1]])
        tile, offset = slot // cols, slot % cols
        mask = (lane >= offset) & (lane < offset + width)
        first = pltpu.roll(value, offset, 1) if offset else value
        turn = (offset + width) % cols
        last = pltpu.roll(value, turn, 1) if turn else value
        if tile in packed:
            a, b = packed[tile]
            packed[tile] = (jnp.where(mask, first, a), jnp.where(mask, last, b))
        else:
            packed[tile] = (first, last)
    for tile, (a, b) in packed.items():
        where = slice(tile * cols, (tile + 1) * cols)
        left[:, where] = a
        right[:, where] = b

    copy_either(column, right, cols_a, cols_b)
    copy_either(column, left, cols_b, cols_a)

    for level in range(levels):
        speed = wave_speed[level] * depth[...]
        both = near_rows(atm[0, level], atm[1, level], atm[2, level], speed, rows, cols)
        for ref, values in zip((up, down), both):
            for i, value in enumerate(values):
                at = i * levels + level
                ref[at : at + 1, :] = value
    at = own
    for strip in (left, right):
        for i in range(strip.shape[1] // cols):
            where = slice(i * cols, (i + 1) * cols)
            up[at : at + AH, :] = strip[0:AH, where]
            down[at : at + AH, :] = strip[rows - AH : rows, where]
            at += AH
    for i in range(tracers):
        at = obase + OH * i
        up[at : at + OH, :] = ocean[i // each, i % each, 0:OH, :]
        down[at : at + OH, :] = ocean[i // each, i % each, rows - OH : rows, :]
    for at, value, width in (
        (mbase, depth[...], AH),
        (mbase + AH, wetness, OH),
        (mbase + AH + OH, kappa[...], OH),
    ):
        up[at : at + width, :] = value[0:width]
        down[at : at + width, :] = value[rows - width : rows]
    copy_either(line, down, rows_a.at[0:halo], rows_b.at[0:halo])
    copy_either(line, up, rows_b.at[0:halo], rows_a.at[0:halo])

    cell = atm_cell[...]
    hot_atm = jnp.where(one_hot(cell % cols, cols), 1.0, 0.0).astype(BF16)
    airx = gather_rows(air[...], one_hot(cell // cols, rows), hot_atm)
    w = weight[...]
    wair = w * airx
    wair_buf[...] = wair
    copy(wair_buf, wair_out)
    cell = sea_cell[...]
    hot_sea = jnp.where(one_hot(cell % cols, cols), 1.0, 0.0).astype(BF16)
    row = dest[...] * rows + cell // cols
    tail = slice(halo, halo + 3 * rows)
    for shift in range(tiles):
        target = tile_at(shift, tiles)
        s1, s2 = scatter_rows([wair, w], one_hot(row - target * rows, rows), hot_sea)
        sums[shift, 0:rows, :] = s1
        sums[shift, rows : 2 * rows, :] = s2
        sums[shift, 2 * rows : 3 * rows, :] = ocean[0, 0]
        if len(sums_out) == 1:
            copy(sums.at[shift], sums_out[0].at[target])
        elif shift == 1:
            copy_either(line, sums.at[shift], rows_a.at[tail], rows_b.at[tail])
        elif shift == tiles - 1:
            copy_either(line, sums.at[shift], rows_b.at[tail], rows_a.at[tail])
        else:
            copy(sums.at[shift], sums_out[max(shift - 1, 0)])
    for one in used[arrived:]:
        one.wait()


def strips(cols, slot, width, left_part, right_part):
    low_half = lax.broadcasted_iota(jnp.int32, (1, cols), 1) < cols // 2
    offset = slot % cols
    a, b = right_part(slot // cols), left_part(slot // cols)
    if offset:
        a = pltpu.roll(a, cols - offset, 1)
    turn = (cols - width - offset) % cols
    if turn:
        b = pltpu.roll(b, turn, 1)
    return jnp.where(low_half, a, b)


def final_kernel(tiles, *refs):
    speed_in, atm_in, ocean_in, depth_in, kappa_in = refs[:5]
    kept = (len(refs) - 5 - 8 - 4) // 2
    sources, rest = refs[5 : 5 + kept], refs[5 + kept :]
    atm_out, ocean_out, speed, us, vs, hs, fs, ms = rest[:8]
    held, (edge, atm_buf, ocean_buf, sems) = rest[8 : 8 + kept], rest[8 + kept :]
    wet, atm_cell, dest, sea_cell, weight, wair, from_up, from_down, from_left, from_right, from_below, from_above = held[:12]
    messages = held[12:]
    levels = us.shape[0]
    each = ocean_out.shape[1]
    tracers = ocean_out.shape[0] * each
    rows, cols = atm_out.shape[2:]
    slots, lanes = lane_slots(levels, tracers)
    obase, mbase, own, halo = row_slots(levels, tracers)
    top, end = 2 * AH, 2 * AH + rows
    block = (slice(None), slice(top, end), slice(0, cols))
    rows_a, rows_b, cols_a, cols_b = sources[6:10]
    either = [(tile_parity(), rows_b, rows_a, from_up), (tile_parity(), rows_a, rows_b, from_down)]
    either += [(column_parity(), cols_b, cols_a, from_left), (column_parity(), cols_a, cols_b, from_right)]
    pairs = [pair for i, pair in enumerate(zip(sources, held)) if not 6 <= i < 10] + [(speed_in, speed)]
    pairs += [(atm_in.at[i], ref.at[block]) for i, ref in enumerate((us, vs, hs))]
    pairs += [(ocean_in.at[i], fs.at[(i, *block)]) for i in range(ocean_out.shape[0])]
    pairs += [(ref, ms.at[(i, *block[1:])]) for i, ref in ((0, depth_in), (2, kappa_in))]
    copies = [pltpu.make_async_copy(source, target, sems.at[i]) for i, (source, target) in enumerate(pairs)]
    for copy in copies:
        copy.start()
    for parity, even, odd, target in either:
        choices = [pltpu.make_async_copy(source, target, sems.at[len(copies)]) for source in (even, odd)]
        pl.when(parity == 0)(choices[0].start)
        pl.when(parity != 0)(choices[1].start)
        copies.append(choices[0])
    for copy in copies:
        copy.wait()
    corner_a, corner_b = from_below, from_above
    even_line, even_column = tile_parity() == 0, column_parity() == 0

    def message(shift, part):
        where = slice(part * rows, (part + 1) * rows)
        if len(messages) == 1:
            return messages[0][tile_at(-shift, tiles), where, :]
        if shift in (1, tiles - 1):
            return (from_up if shift == 1 else from_down)[halo + part * rows : halo + (part + 1) * rows, :]
        return messages[max(shift - 1, 0)][where, :]

    surface = fs[0, 0, top:end, 0:cols]
    cell = sea_cell[...]
    hot_sea = jnp.where(one_hot(cell % cols, cols), 1.0, 0.0).astype(BF16)
    row = dest[...] * rows + cell // cols
    s1, s2 = message(0, 0), message(0, 1)
    sstx = jnp.zeros(cell.shape, F32)
    for shift in range(tiles):
        if shift:
            s1 = s1 + message(shift, 0)
            s2 = s2 + message(shift, 1)
        sstx = sstx + gather_rows(message(shift, 2), one_hot(row - tile_at(-shift, tiles) * rows, rows), hot_sea)
    sea_flux = s1 - surface * s2
    flux = wair[...] - weight[...] * sstx
    cell = atm_cell[...]
    hot_atm = jnp.where(one_hot(cell % cols, cols), 1.0, 0.0).astype(BF16)
    (atm_flux,) = scatter_rows([flux], one_hot(cell // cols, rows), hot_atm)

    half = lanes // cols
    for i in range(2 * half):
        where = slice(i % half * cols, (i % half + 1) * cols)
        first, second = (slice(AH, 2 * AH), slice(0, AH)) if i < half else (slice(0, AH), slice(AH, 2 * AH))
        a = jnp.where(even_column, corner_a[first, where], corner_a[second, where])
        b = jnp.where(even_column, corner_b[first, where], corner_b[second, where])
        edge[i, 0:AH, :] = jnp.where(even_line, a, b)
        edge[i, AH : 2 * AH, :] = jnp.where(even_line, b, a)
        at = own + AH * i
        edge[2 * half + i, 0:AH, :] = from_down[at : at + AH, :]
        edge[2 * half + i, AH : 2 * AH, :] = from_up[at : at + AH, :]

    def extend(view, field, width):
        slot = slots[field]
        view[top:end, cols : 2 * cols] = strips(
            cols,
            slot,
            width,
            lambda t: from_left[:, t * cols : (t + 1) * cols],
            lambda t: from_right[:, t * cols : (t + 1) * cols],
        )
        both = strips(cols, slot, width, lambda t: edge[t], lambda t: edge[half + t])
        view[end : end + AH, cols : 2 * cols] = both[0:AH]
        view[top - AH : top, cols : 2 * cols] = both[AH : 2 * AH]

    def extend_rows(view, at, high):
        view[end : end + high, 0:cols] = from_down[at : at + high, :]
        view[top - high : top, 0:cols] = from_up[at : at + high, :]

    lane = lax.broadcasted_iota(jnp.int32, (2 * AH, cols), 1)
    line = lax.broadcasted_iota(jnp.int32, (2 * AH, cols), 0)
    whole_strip = (lane < AH) | (lane >= cols - AH)
    outer = (lane < AH - 1) | (lane > cols - AH)

    def near(which, level):
        at = which * levels + level
        return from_down[at : at + 1, :], from_up[at : at + 1, :]

    def extend_level(view, which, level):
        strip = strips(cols, slots[which * levels + level], AH, lambda t: edge[3 * half + t], lambda t: edge[2 * half + t])
        below, above = near(which, level)
        inner = jnp.where(line == 0, below, jnp.where(line == 2 * AH - 1, above, 0.0))
        both = jnp.where(whole_strip if which == 0 else outer, strip, inner)
        view[end : end + AH, 0:cols] = both[0:AH]
        view[top - AH : top, 0:cols] = both[AH : 2 * AH]

    def new_height_rows(view, level):
        below, above = near(3, level), near(4, level)
        here = ((line[0:AH] == 1) | (line[0:AH] == 2)) & jnp.logical_not(outer[0:AH])
        for at, one, two in ((end, below[0], above[0]), (top - AH, above[1], below[1])):
            sent = jnp.where(line[0:AH] == 1, one, two)
            view[at : at + AH, 0:cols] = jnp.where(here, sent, view[at : at + AH, 0:cols])

    def east(f):
        return pltpu.roll(f, 2 * cols - 1, 1)

    def west(f):
        return pltpu.roll(f, 1, 1)

    wide, inner = (top - AH, rows + 2 * AH), (top, rows)

    def rows_of(window, shift=0):
        return slice(window[0] + shift, window[0] + shift + window[1])

    base = 3 * levels + tracers
    ms[1, top:end, 0:cols] = wet[...].astype(F32)
    for i, (at, high) in enumerate(((mbase, AH), (mbase + AH, OH), (mbase + AH + OH, OH))):
        extend(ms.at[i], base + i, AH)
        extend_rows(ms.at[i], at, high)
    for i in range(tracers):
        extend(fs.at[i // each, i % each], 3 * levels + i, OH)
        extend_rows(fs.at[i // each, i % each], obase + OH * i, OH)
    for level in range(levels):
        for which, ref in enumerate((us, vs, hs)):
            extend(ref.at[level], which * levels + level, AH)
            extend_level(ref.at[level], which, level)

    here, lower, upper = rows_of(wide), rows_of(wide, 1), rows_of(wide, -1)
    w = ms[1, here]
    kw = ms[2, here] * w
    weights = (kw * east(w), kw * west(w), kw * ms[1, lower], kw * ms[1, upper])
    for i, weight_of in enumerate(weights):
        ms[3 + i, here] = weight_of
    ms[7, here] = 1.0 - (weights[0] + weights[1] + weights[2] + weights[3])
    for step in range(OCEAN_STEPS):
        window = wide if step < OCEAN_STEPS - 1 else inner
        here, lower, upper = rows_of(window), rows_of(window, 1), rows_of(window, -1)
        ce, cw, cs, cn, center = [ms[3 + i, here] for i in range(5)]
        for i in range(tracers):
            view = fs.at[i // each, i % each]
            f = view[here]
            f = center * f + ce * east(f) + cw * west(f) + cs * view[lower] + cn * view[upper]
            if step < OCEAN_STEPS - 1:
                view[here] = f
            else:
                f = f[:, 0:cols]
                ocean_buf[i // each, i % each] = f + SEA_GAIN * sea_flux if i == 0 else f
    used = len(copies)
    copies = [pltpu.make_async_copy(ocean_buf, ocean_out, sems.at[used])]
    copies[0].start()

    d = 0.5 * ms[0, rows_of(wide)]
    chunk = max(1, levels // 4)
    for step in range(ACOUSTIC):
        here, lower, upper = rows_of(wide), rows_of(wide, 1), rows_of(wide, -1)
        for level in range(levels):
            u = us[level, here]
            turning = (east(u) - west(u)) + (vs[level, lower] - vs[level, upper])
            hs[level, here] = hs[level, here] - (speed[level] * d) * turning
            if step == 0:
                new_height_rows(hs.at[level], level)
        window = wide if step < ACOUSTIC - 1 else inner
        here, lower, upper = rows_of(window), rows_of(window, 1), rows_of(window, -1)
        for level in range(levels):
            h = hs[level, here]
            u = us[level, here] - (east(h) - west(h)) * 0.5
            v = vs[level, here] - (hs[level, lower] - hs[level, upper]) * 0.5
            if step < ACOUSTIC - 1:
                us[level, here], vs[level, here] = u, v
            else:
                h = h[:, 0:cols]
                atm_buf[0, level] = u[:, 0:cols]
                atm_buf[1, level] = v[:, 0:cols]
                atm_buf[2, level] = h - ATM_GAIN * atm_flux if level == levels - 1 else h
                if (level + 1) % chunk == 0:
                    where = pl.ds(level + 1 - chunk, chunk)
                    copies.append(
                        pltpu.make_async_copy(
                            atm_buf.at[:, where], atm_out.at[:, where], sems.at[used + len(copies)]
                        )
                    )
                    copies[-1].start()
    for copy in copies:
        copy.wait()


def on_device(
    tile_count,
    atm_state,
    air_temp,
    depth,
    wave_speed,
    ocean_state,
    wet_mask,
    diffusivity,
    xg_atm_cell,
    xg_dest,
    xg_ocean_cell,
    xg_weight,
):
    levels = atm_state.shape[1]
    rows, cols = atm_state.shape[2:]
    tracers = ocean_state.shape[0] * ocean_state.shape[1]
    cells = xg_weight.shape[-1]
    _, lanes = lane_slots(levels, tracers)
    _, _, _, halo = row_slots(levels, tracers)
    message_rows = halo
    vmem = pl.BlockSpec(memory_space=pltpu.VMEM)
    hbm = pl.BlockSpec(memory_space=pltpu.HBM)
    whole = pltpu.CompilerParams(vmem_limit_bytes=64 * 1024 * 1024)
    full = rows + 4 * AH

    def shape(*dims):
        return jax.ShapeDtypeStruct(dims, F32)

    by_shift = tile_count <= 4
    if by_shift:
        message_rows += 3 * rows
        sums = [shape(3 * rows, cols)] * (tile_count - 2)
    else:
        sums = [shape(tile_count, 3 * rows, cols)]
    atm_cell = xg_atm_cell.reshape(1, cells)
    dest = xg_dest.reshape(1, cells)
    sea_cell = xg_ocean_cell.reshape(1, cells)
    weight = xg_weight.reshape(1, cells)
    operands = (atm_state, ocean_state, depth, wet_mask, diffusivity, air_temp, atm_cell, dest, sea_cell, weight)
    operands += (wave_speed,)
    cols_a, cols_b, rows_a, rows_b, wair, *messages = pl.pallas_call(
        functools.partial(first_kernel, tile_count),
        out_shape=[shape(rows, lanes)] * 2 + [shape(message_rows, cols)] * 2 + [shape(1, cells)] + sums,
        in_specs=[hbm] * 11,
        out_specs=[hbm] * (5 + len(sums)),
        scratch_shapes=[pltpu.VMEM(x.shape, x.dtype) for x in operands[:-1]]
        + [pltpu.SMEM(wave_speed.shape, F32)]
        + [pltpu.VMEM((halo, cols), F32)] * 2
        + [pltpu.VMEM((rows, lanes), F32)] * 2
        + [
            pltpu.VMEM((1, cells), F32),
            pltpu.VMEM((tile_count, 3 * rows, cols), F32),
            pltpu.SemaphoreType.DMA((16 + tile_count,)),
        ],
        compiler_params=whole,
        name="first",
    )(*operands)

    column_axes = ("sub", "comp")
    column_count = lax.axis_size("sub") * lax.axis_size("comp")

    def shift(value, axes, count, by):
        return lax.ppermute(value, axes, [(i, (i + by) % count) for i in range(count)])

    def swap(value, axes, count, odd):
        return lax.ppermute(value, axes, [(i, (i + (1 if (i + odd) % 2 == 0 else -1)) % count) for i in range(count)])

    got_a = swap(cols_a, column_axes, column_count, 0)
    got_b = swap(cols_b, column_axes, column_count, 1)
    near_a = swap(rows_a, "tile", tile_count, 1)
    near_b = swap(rows_b, "tile", tile_count, 0)

    low = jnp.where(tile_parity() == 0, rows - AH, 0)
    corner_a, corner_b = [
        jnp.concatenate([lax.dynamic_slice_in_dim(x, at, AH) for x in (got_a, got_b)]) for at in (low, rows - AH - low)
    ]
    corner_a = swap(corner_a, "tile", tile_count, 1)
    corner_b = swap(corner_b, "tile", tile_count, 0)
    if by_shift:
        got = messages[:1] + [shift(messages[s - 1], "tile", tile_count, s) for s in range(2, tile_count - 1)]
    else:
        got = [lax.all_to_all(messages[0], "tile", split_axis=0, concat_axis=0, tiled=True)]

    operands = (wave_speed, atm_state, ocean_state, depth, diffusivity)
    operands += (wet_mask, atm_cell, dest, sea_cell, weight, wair, near_a, near_b, got_a, got_b)
    operands += (corner_a, corner_b, *got)
    return tuple(
        pl.pallas_call(
            functools.partial(final_kernel, tile_count),
            out_shape=[shape(*atm_state.shape), shape(*ocean_state.shape)],
            in_specs=[hbm] * len(operands),
            out_specs=[hbm] * 2,
            scratch_shapes=[pltpu.SMEM(wave_speed.shape, F32)]
            + [pltpu.VMEM((levels, full, 2 * cols), F32)] * 3
            + [
                pltpu.VMEM((*ocean_state.shape[:2], full, 2 * cols), F32),
                pltpu.VMEM((8, full, 2 * cols), F32),
            ]
            + [pltpu.VMEM(x.shape, x.dtype) for x in operands[5:]]
            + [
                pltpu.VMEM((4 * (lanes // cols), 2 * AH, cols), F32),
                pltpu.VMEM(atm_state.shape, F32),
                pltpu.VMEM(ocean_state.shape, F32),
                pltpu.SemaphoreType.DMA((len(operands) + 10,)),
            ],
            compiler_params=whole,
            name="steps",
        )(*operands)
    )


def solution(mesh):
    grid = P(("member", "tile"), ("sub", "comp"))
    state = P(None, None, ("member", "tile"), ("sub", "comp"))
    cells = P(("member", "tile"), ("sub", "comp"), None)
    return jax.shard_map(
        functools.partial(on_device, mesh.shape["tile"]),
        mesh=mesh,
        in_specs=(
            state,
            grid,
            grid,
            P(),
            state,
            grid,
            grid,
            cells,
            P(("member", "tile"), ("sub", "comp"), None, None),
            cells,
            cells,
        ),
        out_specs=(state, state),
        check_vma=False,
    )
```

```python
import functools

import jax
import jax.numpy as jnp
from jax import lax
from jax.experimental import pallas as pl
from jax.experimental.pallas import tpu as pltpu
from jax.sharding import PartitionSpec as P

ACOUSTIC = 2
OCEAN_STEPS = 2
AH = 2 * ACOUSTIC
OH = OCEAN_STEPS

ATM_GAIN = 0.5
SEA_GAIN = 0.5

F32 = jnp.float32
BF16 = jnp.bfloat16


def lane_slots(levels, tracers):
    slots = [AH * i for i in range(3 * levels)]
    base = AH * 3 * levels
    slots += [base + OH * i for i in range(tracers)]
    base += OH * tracers
    slots += [base + AH * i for i in range(3)]
    total = base + 3 * AH
    return slots, -(-total // 128) * 128


def row_slots(levels, tracers):
    tracer = 5 * levels
    misc = tracer + OH * tracers
    own = misc + AH + 2 * OH
    _, lanes = lane_slots(levels, tracers)
    return tracer, misc, own, own + 2 * AH * (lanes // 128)


def near_rows(u, v, h, speed, rows, cols):
    east_west = (pltpu.roll(u, cols - 1, 1) - pltpu.roll(u, 1, 1)) * 0.5
    south_north = (pltpu.roll(v, rows - 1, 0) - pltpu.roll(v, 1, 0)) * 0.5
    h1 = h - speed * (east_west + south_north)
    out = []
    for near, turn in ((0, 1), (rows - 1, -1)):
        at = [slice(near + turn * i, near + turn * i + 1) for i in range(3)]
        out.append(
            (
                u[at[0]],
                v[at[0]],
                h[at[0]] - (0.5 * turn) * speed[at[0]] * v[at[1]],
                h1[at[1]],
                h1[at[2]] - (2.0 * turn) * v[at[1]],
            )
        )
    return out


def split3(value):
    hi = value.astype(BF16)
    rest = value - hi.astype(F32)
    mid = rest.astype(BF16)
    low = (rest - mid.astype(F32)).astype(BF16)
    return hi, mid, low


def one_hot(index, size):
    shape = (size, index.shape[-1])
    return lax.broadcasted_iota(jnp.int32, shape, 0) == index


def gather_rows(table, hot_rows, hot_cols):
    r = table.shape[0]
    parts = jnp.concatenate(split3(table), axis=0)
    g = jnp.dot(parts, hot_cols, preferred_element_type=F32)
    g = g[0:r] + g[r : 2 * r] + g[2 * r : 3 * r]
    return jnp.sum(jnp.where(hot_rows, g, 0.0), axis=0, keepdims=True)


def scatter_rows(values, hot_rows, hot_cols):
    r = hot_rows.shape[0]
    hot = jnp.where(hot_rows, 1.0, 0.0).astype(BF16)
    parts = [hot * part for value in values for part in split3(value)]
    s = lax.dot_general(
        jnp.concatenate(parts, axis=0),
        hot_cols,
        (((1,), (1,)), ((), ())),
        preferred_element_type=F32,
    )
    out = []
    for i in range(len(values)):
        base = 3 * r * i
        out.append(s[base : base + r] + s[base + r : base + 2 * r] + s[base + 2 * r : base + 3 * r])
    return out


def tile_at(shift, tiles):
    return lax.rem(lax.axis_index("tile") + shift % tiles, tiles)


def tile_parity():
    return lax.rem(lax.axis_index("tile") + 1, 2)


def column_parity():
    return lax.rem(lax.axis_index(("sub", "comp")), 2)


def first_kernel(tiles, *refs):
    sources, (cols_a, cols_b, rows_a, rows_b, wair_out, *sums_out) = refs[:11], refs[11:-18]
    held, (up, down, left, right, wair_buf, sums, sems) = refs[-18:-7], refs[-7:]
    atm, ocean, depth, wet, kappa, air, atm_cell, dest, sea_cell, weight, wave_speed = held
    used = []

    def copy(source, target):
        used.append(pltpu.make_async_copy(source, target, sems.at[len(used)]))
        used[-1].start()

    def copy_either(parity, source, even, odd):
        choices = [pltpu.make_async_copy(source, target, sems.at[len(used)]) for target in (even, odd)]
        pl.when(parity == 0)(choices[0].start)
        pl.when(parity != 0)(choices[1].start)
        used.append(choices[0])

    column, line = column_parity(), tile_parity()
    for source, target in zip(sources, held):
        copy(source, target)
    levels = atm.shape[1]
    rows, cols = atm.shape[2:]
    tracers = ocean.shape[0] * ocean.shape[1]
    each = ocean.shape[1]
    obase, mbase, own, halo = row_slots(levels, tracers)
    slots, _ = lane_slots(levels, tracers)
    for one in used:
        one.wait()
    arrived = len(used)
    cell = atm_cell[...]
    hot_atm = jnp.where(one_hot(cell % cols, cols), 1.0, 0.0).astype(BF16)
    airx = gather_rows(air[...], one_hot(cell // cols, rows), hot_atm)
    w = weight[...]
    wair = w * airx
    wair_buf[...] = wair
    copy(wair_buf, wair_out)

    wetness = wet[...].astype(F32)

    lane = lax.broadcasted_iota(jnp.int32, (rows, cols), 1)
    fields = [(atm, (k, l), AH) for k in range(3) for l in range(levels)]
    fields += [(ocean, (i // each, i % each), OH) for i in range(tracers)]
    fields += [(depth, None, AH), (None, None, AH), (kappa, None, AH)]
    packed = {}
    for (ref, at, width), slot in zip(fields, slots):
        value = wetness if ref is None else (ref[...] if at is None else ref[at[0], at[1]])
        tile, offset = slot // cols, slot % cols
        mask = (lane >= offset) & (lane < offset + width)
        first = pltpu.roll(value, offset, 1) if offset else value
        turn = (offset + width) % cols
        last = pltpu.roll(value, turn, 1) if turn else value
        if tile in packed:
            a, b = packed[tile]
            packed[tile] = (jnp.where(mask, first, a), jnp.where(mask, last, b))
        else:
            packed[tile] = (first, last)
    for tile, (a, b) in packed.items():
        where = slice(tile * cols, (tile + 1) * cols)
        left[:, where] = a
        right[:, where] = b

    copy_either(column, right, cols_a, cols_b)
    copy_either(column, left, cols_b, cols_a)

    for level in range(levels):
        speed = wave_speed[level] * depth[...]
        both = near_rows(atm[0, level], atm[1, level], atm[2, level], speed, rows, cols)
        for ref, values in zip((up, down), both):
            for i, value in enumerate(values):
                at = i * levels + level
                ref[at : at + 1, :] = value
    at = own
    for strip in (left, right):
        for i in range(strip.shape[1] // cols):
            where = slice(i * cols, (i + 1) * cols)
            up[at : at + AH, :] = strip[0:AH, where]
            down[at : at + AH, :] = strip[rows - AH : rows, where]
            at += AH
    for i in range(tracers):
        at = obase + OH * i
        up[at : at + OH, :] = ocean[i // each, i % each, 0:OH, :]
        down[at : at + OH, :] = ocean[i // each, i % each, rows - OH : rows, :]
    for at, value, width in (
        (mbase, depth[...], AH),
        (mbase + AH, wetness, OH),
        (mbase + AH + OH, kappa[...], OH),
    ):
        up[at : at + width, :] = value[0:width]
        down[at : at + width, :] = value[rows - width : rows]
    copy_either(line, down, rows_a.at[0:halo], rows_b.at[0:halo])
    copy_either(line, up, rows_b.at[0:halo], rows_a.at[0:halo])

    cell = sea_cell[...]
    hot_sea = jnp.where(one_hot(cell % cols, cols), 1.0, 0.0).astype(BF16)
    row = dest[...] * rows + cell // cols
    tail = slice(halo, halo + 3 * rows)
    for shift in range(tiles):
        target = tile_at(shift, tiles)
        s1, s2 = scatter_rows([wair, w], one_hot(row - target * rows, rows), hot_sea)
        sums[shift, 0:rows, :] = s1
        sums[shift, rows : 2 * rows, :] = s2
        sums[shift, 2 * rows : 3 * rows, :] = ocean[0, 0]
        if len(sums_out) == 1:
            copy(sums.at[shift], sums_out[0].at[target])
        elif shift == 1:
            copy_either(line, sums.at[shift], rows_a.at[tail], rows_b.at[tail])
        elif shift == tiles - 1:
            copy_either(line, sums.at[shift], rows_b.at[tail], rows_a.at[tail])
        else:
            copy(sums.at[shift], sums_out[max(shift - 1, 0)])
    for one in used[arrived:]:
        one.wait()


def strips(cols, slot, width, left_part, right_part):
    low_half = lax.broadcasted_iota(jnp.int32, (1, cols), 1) < cols // 2
    offset = slot % cols
    a, b = right_part(slot // cols), left_part(slot // cols)
    if offset:
        a = pltpu.roll(a, cols - offset, 1)
    turn = (cols - width - offset) % cols
    if turn:
        b = pltpu.roll(b, turn, 1)
    return jnp.where(low_half, a, b)


def final_kernel(tiles, *refs):
    speed_in, atm_in, ocean_in, depth_in, kappa_in = refs[:5]
    kept = (len(refs) - 5 - 8 - 4) // 2
    sources, rest = refs[5 : 5 + kept], refs[5 + kept :]
    atm_out, ocean_out, speed, us, vs, hs, fs, ms = rest[:8]
    held, (edge, atm_buf, ocean_buf, sems) = rest[8 : 8 + kept], rest[8 + kept :]
    wet, atm_cell, dest, sea_cell, weight, wair, from_up, from_down, from_left, from_right, from_below, from_above = held[:12]
    messages = held[12:]
    levels = us.shape[0]
    each = ocean_out.shape[1]
    tracers = ocean_out.shape[0] * each
    rows, cols = atm_out.shape[2:]
    slots, lanes = lane_slots(levels, tracers)
    obase, mbase, own, halo = row_slots(levels, tracers)
    full = rows + 2 * AH
    block = (slice(None), slice(0, rows), slice(0, cols))
    rows_a, rows_b, cols_a, cols_b = sources[6:10]
    either = [(tile_parity(), rows_b, rows_a, from_up), (tile_parity(), rows_a, rows_b, from_down)]
    either += [(column_parity(), cols_b, cols_a, from_left), (column_parity(), cols_a, cols_b, from_right)]
    pairs = [pair for i, pair in enumerate(zip(sources, held)) if not 6 <= i < 10] + [(speed_in, speed)]
    pairs += [(atm_in.at[i], ref.at[block]) for i, ref in enumerate((us, vs, hs))]
    pairs += [(ocean_in.at[i], fs.at[(i, *block)]) for i in range(ocean_out.shape[0])]
    pairs += [(ref, ms.at[(i, *block[1:])]) for i, ref in ((0, depth_in), (2, kappa_in))]
    copies = [pltpu.make_async_copy(source, target, sems.at[i]) for i, (source, target) in enumerate(pairs)]
    for copy in copies:
        copy.start()
    for parity, even, odd, target in either:
        choices = [pltpu.make_async_copy(source, target, sems.at[len(copies)]) for source in (even, odd)]
        pl.when(parity == 0)(choices[0].start)
        pl.when(parity != 0)(choices[1].start)
        copies.append(choices[0])
    for copy in copies:
        copy.wait()
    corner_a, corner_b = from_below, from_above
    even_line, even_column = tile_parity() == 0, column_parity() == 0

    def message(shift, part):
        where = slice(part * rows, (part + 1) * rows)
        if len(messages) == 1:
            return messages[0][tile_at(-shift, tiles), where, :]
        if shift in (1, tiles - 1):
            return (from_up if shift == 1 else from_down)[halo + part * rows : halo + (part + 1) * rows, :]
        return messages[max(shift - 1, 0)][where, :]

    surface = fs[0, 0, 0:rows, 0:cols]
    cell = sea_cell[...]
    hot_sea = jnp.where(one_hot(cell % cols, cols), 1.0, 0.0).astype(BF16)
    row = dest[...] * rows + cell // cols
    s1, s2 = message(0, 0), message(0, 1)
    for shift in range(1, tiles):
        s1 = s1 + message(shift, 0)
        s2 = s2 + message(shift, 1)
    sea_flux = s1 - surface * s2

    half = lanes // cols
    for i in range(2 * half):
        where = slice(i % half * cols, (i % half + 1) * cols)
        first, second = (slice(AH, 2 * AH), slice(0, AH)) if i < half else (slice(0, AH), slice(AH, 2 * AH))
        a = jnp.where(even_column, corner_a[first, where], corner_a[second, where])
        b = jnp.where(even_column, corner_b[first, where], corner_b[second, where])
        edge[i, 0:AH, :] = jnp.where(even_line, a, b)
        edge[i, AH : 2 * AH, :] = jnp.where(even_line, b, a)
        at = own + AH * i
        edge[2 * half + i, 0:AH, :] = from_down[at : at + AH, :]
        edge[2 * half + i, AH : 2 * AH, :] = from_up[at : at + AH, :]

    def extend(view, field, width):
        slot = slots[field]
        view[0:rows, cols : 2 * cols] = strips(
            cols,
            slot,
            width,
            lambda t: from_left[:, t * cols : (t + 1) * cols],
            lambda t: from_right[:, t * cols : (t + 1) * cols],
        )
        view[rows:full, cols : 2 * cols] = strips(cols, slot, width, lambda t: edge[t], lambda t: edge[half + t])

    def extend_rows(view, at, high):
        view[rows : rows + high, 0:cols] = from_down[at : at + high, :]
        view[full - high : full, 0:cols] = from_up[at : at + high, :]

    lane = lax.broadcasted_iota(jnp.int32, (2 * AH, cols), 1)
    line = lax.broadcasted_iota(jnp.int32, (2 * AH, cols), 0)
    whole_strip = (lane < AH) | (lane >= cols - AH)
    outer = (lane < AH - 1) | (lane > cols - AH)

    def near(which, level):
        at = which * levels + level
        return from_down[at : at + 1, :], from_up[at : at + 1, :]

    def extend_level(view, which, level):
        strip = strips(cols, slots[which * levels + level], AH, lambda t: edge[3 * half + t], lambda t: edge[2 * half + t])
        below, above = near(which, level)
        inner = jnp.where(line == 0, below, jnp.where(line == 2 * AH - 1, above, 0.0))
        view[rows:full, 0:cols] = jnp.where(whole_strip if which == 0 else outer, strip, inner)

    def new_height_rows(tile, level):
        below, above = near(3, level), near(4, level)
        sent = jnp.where(
            line == 1, below[0], jnp.where(line == 2, above[0], jnp.where(line == 2 * AH - 3, above[1], below[1]))
        )
        here = (line == 1) | (line == 2) | (line == 2 * AH - 3) | (line == 2 * AH - 2)
        return jnp.where(here & jnp.logical_not(outer), sent, tile)

    def east(f):
        return pltpu.roll(f, 2 * cols - 1, 1)

    def west(f):
        return pltpu.roll(f, 1, 1)

    def south(f):
        return pltpu.roll(f, full - 1, 0)

    def north(f):
        return pltpu.roll(f, 1, 0)

    base = 3 * levels + tracers
    ms[1, 0:rows, 0:cols] = wet[...].astype(F32)
    for i, (at, high) in enumerate(((mbase, AH), (mbase + AH, OH), (mbase + AH + OH, OH))):
        extend(ms.at[i], base + i, AH)
        extend_rows(ms.at[i], at, high)
    sstx = jnp.zeros(cell.shape, F32)
    for shift in range(tiles):
        sstx = sstx + gather_rows(message(shift, 2), one_hot(row - tile_at(-shift, tiles) * rows, rows), hot_sea)
        for i in range(tracers * shift // tiles, tracers * (shift + 1) // tiles):
            extend(fs.at[i // each, i % each], 3 * levels + i, OH)
            extend_rows(fs.at[i // each, i % each], obase + OH * i, OH)
        for level in range(levels * shift // tiles, levels * (shift + 1) // tiles):
            for which, ref in enumerate((us, vs, hs)):
                extend(ref.at[level], which * levels + level, AH)
                extend_level(ref.at[level], which, level)
    flux = wair[...] - weight[...] * sstx
    cell = atm_cell[...]
    hot_atm = jnp.where(one_hot(cell % cols, cols), 1.0, 0.0).astype(BF16)

    w = ms[1]
    k = ms[2]
    kw = k * w
    ce, cw, cs, cn = kw * east(w), kw * west(w), kw * south(w), kw * north(w)
    center = 1.0 - (ce + cw + cs + cn)
    for step in range(OCEAN_STEPS):
        if step == OCEAN_STEPS - 1:
            (atm_flux,) = scatter_rows([flux], one_hot(cell // cols, rows), hot_atm)
        for i in range(tracers):
            f = fs[i // each, i % each]
            f = center * f + ce * east(f) + cw * west(f) + cs * south(f) + cn * north(f)
            if step < OCEAN_STEPS - 1:
                fs[i // each, i % each] = f
            else:
                f = f[0:rows, 0:cols]
                ocean_buf[i // each, i % each] = f + SEA_GAIN * sea_flux if i == 0 else f
    used = len(copies)
    copies = [pltpu.make_async_copy(ocean_buf, ocean_out, sems.at[used])]
    copies[0].start()

    d = 0.5 * ms[0]
    chunk = max(1, levels // 4)
    for step in range(ACOUSTIC):
        for level in range(levels):
            u, v, h = us[level], vs[level], hs[level]
            hs[level] = h - (speed[level] * d) * ((east(u) - west(u)) + (south(v) - north(v)))
            if step == 0:
                hs[level, rows:full, 0:cols] = new_height_rows(hs[level, rows:full, 0:cols], level)
        for level in range(levels):
            u, v, h = us[level], vs[level], hs[level]
            u = u - (east(h) - west(h)) * 0.5
            v = v - (south(h) - north(h)) * 0.5
            if step < ACOUSTIC - 1:
                us[level], vs[level] = u, v
            else:
                h = h[0:rows, 0:cols]
                atm_buf[0, level] = u[0:rows, 0:cols]
                atm_buf[1, level] = v[0:rows, 0:cols]
                atm_buf[2, level] = h - ATM_GAIN * atm_flux if level == levels - 1 else h
                if (level + 1) % chunk == 0:
                    where = pl.ds(level + 1 - chunk, chunk)
                    copies.append(
                        pltpu.make_async_copy(
                            atm_buf.at[:, where], atm_out.at[:, where], sems.at[used + len(copies)]
                        )
                    )
                    copies[-1].start()
    for copy in copies:
        copy.wait()


def on_device(
    tile_count,
    atm_state,
    air_temp,
    depth,
    wave_speed,
    ocean_state,
    wet_mask,
    diffusivity,
    xg_atm_cell,
    xg_dest,
    xg_ocean_cell,
    xg_weight,
):
    levels = atm_state.shape[1]
    rows, cols = atm_state.shape[2:]
    tracers = ocean_state.shape[0] * ocean_state.shape[1]
    cells = xg_weight.shape[-1]
    _, lanes = lane_slots(levels, tracers)
    _, _, _, halo = row_slots(levels, tracers)
    message_rows = halo
    vmem = pl.BlockSpec(memory_space=pltpu.VMEM)
    hbm = pl.BlockSpec(memory_space=pltpu.HBM)
    whole = pltpu.CompilerParams(vmem_limit_bytes=64 * 1024 * 1024)
    full = rows + 2 * AH

    def shape(*dims):
        return jax.ShapeDtypeStruct(dims, F32)

    by_shift = tile_count <= 4
    if by_shift:
        message_rows += 3 * rows
        sums = [shape(3 * rows, cols)] * (tile_count - 2)
    else:
        sums = [shape(tile_count, 3 * rows, cols)]
    atm_cell = xg_atm_cell.reshape(1, cells)
    dest = xg_dest.reshape(1, cells)
    sea_cell = xg_ocean_cell.reshape(1, cells)
    weight = xg_weight.reshape(1, cells)
    operands = (atm_state, ocean_state, depth, wet_mask, diffusivity, air_temp, atm_cell, dest, sea_cell, weight)
    operands += (wave_speed,)
    cols_a, cols_b, rows_a, rows_b, wair, *messages = pl.pallas_call(
        functools.partial(first_kernel, tile_count),
        out_shape=[shape(rows, lanes)] * 2 + [shape(message_rows, cols)] * 2 + [shape(1, cells)] + sums,
        in_specs=[hbm] * 11,
        out_specs=[hbm] * (5 + len(sums)),
        scratch_shapes=[pltpu.VMEM(x.shape, x.dtype) for x in operands[:-1]]
        + [pltpu.SMEM(wave_speed.shape, F32)]
        + [pltpu.VMEM((halo, cols), F32)] * 2
        + [pltpu.VMEM((rows, lanes), F32)] * 2
        + [
            pltpu.VMEM((1, cells), F32),
            pltpu.VMEM((tile_count, 3 * rows, cols), F32),
            pltpu.SemaphoreType.DMA((16 + tile_count,)),
        ],
        compiler_params=whole,
        name="first",
    )(*operands)

    column_axes = ("sub", "comp")
    column_count = lax.axis_size("sub") * lax.axis_size("comp")

    def shift(value, axes, count, by):
        return lax.ppermute(value, axes, [(i, (i + by) % count) for i in range(count)])

    def swap(value, axes, count, odd):
        return lax.ppermute(value, axes, [(i, (i + (1 if (i + odd) % 2 == 0 else -1)) % count) for i in range(count)])

    got_a = swap(cols_a, column_axes, column_count, 0)
    got_b = swap(cols_b, column_axes, column_count, 1)
    near_a = swap(rows_a, "tile", tile_count, 1)
    near_b = swap(rows_b, "tile", tile_count, 0)

    low = jnp.where(tile_parity() == 0, rows - AH, 0)
    corner_a, corner_b = [
        jnp.concatenate([lax.dynamic_slice_in_dim(x, at, AH) for x in (got_a, got_b)]) for at in (low, rows - AH - low)
    ]
    corner_a = swap(corner_a, "tile", tile_count, 1)
    corner_b = swap(corner_b, "tile", tile_count, 0)
    if by_shift:
        got = messages[:1] + [shift(messages[s - 1], "tile", tile_count, s) for s in range(2, tile_count - 1)]
    else:
        got = [lax.all_to_all(messages[0], "tile", split_axis=0, concat_axis=0, tiled=True)]

    operands = (wave_speed, atm_state, ocean_state, depth, diffusivity)
    operands += (wet_mask, atm_cell, dest, sea_cell, weight, wair, near_a, near_b, got_a, got_b)
    operands += (corner_a, corner_b, *got)
    return tuple(
        pl.pallas_call(
            functools.partial(final_kernel, tile_count),
            out_shape=[shape(*atm_state.shape), shape(*ocean_state.shape)],
            in_specs=[hbm] * len(operands),
            out_specs=[hbm] * 2,
            scratch_shapes=[pltpu.SMEM(wave_speed.shape, F32)]
            + [pltpu.VMEM((levels, full, 2 * cols), F32)] * 3
            + [
                pltpu.VMEM((*ocean_state.shape[:2], full, 2 * cols), F32),
                pltpu.VMEM((3, full, 2 * cols), F32),
            ]
            + [pltpu.VMEM(x.shape, x.dtype) for x in operands[5:]]
            + [
                pltpu.VMEM((4 * (lanes // cols), 2 * AH, cols), F32),
                pltpu.VMEM(atm_state.shape, F32),
                pltpu.VMEM(ocean_state.shape, F32),
                pltpu.SemaphoreType.DMA((len(operands) + 10,)),
            ],
            compiler_params=whole,
            name="steps",
        )(*operands)
    )


def solution(mesh):
    grid = P(("member", "tile"), ("sub", "comp"))
    state = P(None, None, ("member", "tile"), ("sub", "comp"))
    cells = P(("member", "tile"), ("sub", "comp"), None)
    return jax.shard_map(
        functools.partial(on_device, mesh.shape["tile"]),
        mesh=mesh,
        in_specs=(
            state,
            grid,
            grid,
            P(),
            state,
            grid,
            grid,
            cells,
            P(("member", "tile"), ("sub", "comp"), None, None),
            cells,
            cells,
        ),
        out_specs=(state, state),
        check_vma=False,
    )
```

```python
import functools

import jax
import jax.numpy as jnp
from jax import lax
from jax.experimental import pallas as pl
from jax.experimental.pallas import tpu as pltpu
from jax.sharding import PartitionSpec as P

ACOUSTIC = 2
OCEAN_STEPS = 2
AH = 2 * ACOUSTIC
OH = OCEAN_STEPS

ATM_GAIN = 0.5
SEA_GAIN = 0.5

F32 = jnp.float32
BF16 = jnp.bfloat16


def lane_slots(levels, tracers):
    slots = [AH * i for i in range(3 * levels)]
    base = AH * 3 * levels
    slots += [base + OH * i for i in range(tracers)]
    base += OH * tracers
    slots += [base + AH * i for i in range(3)]
    total = base + 3 * AH
    return slots, -(-total // 128) * 128


def row_slots(levels, tracers):
    tracer = 5 * levels
    misc = tracer + OH * tracers
    own = misc + AH + 2 * OH
    _, lanes = lane_slots(levels, tracers)
    return tracer, misc, own, own + 2 * AH * (lanes // 128)


def near_rows(u, v, h, speed, rows, cols):
    east_west = (pltpu.roll(u, cols - 1, 1) - pltpu.roll(u, 1, 1)) * 0.5
    south_north = (pltpu.roll(v, rows - 1, 0) - pltpu.roll(v, 1, 0)) * 0.5
    h1 = h - speed * (east_west + south_north)
    out = []
    for near, turn in ((0, 1), (rows - 1, -1)):
        at = [slice(near + turn * i, near + turn * i + 1) for i in range(3)]
        out.append(
            (
                u[at[0]],
                v[at[0]],
                h[at[0]] - (0.5 * turn) * speed[at[0]] * v[at[1]],
                h1[at[1]],
                h1[at[2]] - (2.0 * turn) * v[at[1]],
            )
        )
    return out


def split3(value):
    hi = value.astype(BF16)
    rest = value - hi.astype(F32)
    mid = rest.astype(BF16)
    low = (rest - mid.astype(F32)).astype(BF16)
    return hi, mid, low


def one_hot(index, size):
    shape = (size, index.shape[-1])
    return lax.broadcasted_iota(jnp.int32, shape, 0) == index


def gather_rows(table, hot_rows, hot_cols):
    r = table.shape[0]
    parts = jnp.concatenate(split3(table), axis=0)
    g = jnp.dot(parts, hot_cols, preferred_element_type=F32)
    g = g[0:r] + g[r : 2 * r] + g[2 * r : 3 * r]
    return jnp.sum(jnp.where(hot_rows, g, 0.0), axis=0, keepdims=True)


def scatter_rows(values, hot_rows, hot_cols):
    r = hot_rows.shape[0]
    hot = jnp.where(hot_rows, 1.0, 0.0).astype(BF16)
    parts = [hot * part for value in values for part in split3(value)]
    s = lax.dot_general(
        jnp.concatenate(parts, axis=0),
        hot_cols,
        (((1,), (1,)), ((), ())),
        preferred_element_type=F32,
    )
    out = []
    for i in range(len(values)):
        base = 3 * r * i
        out.append(s[base : base + r] + s[base + r : base + 2 * r] + s[base + 2 * r : base + 3 * r])
    return out


def tile_at(shift, tiles):
    return lax.rem(lax.axis_index("tile") + shift % tiles, tiles)


def tile_parity():
    return lax.rem(lax.axis_index("tile") + 1, 2)


def column_parity():
    return lax.rem(lax.axis_index(("sub", "comp")), 2)


def first_kernel(tiles, *refs):
    sources, (cols_a, cols_b, rows_a, rows_b, wair_out, *sums_out) = refs[:11], refs[11:-18]
    held, (up, down, left, right, wair_buf, sums, sems) = refs[-18:-7], refs[-7:]
    atm, ocean, depth, wet, kappa, air, atm_cell, dest, sea_cell, weight, wave_speed = held
    used = []

    def copy(source, target):
        used.append(pltpu.make_async_copy(source, target, sems.at[len(used)]))
        used[-1].start()

    def copy_either(parity, source, even, odd):
        choices = [pltpu.make_async_copy(source, target, sems.at[len(used)]) for target in (even, odd)]
        pl.when(parity == 0)(choices[0].start)
        pl.when(parity != 0)(choices[1].start)
        used.append(choices[0])

    column, line = column_parity(), tile_parity()
    for source, target in zip(sources, held):
        copy(source, target)
    levels = atm.shape[1]
    rows, cols = atm.shape[2:]
    tracers = ocean.shape[0] * ocean.shape[1]
    each = ocean.shape[1]
    obase, mbase, own, halo = row_slots(levels, tracers)
    slots, _ = lane_slots(levels, tracers)
    for one in used:
        one.wait()
    arrived = len(used)
    cell = atm_cell[...]
    hot_atm = jnp.where(one_hot(cell % cols, cols), 1.0, 0.0).astype(BF16)
    airx = gather_rows(air[...], one_hot(cell // cols, rows), hot_atm)
    w = weight[...]
    wair = w * airx
    wair_buf[...] = wair
    copy(wair_buf, wair_out)

    wetness = wet[...].astype(F32)

    lane = lax.broadcasted_iota(jnp.int32, (rows, cols), 1)
    fields = [(atm, (k, l), AH) for k in range(3) for l in range(levels)]
    fields += [(ocean, (i // each, i % each), OH) for i in range(tracers)]
    fields += [(depth, None, AH), (None, None, AH), (kappa, None, AH)]
    packed = {}
    for (ref, at, width), slot in zip(fields, slots):
        value = wetness if ref is None else (ref[...] if at is None else ref[at[0], at[1]])
        tile, offset = slot // cols, slot % cols
        mask = (lane >= offset) & (lane < offset + width)
        first = pltpu.roll(value, offset, 1) if offset else value
        turn = (offset + width) % cols
        last = pltpu.roll(value, turn, 1) if turn else value
        if tile in packed:
            a, b = packed[tile]
            packed[tile] = (jnp.where(mask, first, a), jnp.where(mask, last, b))
        else:
            packed[tile] = (first, last)
    for tile, (a, b) in packed.items():
        where = slice(tile * cols, (tile + 1) * cols)
        left[:, where] = a
        right[:, where] = b

    copy_either(column, right, cols_a, cols_b)
    copy_either(column, left, cols_b, cols_a)

    for level in range(levels):
        speed = wave_speed[level] * depth[...]
        both = near_rows(atm[0, level], atm[1, level], atm[2, level], speed, rows, cols)
        for ref, values in zip((up, down), both):
            for i, value in enumerate(values):
                at = i * levels + level
                ref[at : at + 1, :] = value
    at = own
    for strip in (left, right):
        for i in range(strip.shape[1] // cols):
            where = slice(i * cols, (i + 1) * cols)
            up[at : at + AH, :] = strip[0:AH, where]
            down[at : at + AH, :] = strip[rows - AH : rows, where]
            at += AH
    for i in range(tracers):
        at = obase + OH * i
        up[at : at + OH, :] = ocean[i // each, i % each, 0:OH, :]
        down[at : at + OH, :] = ocean[i // each, i % each, rows - OH : rows, :]
    for at, value, width in (
        (mbase, depth[...], AH),
        (mbase + AH, wetness, OH),
        (mbase + AH + OH, kappa[...], OH),
    ):
        up[at : at + width, :] = value[0:width]
        down[at : at + width, :] = value[rows - width : rows]
    copy_either(line, down, rows_a.at[0:halo], rows_b.at[0:halo])
    copy_either(line, up, rows_b.at[0:halo], rows_a.at[0:halo])

    cell = sea_cell[...]
    hot_sea = jnp.where(one_hot(cell % cols, cols), 1.0, 0.0).astype(BF16)
    row = dest[...] * rows + cell // cols
    tail = slice(halo, halo + 3 * rows)
    for shift in range(tiles):
        target = tile_at(shift, tiles)
        s1, s2 = scatter_rows([wair, w], one_hot(row - target * rows, rows), hot_sea)
        sums[shift, 0:rows, :] = s1
        sums[shift, rows : 2 * rows, :] = s2
        sums[shift, 2 * rows : 3 * rows, :] = ocean[0, 0]
        if len(sums_out) == 1:
            copy(sums.at[shift], sums_out[0].at[target])
        elif shift == 1:
            copy_either(line, sums.at[shift], rows_a.at[tail], rows_b.at[tail])
        elif shift == tiles - 1:
            copy_either(line, sums.at[shift], rows_b.at[tail], rows_a.at[tail])
        else:
            copy(sums.at[shift], sums_out[max(shift - 1, 0)])
    for one in used[arrived:]:
        one.wait()


def strips(cols, slot, width, left_part, right_part):
    low_half = lax.broadcasted_iota(jnp.int32, (1, cols), 1) < cols // 2
    offset = slot % cols
    a, b = right_part(slot // cols), left_part(slot // cols)
    if offset:
        a = pltpu.roll(a, cols - offset, 1)
    turn = (cols - width - offset) % cols
    if turn:
        b = pltpu.roll(b, turn, 1)
    return jnp.where(low_half, a, b)


def final_kernel(tiles, *refs):
    speed_in, atm_in, ocean_in, depth_in, kappa_in = refs[:5]
    kept = (len(refs) - 5 - 8 - 4) // 2
    sources, rest = refs[5 : 5 + kept], refs[5 + kept :]
    atm_out, ocean_out, speed, us, vs, hs, fs, ms = rest[:8]
    held, (edge, atm_buf, ocean_buf, sems) = rest[8 : 8 + kept], rest[8 + kept :]
    wet, atm_cell, dest, sea_cell, weight, wair, from_up, from_down, from_left, from_right, from_below, from_above = held[:12]
    messages = held[12:]
    levels = us.shape[0]
    each = ocean_out.shape[1]
    tracers = ocean_out.shape[0] * each
    rows, cols = atm_out.shape[2:]
    slots, lanes = lane_slots(levels, tracers)
    obase, mbase, own, halo = row_slots(levels, tracers)
    full = rows + 2 * AH
    block = (slice(None), slice(0, rows), slice(0, cols))
    rows_a, rows_b, cols_a, cols_b = sources[6:10]
    either = [(tile_parity(), rows_b, rows_a, from_up), (tile_parity(), rows_a, rows_b, from_down)]
    either += [(column_parity(), cols_b, cols_a, from_left), (column_parity(), cols_a, cols_b, from_right)]
    pairs = [pair for i, pair in enumerate(zip(sources, held)) if not 6 <= i < 10] + [(speed_in, speed)]
    pairs += [(atm_in.at[i], ref.at[block]) for i, ref in enumerate((us, vs, hs))]
    pairs += [(ocean_in.at[i], fs.at[(i, *block)]) for i in range(ocean_out.shape[0])]
    pairs += [(ref, ms.at[(i, *block[1:])]) for i, ref in ((0, depth_in), (2, kappa_in))]
    copies = [pltpu.make_async_copy(source, target, sems.at[i]) for i, (source, target) in enumerate(pairs)]
    for copy in copies:
        copy.start()
    for parity, even, odd, target in either:
        choices = [pltpu.make_async_copy(source, target, sems.at[len(copies)]) for source in (even, odd)]
        pl.when(parity == 0)(choices[0].start)
        pl.when(parity != 0)(choices[1].start)
        copies.append(choices[0])
    for copy in copies:
        copy.wait()
    corner_a, corner_b = from_below, from_above
    even_line, even_column = tile_parity() == 0, column_parity() == 0

    def message(shift, part):
        where = slice(part * rows, (part + 1) * rows)
        if len(messages) == 1:
            return messages[0][tile_at(-shift, tiles), where, :]
        if shift in (1, tiles - 1):
            return (from_up if shift == 1 else from_down)[halo + part * rows : halo + (part + 1) * rows, :]
        return messages[max(shift - 1, 0)][where, :]

    surface = fs[0, 0, 0:rows, 0:cols]
    cell = sea_cell[...]
    hot_sea = jnp.where(one_hot(cell % cols, cols), 1.0, 0.0).astype(BF16)
    row = dest[...] * rows + cell // cols
    s1, s2 = message(0, 0), message(0, 1)
    for shift in range(1, tiles):
        s1 = s1 + message(shift, 0)
        s2 = s2 + message(shift, 1)
    sea_flux = s1 - surface * s2

    half = lanes // cols
    for i in range(2 * half):
        where = slice(i % half * cols, (i % half + 1) * cols)
        first, second = (slice(AH, 2 * AH), slice(0, AH)) if i < half else (slice(0, AH), slice(AH, 2 * AH))
        a = jnp.where(even_column, corner_a[first, where], corner_a[second, where])
        b = jnp.where(even_column, corner_b[first, where], corner_b[second, where])
        edge[i, 0:AH, :] = jnp.where(even_line, a, b)
        edge[i, AH : 2 * AH, :] = jnp.where(even_line, b, a)
        at = own + AH * i
        edge[2 * half + i, 0:AH, :] = from_down[at : at + AH, :]
        edge[2 * half + i, AH : 2 * AH, :] = from_up[at : at + AH, :]

    def extend(view, field, width):
        slot = slots[field]
        view[0:rows, cols : 2 * cols] = strips(
            cols,
            slot,
            width,
            lambda t: from_left[:, t * cols : (t + 1) * cols],
            lambda t: from_right[:, t * cols : (t + 1) * cols],
        )
        view[rows:full, cols : 2 * cols] = strips(cols, slot, width, lambda t: edge[t], lambda t: edge[half + t])

    def extend_rows(view, at, high):
        view[rows : rows + high, 0:cols] = from_down[at : at + high, :]
        view[full - high : full, 0:cols] = from_up[at : at + high, :]

    lane = lax.broadcasted_iota(jnp.int32, (2 * AH, cols), 1)
    line = lax.broadcasted_iota(jnp.int32, (2 * AH, cols), 0)
    whole_strip = (lane < AH) | (lane >= cols - AH)
    outer = (lane < AH - 1) | (lane > cols - AH)

    def near(which, level):
        at = which * levels + level
        return from_down[at : at + 1, :], from_up[at : at + 1, :]

    def extend_level(view, which, level):
        strip = strips(cols, slots[which * levels + level], AH, lambda t: edge[3 * half + t], lambda t: edge[2 * half + t])
        below, above = near(which, level)
        inner = jnp.where(line == 0, below, jnp.where(line == 2 * AH - 1, above, 0.0))
        view[rows:full, 0:cols] = jnp.where(whole_strip if which == 0 else outer, strip, inner)

    def new_height_rows(tile, level):
        below, above = near(3, level), near(4, level)
        sent = jnp.where(
            line == 1, below[0], jnp.where(line == 2, above[0], jnp.where(line == 2 * AH - 3, above[1], below[1]))
        )
        here = (line == 1) | (line == 2) | (line == 2 * AH - 3) | (line == 2 * AH - 2)
        return jnp.where(here & jnp.logical_not(outer), sent, tile)

    def east(f):
        return pltpu.roll(f, 2 * cols - 1, 1)

    def west(f):
        return pltpu.roll(f, 1, 1)

    def south(f):
        return pltpu.roll(f, full - 1, 0)

    def north(f):
        return pltpu.roll(f, 1, 0)

    base = 3 * levels + tracers
    ms[1, 0:rows, 0:cols] = wet[...].astype(F32)
    for i, (at, high) in enumerate(((mbase, AH), (mbase + AH, OH), (mbase + AH + OH, OH))):
        extend(ms.at[i], base + i, AH)
        extend_rows(ms.at[i], at, high)
    sstx = jnp.zeros(cell.shape, F32)
    for shift in range(tiles):
        sstx = sstx + gather_rows(message(shift, 2), one_hot(row - tile_at(-shift, tiles) * rows, rows), hot_sea)
        for i in range(tracers * shift // tiles, tracers * (shift + 1) // tiles):
            extend(fs.at[i // each, i % each], 3 * levels + i, OH)
            extend_rows(fs.at[i // each, i % each], obase + OH * i, OH)
        for level in range(levels * shift // tiles, levels * (shift + 1) // tiles):
            for which, ref in enumerate((us, vs, hs)):
                extend(ref.at[level], which * levels + level, AH)
                extend_level(ref.at[level], which, level)
    flux = wair[...] - weight[...] * sstx
    cell = atm_cell[...]
    hot_atm = jnp.where(one_hot(cell % cols, cols), 1.0, 0.0).astype(BF16)

    w = ms[1]
    k = ms[2]
    kw = k * w
    ce, cw, cs, cn = kw * east(w), kw * west(w), kw * south(w), kw * north(w)
    center = 1.0 - (ce + cw + cs + cn)
    for step in range(OCEAN_STEPS):
        if step == OCEAN_STEPS - 1:
            (atm_flux,) = scatter_rows([flux], one_hot(cell // cols, rows), hot_atm)
        for i in range(tracers):
            f = fs[i // each, i % each]
            f = center * f + ce * east(f) + cw * west(f) + cs * south(f) + cn * north(f)
            if step < OCEAN_STEPS - 1:
                fs[i // each, i % each] = f
            else:
                f = f[0:rows, 0:cols]
                ocean_buf[i // each, i % each] = f + SEA_GAIN * sea_flux if i == 0 else f
    used = len(copies)
    copies = [pltpu.make_async_copy(ocean_buf, ocean_out, sems.at[used])]
    copies[0].start()

    d = 0.5 * ms[0]
    chunk = max(1, levels // 4)
    for step in range(ACOUSTIC):
        for level in range(levels):
            u, v, h = us[level], vs[level], hs[level]
            hs[level] = h - (speed[level] * d) * ((east(u) - west(u)) + (south(v) - north(v)))
            if step == 0:
                hs[level, rows:full, 0:cols] = new_height_rows(hs[level, rows:full, 0:cols], level)
        for level in range(levels):
            u, v, h = us[level], vs[level], hs[level]
            u = u - (east(h) - west(h)) * 0.5
            v = v - (south(h) - north(h)) * 0.5
            if step < ACOUSTIC - 1:
                us[level], vs[level] = u, v
            else:
                h = h[0:rows, 0:cols]
                atm_buf[0, level] = u[0:rows, 0:cols]
                atm_buf[1, level] = v[0:rows, 0:cols]
                atm_buf[2, level] = h - ATM_GAIN * atm_flux if level == levels - 1 else h
                if (level + 1) % chunk == 0:
                    where = pl.ds(level + 1 - chunk, chunk)
                    copies.append(
                        pltpu.make_async_copy(
                            atm_buf.at[:, where], atm_out.at[:, where], sems.at[used + len(copies)]
                        )
                    )
                    copies[-1].start()
    for copy in copies:
        copy.wait()


def on_device(
    tile_count,
    atm_state,
    air_temp,
    depth,
    wave_speed,
    ocean_state,
    wet_mask,
    diffusivity,
    xg_atm_cell,
    xg_dest,
    xg_ocean_cell,
    xg_weight,
):
    levels = atm_state.shape[1]
    rows, cols = atm_state.shape[2:]
    tracers = ocean_state.shape[0] * ocean_state.shape[1]
    cells = xg_weight.shape[-1]
    _, lanes = lane_slots(levels, tracers)
    _, _, _, halo = row_slots(levels, tracers)
    message_rows = halo
    vmem = pl.BlockSpec(memory_space=pltpu.VMEM)
    hbm = pl.BlockSpec(memory_space=pltpu.HBM)
    whole = pltpu.CompilerParams(vmem_limit_bytes=64 * 1024 * 1024)
    full = rows + 2 * AH

    def shape(*dims):
        return jax.ShapeDtypeStruct(dims, F32)

    by_shift = tile_count <= 4
    if by_shift:
        message_rows += 3 * rows
        sums = [shape(3 * rows, cols)] * (tile_count - 2)
    else:
        sums = [shape(tile_count, 3 * rows, cols)]
    atm_cell = xg_atm_cell.reshape(1, cells)
    dest = xg_dest.reshape(1, cells)
    sea_cell = xg_ocean_cell.reshape(1, cells)
    weight = xg_weight.reshape(1, cells)
    operands = (atm_state, ocean_state, depth, wet_mask, diffusivity, air_temp, atm_cell, dest, sea_cell, weight)
    operands += (wave_speed,)
    cols_a, cols_b, rows_a, rows_b, wair, *messages = pl.pallas_call(
        functools.partial(first_kernel, tile_count),
        out_shape=[shape(rows, lanes)] * 2 + [shape(message_rows, cols)] * 2 + [shape(1, cells)] + sums,
        in_specs=[hbm] * 11,
        out_specs=[hbm] * (5 + len(sums)),
        scratch_shapes=[pltpu.VMEM(x.shape, x.dtype) for x in operands[:-1]]
        + [pltpu.SMEM(wave_speed.shape, F32)]
        + [pltpu.VMEM((halo, cols), F32)] * 2
        + [pltpu.VMEM((rows, lanes), F32)] * 2
        + [
            pltpu.VMEM((1, cells), F32),
            pltpu.VMEM((tile_count, 3 * rows, cols), F32),
            pltpu.SemaphoreType.DMA((16 + tile_count,)),
        ],
        compiler_params=whole,
        name="first",
    )(*operands)

    column_axes = ("sub", "comp")
    column_count = lax.axis_size("sub") * lax.axis_size("comp")

    def shift(value, axes, count, by):
        return lax.ppermute(value, axes, [(i, (i + by) % count) for i in range(count)])

    def swap(value, axes, count, odd):
        return lax.ppermute(value, axes, [(i, (i + (1 if (i + odd) % 2 == 0 else -1)) % count) for i in range(count)])

    got_a = swap(cols_a, column_axes, column_count, 0)
    got_b = swap(cols_b, column_axes, column_count, 1)
    near_a = swap(rows_a, "tile", tile_count, 1)
    near_b = swap(rows_b, "tile", tile_count, 0)

    low = jnp.where(tile_parity() == 0, rows - AH, 0)
    corner_a, corner_b = [
        jnp.concatenate([lax.dynamic_slice_in_dim(x, at, AH) for x in (got_a, got_b)]) for at in (low, rows - AH - low)
    ]
    if by_shift:
        *messages, corner_a, corner_b = lax.optimization_barrier((*messages, corner_a, corner_b))
    corner_a = swap(corner_a, "tile", tile_count, 1)
    corner_b = swap(corner_b, "tile", tile_count, 0)
    if by_shift:
        got = messages[:1] + [shift(messages[s - 1], "tile", tile_count, s) for s in range(2, tile_count - 1)]
    else:
        got = [lax.all_to_all(messages[0], "tile", split_axis=0, concat_axis=0, tiled=True)]

    operands = (wave_speed, atm_state, ocean_state, depth, diffusivity)
    operands += (wet_mask, atm_cell, dest, sea_cell, weight, wair, near_a, near_b, got_a, got_b)
    operands += (corner_a, corner_b, *got)
    return tuple(
        pl.pallas_call(
            functools.partial(final_kernel, tile_count),
            out_shape=[shape(*atm_state.shape), shape(*ocean_state.shape)],
            in_specs=[hbm] * len(operands),
            out_specs=[hbm] * 2,
            scratch_shapes=[pltpu.SMEM(wave_speed.shape, F32)]
            + [pltpu.VMEM((levels, full, 2 * cols), F32)] * 3
            + [
                pltpu.VMEM((*ocean_state.shape[:2], full, 2 * cols), F32),
                pltpu.VMEM((3, full, 2 * cols), F32),
            ]
            + [pltpu.VMEM(x.shape, x.dtype) for x in operands[5:]]
            + [
                pltpu.VMEM((4 * (lanes // cols), 2 * AH, cols), F32),
                pltpu.VMEM(atm_state.shape, F32),
                pltpu.VMEM(ocean_state.shape, F32),
                pltpu.SemaphoreType.DMA((len(operands) + 10,)),
            ],
            compiler_params=whole,
            name="steps",
        )(*operands)
    )


def solution(mesh):
    grid = P(("member", "tile"), ("sub", "comp"))
    state = P(None, None, ("member", "tile"), ("sub", "comp"))
    cells = P(("member", "tile"), ("sub", "comp"), None)
    return jax.shard_map(
        functools.partial(on_device, mesh.shape["tile"]),
        mesh=mesh,
        in_specs=(
            state,
            grid,
            grid,
            P(),
            state,
            grid,
            grid,
            cells,
            P(("member", "tile"), ("sub", "comp"), None, None),
            cells,
            cells,
        ),
        out_specs=(state, state),
        check_vma=False,
    )
```

```python
import functools

import jax
import jax.numpy as jnp
from jax import lax
from jax.experimental import pallas as pl
from jax.experimental.pallas import tpu as pltpu
from jax.sharding import PartitionSpec as P

ACOUSTIC = 2
OCEAN_STEPS = 2
AH = 2 * ACOUSTIC
OH = OCEAN_STEPS

ATM_GAIN = 0.5
SEA_GAIN = 0.5

F32 = jnp.float32
BF16 = jnp.bfloat16


def lane_slots(levels, tracers):
    slots = [AH * i for i in range(3 * levels)]
    base = AH * 3 * levels
    slots += [base + OH * i for i in range(tracers)]
    base += OH * tracers
    slots += [base + AH * i for i in range(3)]
    total = base + 3 * AH
    return slots, -(-total // 128) * 128


def row_slots(levels, tracers):
    tracer = 5 * levels
    misc = tracer + OH * tracers
    own = misc + AH + 2 * OH
    _, lanes = lane_slots(levels, tracers)
    return tracer, misc, own, own + 2 * AH * (lanes // 128)


def near_rows(u, v, h, speed, rows, cols):
    east_west = (pltpu.roll(u, cols - 1, 1) - pltpu.roll(u, 1, 1)) * 0.5
    south_north = (pltpu.roll(v, rows - 1, 0) - pltpu.roll(v, 1, 0)) * 0.5
    h1 = h - speed * (east_west + south_north)
    out = []
    for near, turn in ((0, 1), (rows - 1, -1)):
        at = [slice(near + turn * i, near + turn * i + 1) for i in range(3)]
        out.append(
            (
                u[at[0]],
                v[at[0]],
                h[at[0]] - (0.5 * turn) * speed[at[0]] * v[at[1]],
                h1[at[1]],
                h1[at[2]] - (2.0 * turn) * v[at[1]],
            )
        )
    return out


def split3(value):
    hi = value.astype(BF16)
    rest = value - hi.astype(F32)
    mid = rest.astype(BF16)
    low = (rest - mid.astype(F32)).astype(BF16)
    return hi, mid, low


def one_hot(index, size):
    shape = (size, index.shape[-1])
    return lax.broadcasted_iota(jnp.int32, shape, 0) == index


def gather_rows(table, hot_rows, hot_cols):
    r = table.shape[0]
    parts = jnp.concatenate(split3(table), axis=0)
    g = jnp.dot(parts, hot_cols, preferred_element_type=F32)
    g = g[0:r] + g[r : 2 * r] + g[2 * r : 3 * r]
    return jnp.sum(jnp.where(hot_rows, g, 0.0), axis=0, keepdims=True)


def scatter_rows(values, hot_rows, hot_cols):
    r = hot_rows.shape[0]
    hot = jnp.where(hot_rows, 1.0, 0.0).astype(BF16)
    parts = [hot * part for value in values for part in split3(value)]
    s = lax.dot_general(
        jnp.concatenate(parts, axis=0),
        hot_cols,
        (((1,), (1,)), ((), ())),
        preferred_element_type=F32,
    )
    out = []
    for i in range(len(values)):
        base = 3 * r * i
        out.append(s[base : base + r] + s[base + r : base + 2 * r] + s[base + 2 * r : base + 3 * r])
    return out


def tile_at(shift, tiles):
    return lax.rem(lax.axis_index("tile") + shift % tiles, tiles)


def tile_parity():
    return lax.rem(lax.axis_index("tile") + 1, 2)


def column_parity():
    return lax.rem(lax.axis_index(("sub", "comp")), 2)


def first_kernel(tiles, *refs):
    sources, (cols_a, cols_b, rows_a, rows_b, wair_out, *sums_out) = refs[:11], refs[11:-18]
    held, (up, down, left, right, wair_buf, sums, sems) = refs[-18:-7], refs[-7:]
    atm, ocean, depth, wet, kappa, air, atm_cell, dest, sea_cell, weight, wave_speed = held
    used = []

    def copy(source, target):
        used.append(pltpu.make_async_copy(source, target, sems.at[len(used)]))
        used[-1].start()

    def copy_either(parity, source, even, odd):
        choices = [pltpu.make_async_copy(source, target, sems.at[len(used)]) for target in (even, odd)]
        pl.when(parity == 0)(choices[0].start)
        pl.when(parity != 0)(choices[1].start)
        used.append(choices[0])

    column, line = column_parity(), tile_parity()
    for source, target in zip(sources, held):
        copy(source, target)
    levels = atm.shape[1]
    rows, cols = atm.shape[2:]
    tracers = ocean.shape[0] * ocean.shape[1]
    each = ocean.shape[1]
    obase, mbase, own, halo = row_slots(levels, tracers)
    slots, _ = lane_slots(levels, tracers)
    for one in used:
        one.wait()
    arrived = len(used)
    cell = atm_cell[...]
    hot_atm = jnp.where(one_hot(cell % cols, cols), 1.0, 0.0).astype(BF16)
    airx = gather_rows(air[...], one_hot(cell // cols, rows), hot_atm)
    w = weight[...]
    wair = w * airx
    wair_buf[...] = wair
    copy(wair_buf, wair_out)

    wetness = wet[...].astype(F32)

    lane = lax.broadcasted_iota(jnp.int32, (rows, cols), 1)
    fields = [(atm, (k, l), AH) for k in range(3) for l in range(levels)]
    fields += [(ocean, (i // each, i % each), OH) for i in range(tracers)]
    fields += [(depth, None, AH), (None, None, AH), (kappa, None, AH)]
    packed = {}
    for (ref, at, width), slot in zip(fields, slots):
        value = wetness if ref is None else (ref[...] if at is None else ref[at[0], at[1]])
        tile, offset = slot // cols, slot % cols
        mask = (lane >= offset) & (lane < offset + width)
        first = pltpu.roll(value, offset, 1) if offset else value
        turn = (offset + width) % cols
        last = pltpu.roll(value, turn, 1) if turn else value
        if tile in packed:
            a, b = packed[tile]
            packed[tile] = (jnp.where(mask, first, a), jnp.where(mask, last, b))
        else:
            packed[tile] = (first, last)
    for tile, (a, b) in packed.items():
        where = slice(tile * cols, (tile + 1) * cols)
        left[:, where] = a
        right[:, where] = b

    copy_either(column, right, cols_a, cols_b)
    copy_either(column, left, cols_b, cols_a)

    for level in range(levels):
        speed = wave_speed[level] * depth[...]
        both = near_rows(atm[0, level], atm[1, level], atm[2, level], speed, rows, cols)
        for ref, values in zip((up, down), both):
            for i, value in enumerate(values):
                at = i * levels + level
                ref[at : at + 1, :] = value
    at = own
    for strip in (left, right):
        for i in range(strip.shape[1] // cols):
            where = slice(i * cols, (i + 1) * cols)
            up[at : at + AH, :] = strip[0:AH, where]
            down[at : at + AH, :] = strip[rows - AH : rows, where]
            at += AH
    for i in range(tracers):
        at = obase + OH * i
        up[at : at + OH, :] = ocean[i // each, i % each, 0:OH, :]
        down[at : at + OH, :] = ocean[i // each, i % each, rows - OH : rows, :]
    for at, value, width in (
        (mbase, depth[...], AH),
        (mbase + AH, wetness, OH),
        (mbase + AH + OH, kappa[...], OH),
    ):
        up[at : at + width, :] = value[0:width]
        down[at : at + width, :] = value[rows - width : rows]
    copy_either(line, down, rows_a.at[0:halo], rows_b.at[0:halo])
    copy_either(line, up, rows_b.at[0:halo], rows_a.at[0:halo])

    cell = sea_cell[...]
    hot_sea = jnp.where(one_hot(cell % cols, cols), 1.0, 0.0).astype(BF16)
    row = dest[...] * rows + cell // cols
    tail = slice(halo, halo + 3 * rows)
    for shift in range(tiles):
        target = tile_at(shift, tiles)
        s1, s2 = scatter_rows([wair, w], one_hot(row - target * rows, rows), hot_sea)
        sums[shift, 0:rows, :] = s1
        sums[shift, rows : 2 * rows, :] = s2
        sums[shift, 2 * rows : 3 * rows, :] = ocean[0, 0]
        if len(sums_out) == 1:
            copy(sums.at[shift], sums_out[0].at[target])
        elif shift == 1:
            copy_either(line, sums.at[shift], rows_a.at[tail], rows_b.at[tail])
        elif shift == tiles - 1:
            copy_either(line, sums.at[shift], rows_b.at[tail], rows_a.at[tail])
        else:
            copy(sums.at[shift], sums_out[max(shift - 1, 0)])
    for one in used[arrived:]:
        one.wait()


def strips(cols, slot, width, left_part, right_part):
    low_half = lax.broadcasted_iota(jnp.int32, (1, cols), 1) < cols // 2
    offset = slot % cols
    a, b = right_part(slot // cols), left_part(slot // cols)
    if offset:
        a = pltpu.roll(a, cols - offset, 1)
    turn = (cols - width - offset) % cols
    if turn:
        b = pltpu.roll(b, turn, 1)
    return jnp.where(low_half, a, b)


def final_kernel(tiles, *refs):
    speed_in, atm_in, ocean_in, depth_in, kappa_in = refs[:5]
    kept = (len(refs) - 5 - 8 - 4) // 2
    sources, rest = refs[5 : 5 + kept], refs[5 + kept :]
    atm_out, ocean_out, speed, us, vs, hs, fs, ms = rest[:8]
    held, (edge, atm_buf, ocean_buf, sems) = rest[8 : 8 + kept], rest[8 + kept :]
    wet, atm_cell, dest, sea_cell, weight, wair, from_up, from_down, from_left, from_right, from_below, from_above = held[:12]
    messages = held[12:]
    levels = us.shape[0]
    each = ocean_out.shape[1]
    tracers = ocean_out.shape[0] * each
    rows, cols = atm_out.shape[2:]
    slots, lanes = lane_slots(levels, tracers)
    obase, mbase, own, halo = row_slots(levels, tracers)
    full = rows + 2 * AH
    block = (slice(None), slice(0, rows), slice(0, cols))
    rows_a, rows_b, cols_a, cols_b = sources[6:10]
    either = [(tile_parity(), rows_b, rows_a, from_up), (tile_parity(), rows_a, rows_b, from_down)]
    either += [(column_parity(), cols_b, cols_a, from_left), (column_parity(), cols_a, cols_b, from_right)]
    pairs = [pair for i, pair in enumerate(zip(sources, held)) if not 6 <= i < 10] + [(speed_in, speed)]
    pairs += [(atm_in.at[i], ref.at[block]) for i, ref in enumerate((us, vs, hs))]
    pairs += [(ocean_in.at[i], fs.at[(i, *block)]) for i in range(ocean_out.shape[0])]
    pairs += [(ref, ms.at[(i, *block[1:])]) for i, ref in ((0, depth_in), (2, kappa_in))]
    copies = [pltpu.make_async_copy(source, target, sems.at[i]) for i, (source, target) in enumerate(pairs)]
    for copy in copies:
        copy.start()
    for parity, even, odd, target in either:
        choices = [pltpu.make_async_copy(source, target, sems.at[len(copies)]) for source in (even, odd)]
        pl.when(parity == 0)(choices[0].start)
        pl.when(parity != 0)(choices[1].start)
        copies.append(choices[0])
    for copy in copies:
        copy.wait()
    corner_a, corner_b = from_below, from_above
    even_line, even_column = tile_parity() == 0, column_parity() == 0

    def message(shift, part):
        where = slice(part * rows, (part + 1) * rows)
        if len(messages) == 1:
            return messages[0][tile_at(-shift, tiles), where, :]
        if shift in (1, tiles - 1):
            return (from_up if shift == 1 else from_down)[halo + part * rows : halo + (part + 1) * rows, :]
        return messages[max(shift - 1, 0)][where, :]

    surface = fs[0, 0, 0:rows, 0:cols]
    cell = sea_cell[...]
    hot_sea = jnp.where(one_hot(cell % cols, cols), 1.0, 0.0).astype(BF16)
    row = dest[...] * rows + cell // cols
    s1, s2 = message(0, 0), message(0, 1)
    for shift in range(1, tiles):
        s1 = s1 + message(shift, 0)
        s2 = s2 + message(shift, 1)
    sea_flux = s1 - surface * s2

    half = lanes // cols
    for i in range(2 * half):
        where = slice(i % half * cols, (i % half + 1) * cols)
        first, second = (slice(AH, 2 * AH), slice(0, AH)) if i < half else (slice(0, AH), slice(AH, 2 * AH))
        a = jnp.where(even_column, corner_a[first, where], corner_a[second, where])
        b = jnp.where(even_column, corner_b[first, where], corner_b[second, where])
        edge[i, 0:AH, :] = jnp.where(even_line, a, b)
        edge[i, AH : 2 * AH, :] = jnp.where(even_line, b, a)
        at = own + AH * i
        edge[2 * half + i, 0:AH, :] = from_down[at : at + AH, :]
        edge[2 * half + i, AH : 2 * AH, :] = from_up[at : at + AH, :]

    def extend(view, field, width):
        slot = slots[field]
        view[0:rows, cols : 2 * cols] = strips(
            cols,
            slot,
            width,
            lambda t: from_left[:, t * cols : (t + 1) * cols],
            lambda t: from_right[:, t * cols : (t + 1) * cols],
        )
        view[rows:full, cols : 2 * cols] = strips(cols, slot, width, lambda t: edge[t], lambda t: edge[half + t])

    def extend_rows(view, at, high):
        view[rows : rows + high, 0:cols] = from_down[at : at + high, :]
        view[full - high : full, 0:cols] = from_up[at : at + high, :]

    lane = lax.broadcasted_iota(jnp.int32, (2 * AH, cols), 1)
    line = lax.broadcasted_iota(jnp.int32, (2 * AH, cols), 0)
    whole_strip = (lane < AH) | (lane >= cols - AH)
    outer = (lane < AH - 1) | (lane > cols - AH)

    def near(which, level):
        at = which * levels + level
        return from_down[at : at + 1, :], from_up[at : at + 1, :]

    def extend_level(view, which, level):
        strip = strips(cols, slots[which * levels + level], AH, lambda t: edge[3 * half + t], lambda t: edge[2 * half + t])
        below, above = near(which, level)
        inner = jnp.where(line == 0, below, jnp.where(line == 2 * AH - 1, above, 0.0))
        view[rows:full, 0:cols] = jnp.where(whole_strip if which == 0 else outer, strip, inner)

    def new_height_rows(tile, level):
        below, above = near(3, level), near(4, level)
        sent = jnp.where(
            line == 1, below[0], jnp.where(line == 2, above[0], jnp.where(line == 2 * AH - 3, above[1], below[1]))
        )
        here = (line == 1) | (line == 2) | (line == 2 * AH - 3) | (line == 2 * AH - 2)
        return jnp.where(here & jnp.logical_not(outer), sent, tile)

    def east(f):
        return pltpu.roll(f, 2 * cols - 1, 1)

    def west(f):
        return pltpu.roll(f, 1, 1)

    def south(f):
        return pltpu.roll(f, full - 1, 0)

    def north(f):
        return pltpu.roll(f, 1, 0)

    base = 3 * levels + tracers
    ms[1, 0:rows, 0:cols] = wet[...].astype(F32)
    for i, (at, high) in enumerate(((mbase, AH), (mbase + AH, OH), (mbase + AH + OH, OH))):
        extend(ms.at[i], base + i, AH)
        extend_rows(ms.at[i], at, high)
    sstx = jnp.zeros(cell.shape, F32)
    for shift in range(tiles):
        sstx = sstx + gather_rows(message(shift, 2), one_hot(row - tile_at(-shift, tiles) * rows, rows), hot_sea)
        for i in range(tracers * shift // tiles, tracers * (shift + 1) // tiles):
            extend(fs.at[i // each, i % each], 3 * levels + i, OH)
            extend_rows(fs.at[i // each, i % each], obase + OH * i, OH)
        for level in range(levels * shift // tiles, levels * (shift + 1) // tiles):
            for which, ref in enumerate((us, vs, hs)):
                extend(ref.at[level], which * levels + level, AH)
                extend_level(ref.at[level], which, level)
    flux = wair[...] - weight[...] * sstx
    cell = atm_cell[...]
    hot_atm = jnp.where(one_hot(cell % cols, cols), 1.0, 0.0).astype(BF16)

    w = ms[1]
    k = ms[2]
    kw = k * w
    ce, cw, cs, cn = kw * east(w), kw * west(w), kw * south(w), kw * north(w)
    center = 1.0 - (ce + cw + cs + cn)
    for step in range(OCEAN_STEPS):
        if step == OCEAN_STEPS - 1:
            (atm_flux,) = scatter_rows([flux], one_hot(cell // cols, rows), hot_atm)
        for i in range(tracers):
            f = fs[i // each, i % each]
            f = center * f + ce * east(f) + cw * west(f) + cs * south(f) + cn * north(f)
            if step < OCEAN_STEPS - 1:
                fs[i // each, i % each] = f
            else:
                f = f[0:rows, 0:cols]
                ocean_buf[i // each, i % each] = f + SEA_GAIN * sea_flux if i == 0 else f
    used = len(copies)
    copies = [pltpu.make_async_copy(ocean_buf, ocean_out, sems.at[used])]
    copies[0].start()

    d = 0.5 * ms[0]
    chunk = max(1, levels // 4)
    for step in range(ACOUSTIC):
        for level in range(levels):
            u, v, h = us[level], vs[level], hs[level]
            hs[level] = h - (speed[level] * d) * ((east(u) - west(u)) + (south(v) - north(v)))
            if step == 0:
                hs[level, rows:full, 0:cols] = new_height_rows(hs[level, rows:full, 0:cols], level)
        for level in range(levels):
            u, v, h = us[level], vs[level], hs[level]
            u = u - (east(h) - west(h)) * 0.5
            v = v - (south(h) - north(h)) * 0.5
            if step < ACOUSTIC - 1:
                us[level], vs[level] = u, v
            else:
                h = h[0:rows, 0:cols]
                atm_buf[0, level] = u[0:rows, 0:cols]
                atm_buf[1, level] = v[0:rows, 0:cols]
                atm_buf[2, level] = h - ATM_GAIN * atm_flux if level == levels - 1 else h
                if (level + 1) % chunk == 0:
                    where = pl.ds(level + 1 - chunk, chunk)
                    copies.append(
                        pltpu.make_async_copy(
                            atm_buf.at[:, where], atm_out.at[:, where], sems.at[used + len(copies)]
                        )
                    )
                    copies[-1].start()
    for copy in copies:
        copy.wait()


def on_device(
    tile_count,
    atm_state,
    air_temp,
    depth,
    wave_speed,
    ocean_state,
    wet_mask,
    diffusivity,
    xg_atm_cell,
    xg_dest,
    xg_ocean_cell,
    xg_weight,
):
    levels = atm_state.shape[1]
    rows, cols = atm_state.shape[2:]
    tracers = ocean_state.shape[0] * ocean_state.shape[1]
    cells = xg_weight.shape[-1]
    _, lanes = lane_slots(levels, tracers)
    _, _, _, halo = row_slots(levels, tracers)
    message_rows = halo
    vmem = pl.BlockSpec(memory_space=pltpu.VMEM)
    hbm = pl.BlockSpec(memory_space=pltpu.HBM)
    whole = pltpu.CompilerParams(vmem_limit_bytes=64 * 1024 * 1024)
    full = rows + 2 * AH

    def shape(*dims):
        return jax.ShapeDtypeStruct(dims, F32)

    by_shift = tile_count <= 4
    if by_shift:
        message_rows += 3 * rows
        sums = [shape(3 * rows, cols)] * (tile_count - 2)
    else:
        sums = [shape(tile_count, 3 * rows, cols)]
    atm_cell = xg_atm_cell.reshape(1, cells)
    dest = xg_dest.reshape(1, cells)
    sea_cell = xg_ocean_cell.reshape(1, cells)
    weight = xg_weight.reshape(1, cells)
    operands = (atm_state, ocean_state, depth, wet_mask, diffusivity, air_temp, atm_cell, dest, sea_cell, weight)
    operands += (wave_speed,)
    cols_a, cols_b, rows_a, rows_b, wair, *messages = pl.pallas_call(
        functools.partial(first_kernel, tile_count),
        out_shape=[shape(rows, lanes)] * 2 + [shape(message_rows, cols)] * 2 + [shape(1, cells)] + sums,
        in_specs=[hbm] * 11,
        out_specs=[hbm] * (5 + len(sums)),
        scratch_shapes=[pltpu.VMEM(x.shape, x.dtype) for x in operands[:-1]]
        + [pltpu.SMEM(wave_speed.shape, F32)]
        + [pltpu.VMEM((halo, cols), F32)] * 2
        + [pltpu.VMEM((rows, lanes), F32)] * 2
        + [
            pltpu.VMEM((1, cells), F32),
            pltpu.VMEM((tile_count, 3 * rows, cols), F32),
            pltpu.SemaphoreType.DMA((16 + tile_count,)),
        ],
        compiler_params=whole,
        name="first",
    )(*operands)

    column_axes = ("sub", "comp")
    column_count = lax.axis_size("sub") * lax.axis_size("comp")

    def shift(value, axes, count, by):
        return lax.ppermute(value, axes, [(i, (i + by) % count) for i in range(count)])

    def swap(value, axes, count, odd):
        return lax.ppermute(value, axes, [(i, (i + (1 if (i + odd) % 2 == 0 else -1)) % count) for i in range(count)])

    got_a = swap(cols_a, column_axes, column_count, 0)
    got_b = swap(cols_b, column_axes, column_count, 1)
    near_a = swap(rows_a, "tile", tile_count, 1)
    near_b = swap(rows_b, "tile", tile_count, 0)

    low = jnp.where(tile_parity() == 0, rows - AH, 0)
    corner_a, corner_b = [
        jnp.concatenate([lax.dynamic_slice_in_dim(x, at, AH) for x in (got_a, got_b)]) for at in (low, rows - AH - low)
    ]
    corner_a = swap(corner_a, "tile", tile_count, 1)
    corner_b = swap(corner_b, "tile", tile_count, 0)
    if by_shift:
        *messages, got_b = lax.optimization_barrier((*messages, got_b))
        got = messages[:1] + [shift(messages[s - 1], "tile", tile_count, s) for s in range(2, tile_count - 1)]
    else:
        got = [lax.all_to_all(messages[0], "tile", split_axis=0, concat_axis=0, tiled=True)]

    operands = (wave_speed, atm_state, ocean_state, depth, diffusivity)
    operands += (wet_mask, atm_cell, dest, sea_cell, weight, wair, near_a, near_b, got_a, got_b)
    operands += (corner_a, corner_b, *got)
    return tuple(
        pl.pallas_call(
            functools.partial(final_kernel, tile_count),
            out_shape=[shape(*atm_state.shape), shape(*ocean_state.shape)],
            in_specs=[hbm] * len(operands),
            out_specs=[hbm] * 2,
            scratch_shapes=[pltpu.SMEM(wave_speed.shape, F32)]
            + [pltpu.VMEM((levels, full, 2 * cols), F32)] * 3
            + [
                pltpu.VMEM((*ocean_state.shape[:2], full, 2 * cols), F32),
                pltpu.VMEM((3, full, 2 * cols), F32),
            ]
            + [pltpu.VMEM(x.shape, x.dtype) for x in operands[5:]]
            + [
                pltpu.VMEM((4 * (lanes // cols), 2 * AH, cols), F32),
                pltpu.VMEM(atm_state.shape, F32),
                pltpu.VMEM(ocean_state.shape, F32),
                pltpu.SemaphoreType.DMA((len(operands) + 10,)),
            ],
            compiler_params=whole,
            name="steps",
        )(*operands)
    )


def solution(mesh):
    grid = P(("member", "tile"), ("sub", "comp"))
    state = P(None, None, ("member", "tile"), ("sub", "comp"))
    cells = P(("member", "tile"), ("sub", "comp"), None)
    return jax.shard_map(
        functools.partial(on_device, mesh.shape["tile"]),
        mesh=mesh,
        in_specs=(
            state,
            grid,
            grid,
            P(),
            state,
            grid,
            grid,
            cells,
            P(("member", "tile"), ("sub", "comp"), None, None),
            cells,
            cells,
        ),
        out_specs=(state, state),
        check_vma=False,
    )
```
